32 devices in a mesh: rep: 4 (over x, core), shard: 8 (over z, y).
Axes of the slice: x: 2, y: 2, z: 4, core: 2. Of those that a mesh axis runs over, the one named last changes fastest.
Arguments:
- tokens: bfloat16 [4, 4096, 1280], P('rep', 'shard'), may hold values from -6 to 6
- segments: int32 [4, 4096], P('rep', 'shard'), may hold values from 0 to 1, as said below
- cotangent: bfloat16 [4, 4096, 1280], P('rep', 'shard'), may hold values from -6 to 6
- gain_one: bfloat16 [1280], P('shard'), may hold values from 0.099609375 to 1.8984375
- qkv_weight: bfloat16 [1280, 3840], P('shard'), may hold values from -0.15625 to 0.15625
- query_scale: float32 [80], replicated, may hold values from 0.5 to 2.5
- out_weight: bfloat16 [1280, 1280], P('shard'), may hold values from -1.25 to 1.25
- gain_two: bfloat16 [1280], P('shard'), may hold values from 0.099609375 to 1.8984375
- up_weight: bfloat16 [1280, 1280], P('shard'), may hold values from -0.15625 to 0.15625
- up_bias: bfloat16 [1280], P('shard'), may hold values from -3 to 3
- down_weight: bfloat16 [1280, 1280], P('shard'), may hold values from -0.15625 to 0.15625
- down_bias: bfloat16 [1280], P('shard'), may hold values from -3 to 3
Outputs:
- output: bfloat16 [4, 4096, 1280], P('rep', 'shard')
- input_grad: bfloat16 [4, 4096, 1280], P('rep', 'shard')
- gain_one_grad: float32 [1280], P('shard')
- qkv_grad: float32 [1280, 3840], P('shard')
- scale_grad: float32 [80], replicated
- out_grad: float32 [1280, 1280], P('shard')
- gain_two_grad: float32 [1280], P('shard')
- up_grad: float32 [1280, 1280], P('shard')
- up_bias_grad: float32 [1280], P('shard')
- down_grad: float32 [1280, 1280], P('shard')
- down_bias_grad: float32 [1280], P('shard')
The draws below stay inside these ranges and needn't reach their ends.
Inputs may be any that keep to these rules, and one draw needn't show every extreme that they name: `segments`: along each sequence the document numbers start at 0, never fall and each covers one contiguous run of tokens. A sequence holds 2 documents, or one where that is zero; every document but the last holds 1025 to 3071 tokens.
All inputs are finite; a program needn't handle non-finite values.
Results may differ from the reference program's by a relative error of at most 0.019.
Values may be sent and summed in bfloat16 or wider, within the bound.
A program may use at most 320 MiB of HBM per device.

```python
import math
import jax
import jax.numpy as jnp
from jax import lax

D = 1280
HEADS = 16
HEAD = 80
FF = 1280
WINDOW = 1024
QBLOCK = 512
LENGTH = 4096
SEQS = 4
DOC_MEAN = 2048


def draw_segments(key, part):
    key = jax.random.fold_in(key, 11)
    documents = max(1, LENGTH // DOC_MEAN)
    quarter = DOC_MEAN // 4
    offsets = jax.random.randint(key, (SEQS, documents - 1), -quarter, quarter)
    numbers = lax.broadcasted_iota(jnp.int32, (SEQS, documents - 1), 1) + 1
    bounds = (numbers * DOC_MEAN + offsets).astype(jnp.int32)
    places = lax.broadcasted_iota(jnp.int32, (SEQS, LENGTH, documents - 1), 1)
    passed = (places >= bounds[:, None, :]).astype(jnp.int32)
    return jnp.sum(passed, axis=2).astype(jnp.int32)


def shard_levels(stream_key, extent, cuts, smallest, top_value):
    def one(axis_at, blocks):
        draws = jax.random.uniform(jax.random.fold_in(jax.random.fold_in(stream_key, 6), axis_at), (blocks,), jnp.float32, smallest / len(cuts), top_value / len(cuts))
        return jnp.repeat(jnp.exp(draws), extent[axis_at] // blocks).reshape((-1,) + (1,) * (len(extent) - axis_at - 1))

    loudness = one(*cuts[0])
    for cut in cuts[1:]:
        loudness = loudness * one(*cut)
    return loudness


def centred(stream_key, shape, scale, limit, split=(), kind=jnp.bfloat16):
    factor_of = shard_levels(stream_key, shape, split, -0.22, 0.18) if split else 1.0
    values = jax.random.normal(stream_key, shape, jnp.float32) * scale * factor_of
    return jnp.minimum(jnp.maximum(values, -limit), limit).astype(kind)


def setup_inputs(seed: int = 0) -> dict:
    key_of = jax.random.split(jax.random.key(seed), 13)
    tokens = centred(key_of[0], (SEQS, LENGTH, D), 1.0, 6.0, ((0, 4), (1, 8)))
    segments = draw_segments(jax.random.fold_in(key_of[12], 71), 0)
    cotangent = centred(key_of[2], (SEQS, LENGTH, D), 1.0, 6.0, ((0, 4), (1, 8)))
    gain_one = jnp.clip(1.0 + 0.18 * jax.random.normal(key_of[3], (D,), jnp.float32), 0.099609375, 1.8984375).astype(jnp.bfloat16)
    qkv_weight = centred(key_of[4], (D, 3 * D), D ** -0.5, 0.15625, ((0, 8),))
    query_scale = jnp.clip(jax.random.uniform(key_of[5], (HEAD,), jnp.float32, 0.5, 2.5), 0.5, 2.5)
    out_weight = centred(key_of[6], (D, D), (D // 64) ** -0.5, 1.25, ((0, 8),))
    gain_two = jnp.clip(1.0 + 0.18 * jax.random.normal(key_of[7], (D,), jnp.float32), 0.099609375, 1.8984375).astype(jnp.bfloat16)
    up_weight = centred(key_of[8], (D, FF), D ** -0.5, 0.15625, ((0, 8),))
    up_bias = centred(key_of[9], (FF,), 0.5, 3.0, ((0, 8),))
    down_weight = centred(key_of[10], (FF, D), FF ** -0.5, 0.15625, ((0, 8),))
    down_bias = centred(key_of[11], (D,), 0.5, 3.0, ((0, 8),))
    return {"tokens": tokens, "segments": segments, "cotangent": cotangent, "gain_one": gain_one, "qkv_weight": qkv_weight, "query_scale": query_scale, "out_weight": out_weight, "gain_two": gain_two, "up_weight": up_weight, "up_bias": up_bias, "down_weight": down_weight, "down_bias": down_bias}


EPS = 1e-06
LOG2E = 1.442695041
MASKED = -1e+30
HIGH = lax.Precision.HIGHEST

@jax.custom_vjp
def low(v):
    return lax.optimization_barrier(v.astype(jnp.bfloat16)).astype(jnp.float32)

@jax.custom_vjp
def low_back(v):
    return v

def low_keep(v):
    return (low(v), None)

def low_pass(kept, grad):
    return (grad,)

def back_keep(v):
    return (v, None)

def back_low(kept, grad):
    return (low(grad),)
low.defvjp(low_keep, low_pass)
low_back.defvjp(back_keep, back_low)

def rms_scale(state, gain):
    inverse = lax.rsqrt(lax.optimization_barrier(jnp.mean(state * state, axis=-1, keepdims=True)) + EPS)
    return state * inverse * gain

def attend(queries, keys, values, segments):
    length = queries.shape[0]
    span = WINDOW + QBLOCK
    pad_keys = jnp.concatenate([jnp.zeros((WINDOW, D), jnp.float32), keys], 0)
    pad_values = jnp.concatenate([jnp.zeros((WINDOW, D), jnp.float32), values], 0)
    pad_segments = jnp.concatenate([jnp.full((WINDOW,), -1, jnp.int32), segments.astype(jnp.int32)], 0)
    rows = lax.broadcasted_iota(jnp.int32, (QBLOCK, span), 0)
    columns = lax.broadcasted_iota(jnp.int32, (QBLOCK, span), 1)
    near = (columns > rows) & (columns <= rows + WINDOW)

    @jax.checkpoint
    def one_block(start):
        query_part = lax.dynamic_slice_in_dim(queries, start, QBLOCK, 0).reshape(QBLOCK, HEADS, HEAD)
        key_part = lax.dynamic_slice_in_dim(pad_keys, start, span, 0).reshape(span, HEADS, HEAD)
        value_part = lax.dynamic_slice_in_dim(pad_values, start, span, 0).reshape(span, HEADS, HEAD)
        query_segs = lax.dynamic_slice_in_dim(segments.astype(jnp.int32), start, QBLOCK, 0)
        key_segs = lax.dynamic_slice_in_dim(pad_segments, start, span, 0)
        allowed = near & (query_segs[:, None] == key_segs[None, :])
        scores = low_back(jnp.einsum('qhd,khd->hqk', query_part, key_part, precision=HIGH))
        scores = jnp.where(allowed[None], scores, MASKED)
        top = lax.optimization_barrier(jnp.max(scores, axis=-1, keepdims=True))
        expo = jnp.exp(scores - top)
        probs = low(expo / lax.optimization_barrier(jnp.sum(expo, axis=-1, keepdims=True)))
        return jnp.einsum('hqk,khd->qhd', probs, value_part, precision=HIGH).reshape(QBLOCK, D)
    starts = jnp.arange(length // QBLOCK, dtype=jnp.int32) * QBLOCK
    return lax.map(one_block, starts).reshape(length, D)

def layer(state, segments, gain_one, qkv_weight, query_scale, out_weight, gain_two, up_weight, up_bias, down_weight, down_bias):
    acted = low(rms_scale(state, gain_one))
    mixed = jnp.dot(acted, qkv_weight, precision=HIGH)
    query_raw = low_back(mixed[:, :D])
    keys = low(low_back(mixed[:, D:2 * D]))
    values = low(low_back(mixed[:, 2 * D:]))
    factor = jnp.tile(LOG2E / math.sqrt(HEAD) * jax.nn.softplus(query_scale), HEADS)
    queries = low(query_raw * factor)
    heads_out = low(low_back(attend(queries, keys, values, segments)))
    hidden = state + low_back(jnp.dot(heads_out, out_weight, precision=HIGH))
    inner = low(rms_scale(hidden, gain_two))
    upper = low_back(jnp.dot(inner, up_weight, precision=HIGH) + up_bias)
    lower = low(jax.nn.silu(upper))
    return hidden + low_back(jnp.dot(lower, down_weight, precision=HIGH) + down_bias)

def reference(tokens, segments, cotangent, gain_one, qkv_weight, query_scale, out_weight, gain_two, up_weight, up_bias, down_weight, down_bias):
    params = tuple((weight.astype(jnp.float32) for weight in (gain_one, qkv_weight, query_scale, out_weight, gain_two, up_weight, up_bias, down_weight, down_bias)))

    def one_sequence(totals, inputs):
        seq_tokens, seq_segments, seq_cotangent = inputs

        def forward(state, *weights):
            return layer(state, seq_segments, *weights)
        result, pullback = jax.vjp(forward, seq_tokens.astype(jnp.float32), *params)
        grads = pullback(seq_cotangent.astype(jnp.float32))
        totals = tuple((total + grad for total, grad in zip(totals, grads[1:])))
        return (totals, (result.astype(jnp.bfloat16), grads[0].astype(jnp.bfloat16)))
    zeros = tuple((jnp.zeros_like(weight) for weight in params))
    totals, outs = lax.scan(one_sequence, zeros, (tokens, segments, cotangent))
    output, input_grad = outs
    gain_one_grad, qkv_grad, scale_grad, out_grad, gain_two_grad, up_grad, up_bias_grad, down_grad, down_bias_grad = totals
    return (output, input_grad, gain_one_grad, qkv_grad, scale_grad, out_grad, gain_two_grad, up_grad, up_bias_grad, down_grad, down_bias_grad)
```

```python
import functools
import math

import jax
import jax.numpy as jnp
from jax import lax
from jax.experimental import pallas as pl
from jax.experimental.pallas import tpu as pltpu
from jax.sharding import PartitionSpec as P

HEAD = 80
WINDOW = 1024
EPS = 1e-06
LOG2E = 1.442695041
LN2 = math.log(2.0)
MASKED = -1e30
TILE = 256
MESH = pl.DeviceIdType.MESH
F32 = jnp.float32
BF16 = jnp.bfloat16
VMEM_LIMIT = 62 * 2**20
ANY = pl.BlockSpec(memory_space=pl.ANY)
VM = pl.BlockSpec(memory_space=pltpu.VMEM)


def mul(a, b, left=1, right=0):
    return lax.dot_general(a, b, (((left,), (right,)), ((), ())), preferred_element_type=F32)


def at(start, size, unit):
    return pl.ds(pl.multiple_of(start, unit), size)


def bit_of(index, bit):
    return lax.rem(lax.div(index, 1 << bit), 2)


def flip(index, mask):
    out = index
    bit = 0
    while mask >> bit:
        if (mask >> bit) & 1:
            out = out + (1 - 2 * bit_of(index, bit)) * (1 << bit)
        bit += 1
    return out


def span(bits):
    masks = [0]
    for bit in bits:
        masks = masks + [mask | (1 << bit) for mask in masks]
    return masks


def stage_orders(bits):
    rest = list(range(2, bits))
    return (["x", 0, 1] + rest, [0, 1, "x"] + rest, [1, "x", 0] + rest)


def greet(count):
    rep, shard = lax.axis_index("rep"), lax.axis_index("shard")
    barrier = pltpu.get_barrier_semaphore()
    for step in range(1, count):
        other = lax.rem(shard + step, count)
        pl.semaphore_signal(barrier, inc=1, device_id={"rep": rep, "shard": other}, device_id_type=MESH)
    for mask in (1, 2):
        pl.semaphore_signal(barrier, inc=1, device_id={"rep": flip(rep, mask), "shard": shard}, device_id_type=MESH)
    pl.semaphore_wait(barrier, count + 1)


class Sems:
    def __init__(self, send, recv):
        self.send, self.recv, self.used = send, recv, 0

    def slot(self):
        self.used += 1
        return self.used - 1

    def remote(self, src, dst, rep, shard, slot=None):
        slot = self.slot() if slot is None else slot
        return pltpu.make_async_remote_copy(
            src_ref=src,
            dst_ref=dst,
            send_sem=self.send.at[slot],
            recv_sem=self.recv.at[slot],
            device_id={"rep": rep, "shard": shard},
            device_id_type=MESH,
        )


class Doubling:
    def __init__(self, sems, count, rows, parts):
        self.sems, self.rows, self.half, self.parts = sems, rows, rows // 2, parts
        bits = count.bit_length() - 1
        self.stages = bits + 1
        self.plan = []
        for order in stage_orders(bits):
            have, whole, stages = [], False, []
            for what in order[::-1]:
                masks = span(have)[1:] if what == "x" else span(have)
                stages.append([(what, mask, whole, sems.slot(), sems.slot()) for mask in masks])
                if what == "x":
                    whole = True
                else:
                    have.append(what)
            self.plan.append(stages)

    def copy(self, part, step):
        what, mask, whole, slot, _ = step
        rep, shard = lax.axis_index("rep"), lax.axis_index("shard")
        core, cross = lax.rem(rep, 2), lax.div(rep, 2)
        src, dst, first, cols = self.parts[part]
        across = at(first + core * cols, cols, 128)
        shift, size = (0, self.rows) if whole else (cross * self.half, self.half)
        row = flip(shard, mask) * self.rows + shift
        to = dst.at[at(row, size, 16), across]
        here = src.at[at(shift, size, 16), across] if mask == 0 else to
        if what == "x":
            return self.sems.remote(here, to, flip(rep, 2), shard, slot)
        return self.sems.remote(here, to, rep, flip(shard, 1 << what), slot)

    def ahead(self, part, step):
        what, mask, whole, _, slot = step
        rep, shard = lax.axis_index("rep"), lax.axis_index("shard")
        core, cross = lax.rem(rep, 2), lax.div(rep, 2)
        _, dst, first, cols = self.parts[part]
        if what == "x":
            row, size = flip(shard, mask) * self.rows + (1 - cross) * self.half, self.half
        else:
            shift, size = (0, self.rows) if whole else (cross * self.half, self.half)
            row = flip(shard, mask | (1 << what)) * self.rows + shift
        spot = dst.at[at(row, size, 16), at(first + core * cols, cols, 128)]
        return self.sems.remote(spot, spot, flip(rep, 1), shard, slot)

    def send(self, stage):
        for part in range(3):
            for step in self.plan[part][stage]:
                self.copy(part, step).start()

    def settle(self, stage):
        for part in range(3):
            for step in self.plan[part][stage]:
                self.copy(part, step).wait_recv()
                self.ahead(part, step).start()

    def move(self, stage):
        for part in range(3):
            for step in self.plan[part][stage]:
                self.copy(part, step).wait_recv()
            for step in self.plan[part][stage + 1]:
                self.copy(part, step).start()
            for step in self.plan[part][stage]:
                self.ahead(part, step).start()

    def finish(self):
        for part in range(3):
            for stage in self.plan[part]:
                for step in stage:
                    self.ahead(part, step).wait_recv()

    def drain(self):
        for part in range(3):
            for stage in self.plan[part]:
                for step in stage:
                    self.copy(part, step).wait_send()
                    self.ahead(part, step).wait_send()


class Gathered:
    stages = 1

    def send(self, stage):
        pass

    settle = move = send

    def finish(self):
        pass

    drain = finish


def forward_kernel(count, *refs):
    (tokens, earlier, segs, vec, factor, w_qkv, w_out, w_up, w_down) = refs[:9]
    results = refs[9:26]
    alone = earlier is not None
    (
        output_hbm, acted_t_hbm, q_t_hbm, k_t_hbm, v_t_hbm, o_t_hbm, lse, hidden_hbm,
        inner_t_hbm, upper_hbm, lower_t_hbm, rows_out, qkv_hbm, out_hbm, up_hbm, down_hbm, mask_hbm,
    ) = results
    (
        seg_ext, vec_full, qkv, out, up, down, acted, acted_t, q_t, k_t, v_t, o_t, heads, inner,
        hidden, upper, inner_t, lower_t, mask, state_low, send, recv, lsem,
    ) = refs[26:]
    rep, shard = lax.axis_index("rep"), lax.axis_index("shard")
    length, width = tokens.shape
    total = 3 * length
    rows = w_qkv.shape[0]
    tiles = width // TILE
    own = pl.ds(total - length, length)
    sems = Sems(send, recv)
    lower, output = heads, inner

    first_cols = (tiles * 3 // 5) * TILE
    rest_cols = width - first_cols
    groups = (Gathered(),) * 3 if alone else (
        Doubling(sems, count, rows, [(w_qkv, qkv, p * width, first_cols // 2) for p in range(3)]),
        Doubling(sems, count, rows, [(w_qkv, qkv, p * width + first_cols, rest_cols // 2) for p in range(3)]),
        Doubling(sems, count, rows, [(w, full, 0, width // 2) for w, full in ((w_out, out), (w_up, up), (w_down, down))]),
    )

    pairs = [(tokens, acted.at[own]), (tokens, state_low)]
    if alone:
        pairs += [(earlier, acted.at[pl.ds(0, 2 * length)]), (segs, seg_ext), (vec, vec_full)]
        pairs += [(w_qkv, qkv), (w_out, out), (w_up, up), (w_down, down)]
    else:
        mine = at(shard * rows, rows, 16)
        pairs += [(segs, seg_ext.at[2]), (vec, vec_full.at[shard])]
        pairs += [(w_qkv, qkv.at[mine]), (w_out, out.at[mine]), (w_up, up.at[mine]), (w_down, down.at[mine])]
    loads = [pltpu.make_async_copy(src, dst, lsem.at[i]) for i, (src, dst) in enumerate(pairs)]
    for copy in loads:
        copy.start()

    odd = lax.rem(shard, 2) == 1
    even = jnp.logical_not(odd)
    far_ok, far_got = shard < count - 2, shard >= 2
    buddy = flip(shard, 1)
    far_to = lax.rem(shard + 2, count)
    nchunk = 4
    part = length // nchunk
    far, near, relay, vecs = [], [], [], []
    for i in range(0 if alone else nchunk):
        here = pl.ds(i * part, part)
        far_spot, near_spot = acted.at[pl.ds(i * part, part)], acted.at[pl.ds(length + i * part, part)]
        slot = sems.slot()
        far.append(sems.remote(tokens.at[here], far_spot, rep, far_to, sems.slot()))
        near.append(sems.remote(tokens.at[here], near_spot, rep, buddy, slot))
        relay.append(sems.remote(far_spot, near_spot, rep, buddy, slot))
    if not alone:
        slot = sems.slot()
        far.append(sems.remote(segs, seg_ext.at[0], rep, far_to, sems.slot()))
        near.append(sems.remote(segs, seg_ext.at[1], rep, buddy, slot))
        relay.append(sems.remote(seg_ext.at[0], seg_ext.at[1], rep, buddy, slot))
        vecs = [
            sems.remote(vec, vec_full.at[shard], rep, lax.rem(shard + step, count), sems.slot()) for step in range(1, count)
        ]

    def far_start(*which):
        @pl.when(far_ok)
        def _():
            for i in which:
                far[i].start()

    def near_start(*which):
        @pl.when(even)
        def _():
            for i in which:
                near[i].start()

    def relay_start(*which):
        @pl.when(far_got)
        def _():
            for i in which:
                far[i].wait_recv()

        @pl.when(odd & far_got)
        def _():
            for i in which:
                relay[i].start()

    if not alone:
        greet(count)
        groups[0].send(0)
        for copy in vecs:
            copy.start()
        far_start(4, 0, 1)
        near_start(4, 0)
        groups[0].move(0)
        far_start(2)
        near_start(1)
        groups[0].move(1)
        groups[1].send(0)
        far_start(3)
        near_start(2, 3)
        relay_start(4, 0, 1)
        groups[0].move(2)
        groups[1].move(0)
        relay_start(2, 3)

    for copy in loads:
        copy.wait()
    for copy in vecs:
        copy.wait_recv()
    each = width // count
    vectors = jnp.concatenate([vec_full[i][:, :each].astype(F32) for i in range(count)], axis=1)
    rows_out[...] = vectors[:8, :]
    gain_one, gain_two = rows_out[0:1, :], rows_out[1:2, :]

    def norm_rows(i):
        sl = at(i * TILE, TILE, TILE)
        state = acted[sl, :].astype(F32)
        scale = lax.rsqrt(jnp.mean(state * state, axis=-1, keepdims=True) + EPS)
        value = (state * scale * rows_out[0:1, :]).astype(BF16)
        value = jnp.where(shard + i * TILE // length >= 2, value, jnp.zeros_like(value))
        acted[sl, :] = value
        acted_t[:, sl] = value.T

    def norm_step(i, carry):
        norm_rows(i)
        return carry

    per = length // TILE
    lax.fori_loop(2 * per, 3 * per, norm_step, 0)

    if not alone:

        @pl.when(odd)
        def _():
            for copy in near:
                copy.wait_recv()

        @pl.when(even & far_got)
        def _():
            for copy in relay:
                copy.wait_recv()

        @pl.when(odd & far_got)
        def _():
            for copy in relay:
                copy.wait_send()

    lax.fori_loop(0, 2 * per, norm_step, 0)

    mine = seg_ext[2].astype(F32)[0:1, :]
    for j in range(3):
        column = jnp.where(shard + j >= 2, seg_ext[j].astype(F32).T[:, 0:1], -1.0)
        place = lax.broadcasted_iota(jnp.int32, (length, length), 0) + j * length
        lane = lax.broadcasted_iota(jnp.int32, (length, length), 1)
        near_by = (place > lane) & (place <= lane + WINDOW)
        mask[j * length : (j + 1) * length, :] = jnp.where(near_by & (column == mine), 0.0, MASKED)

    groups[0].settle(groups[0].stages - 1)
    groups[1].move(1)
    groups[2].send(0)
    groups[0].finish()

    def project(i, carry):
        sl = at(i * TILE, TILE, TILE)
        q_t[sl, :] = (mul(acted[own, :], qkv[:, sl]) * factor[:, sl]).astype(BF16).T
        k_t[sl, :] = mul(acted[...], qkv[:, at(width + i * TILE, TILE, TILE)]).astype(BF16).T
        v_t[sl, :] = mul(acted[...], qkv[:, at(2 * width + i * TILE, TILE, TILE)]).astype(BF16).T
        return carry

    lax.fori_loop(0, first_cols // TILE, project, 0)
    groups[1].move(2)
    groups[2].move(0)

    def attend(h):
        sl = at(h * HEAD, HEAD, 16)
        scores = mul(k_t[sl, :].T, q_t[sl, :]) + mask[...]
        top = jnp.max(scores, axis=0, keepdims=True)
        probs = jnp.exp2(scores - top)
        norm = jnp.sum(probs, axis=0, keepdims=True)
        o_t[sl, :] = (mul(v_t[sl, :], probs.astype(BF16)) * (1.0 / norm)).astype(BF16)
        lse[h] = top + jnp.log2(norm)

    ready = first_cols // HEAD
    count_heads = width // HEAD

    def attend_first(h, carry):
        attend(h)

        @pl.when(h == 1)
        def _():
            groups[1].settle(groups[1].stages - 1)
            groups[2].move(1)

        @pl.when(h == 6)
        def _():
            groups[2].move(2)

        return carry

    lax.fori_loop(0, ready, attend_first, 0)
    groups[1].finish()
    lax.fori_loop(first_cols // TILE, tiles, project, 0)
    keep = [
        pltpu.make_async_copy(src, dst, lsem.at[8 + i])
        for i, (src, dst) in enumerate(((qkv, qkv_hbm), (acted_t, acted_t_hbm), (q_t, q_t_hbm), (k_t, k_t_hbm), (v_t, v_t_hbm), (mask, mask_hbm)))
    ]
    for copy in keep:
        copy.start()

    def attend_rest(h, carry):
        attend(h)

        @pl.when(h == count_heads - 3)
        def _():
            groups[2].settle(groups[2].stages - 1)

        return carry

    lax.fori_loop(ready, count_heads, attend_rest, 0)

    def keep_more(*pairs):
        for src, dst in pairs:
            copy = pltpu.make_async_copy(src, dst, lsem.at[8 + len(keep)])
            copy.start()
            keep.append(copy)

    keep_more((o_t, o_t_hbm))

    def turn(i, carry):
        sl = at(i * TILE, TILE, TILE)
        heads[:, sl] = o_t[sl, :].T
        return carry

    lax.fori_loop(0, tiles, turn, 0)
    groups[2].finish()
    keep_more((out, out_hbm), (up, up_hbm), (down, down_hbm))

    def out_step(i, carry):
        sl = at(i * TILE, TILE, TILE)
        hidden[:, sl] = state_low[:, sl].astype(F32) + mul(heads[...], out[:, sl])
        return carry

    lax.fori_loop(0, tiles, out_step, 0)
    keep_more((hidden, hidden_hbm))

    def norm_two(i, carry):
        sl = at(i * TILE, TILE, TILE)
        value = hidden[sl, :]
        scale = lax.rsqrt(jnp.mean(value * value, axis=-1, keepdims=True) + EPS)
        normed = (value * scale * rows_out[1:2, :]).astype(BF16)
        inner[sl, :] = normed
        inner_t[:, sl] = normed.T
        return carry

    lax.fori_loop(0, length // TILE, norm_two, 0)
    keep_more((inner_t, inner_t_hbm))

    def up_step(i, carry):
        sl = at(i * TILE, TILE, TILE)
        value = mul(inner[...], up[:, sl]) + rows_out[2:3, sl]
        upper[:, sl] = value
        act = (value / (1.0 + jnp.exp(-value))).astype(BF16)
        lower[:, sl] = act
        lower_t[sl, :] = act.T
        return carry

    lax.fori_loop(0, tiles, up_step, 0)
    keep_more((upper, upper_hbm), (lower_t, lower_t_hbm))

    def down_step(i, carry):
        sl = at(i * TILE, TILE, TILE)
        output[:, sl] = (hidden[:, sl] + (mul(lower[...], down[:, sl]) + rows_out[3:4, sl])).astype(BF16)
        return carry

    lax.fori_loop(0, tiles, down_step, 0)
    keep_more((output, output_hbm))

    if not alone:

        @pl.when(far_ok)
        def _():
            for copy in far:
                copy.wait_send()

        @pl.when(even)
        def _():
            for copy in near:
                copy.wait_send()

    for copy in vecs:
        copy.wait_send()
    for group in groups:
        group.drain()
    for copy in keep:
        copy.wait()


def forward(count, tokens, earlier, segs, vec, factor, w_qkv, w_out, w_up, w_down):
    length, width = tokens.shape
    total = 3 * length
    heads = width // HEAD
    inputs = [x for x in (tokens, earlier, segs, vec, factor, w_qkv, w_out, w_up, w_down) if x is not None]
    if earlier is None:
        params = pltpu.CompilerParams(collective_id=0, has_side_effects=True, vmem_limit_bytes=VMEM_LIMIT)
    else:
        params = pltpu.CompilerParams(vmem_limit_bytes=VMEM_LIMIT)
    shape = jax.ShapeDtypeStruct
    outs = (
        shape((length, width), BF16),
        shape((width, total), BF16),
        shape((width, length), BF16),
        shape((width, total), BF16),
        shape((width, total), BF16),
        shape((width, length), BF16),
        shape((heads, 1, length), F32),
        shape((length, width), F32),
        shape((width, length), BF16),
        shape((length, width), F32),
        shape((width, length), BF16),
        shape((8, width), F32),
        shape((width, 3 * width), BF16),
        shape((width, width), BF16),
        shape((width, width), BF16),
        shape((width, width), BF16),
        shape((total, length), F32),
    )
    specs = [ANY] * 17
    specs[6] = specs[11] = VM
    buffer = pltpu.VMEM
    return pl.pallas_call(
        functools.partial(forward_kernel, count) if earlier is not None else lambda *refs: forward_kernel(count, refs[0], None, *refs[1:]),
        name="forward_layer",
        out_shape=outs,
        in_specs=[ANY] * (len(inputs) - 5) + [VM] + [ANY] * 4,
        out_specs=tuple(specs),
        scratch_shapes=[
            buffer((3,) + segs.shape[-2:], jnp.int32),
            buffer((count,) + vec.shape[-2:], BF16),
            buffer((width, 3 * width), BF16),
            buffer((width, width), BF16),
            buffer((width, width), BF16),
            buffer((width, width), BF16),
            buffer((total, width), BF16),
            buffer((width, total), BF16),
            buffer((width, length), BF16),
            buffer((width, total), BF16),
            buffer((width, total), BF16),
            buffer((width, length), BF16),
            buffer((length, width), BF16),
            buffer((length, width), BF16),
            buffer((length, width), F32),
            buffer((length, width), F32),
            buffer((width, length), BF16),
            buffer((width, length), BF16),
            buffer((total, length), F32),
            buffer((length, width), BF16),
            pltpu.SemaphoreType.DMA((256,)),
            pltpu.SemaphoreType.DMA((256,)),
            pltpu.SemaphoreType.DMA((32,)),
        ],
        compiler_params=params,
    )(*inputs)


def backward_kernel(*refs):
    (cot, mask, gain_two, hidden, inner_t, upper, lower_t, o_t, q_t, k_t, v_t, lse, out, up, down) = refs[:15]
    (down_grad, up_grad, out_grad, grad_hidden, dq_t, dk_t, dv_t, rows_out) = refs[15:23]
    grad_upper, grad_attn, do_t = refs[23:]
    length, width = cot.shape
    tiles = width // TILE
    rows_out[...] = jnp.zeros_like(rows_out)

    def down_step(i, carry):
        sl = at(i * TILE, TILE, TILE)
        down_grad[:, sl] = mul(lower_t[...], cot[:, sl]).astype(BF16)
        grad_lower = mul(cot[...], down[sl, :], 1, 1)
        value = upper[:, sl]
        gate = 1.0 / (1.0 + jnp.exp(-value))
        grad = (grad_lower * (gate + value * gate * (1.0 - gate))).astype(BF16)
        grad_upper[:, sl] = grad
        rows_out[2:3, sl] = jnp.sum(grad.astype(F32), axis=0, keepdims=True)
        rows_out[3:4, sl] = jnp.sum(cot[:, sl].astype(F32), axis=0, keepdims=True)
        return carry

    lax.fori_loop(0, tiles, down_step, 0)

    def up_step(i, carry):
        sl = at(i * TILE, TILE, TILE)
        up_grad[:, sl] = mul(inner_t[...], grad_upper[:, sl]).astype(BF16)
        grad_hidden[:, sl] = mul(grad_upper[...], up[sl, :], 1, 1)
        return carry

    lax.fori_loop(0, tiles, up_step, 0)

    def norm_step(i, carry):
        sl = at(i * TILE, TILE, TILE)
        value = hidden[sl, :]
        scale = lax.rsqrt(jnp.mean(value * value, axis=-1, keepdims=True) + EPS)
        normed = value * scale
        grad = grad_hidden[sl, :]
        rows_out[1:2, :] += jnp.sum(grad * normed, axis=0, keepdims=True)
        weighted = grad * gain_two[...]
        along = jnp.mean(weighted * normed, axis=-1, keepdims=True)
        total = cot[sl, :].astype(F32) + scale * (weighted - normed * along)
        grad_hidden[sl, :] = total
        grad_attn[sl, :] = total.astype(BF16)
        return carry

    lax.fori_loop(0, length // TILE, norm_step, 0)

    def out_step(i, carry):
        sl = at(i * TILE, TILE, TILE)
        out_grad[:, sl] = mul(o_t[...], grad_attn[:, sl]).astype(BF16)
        do_t[sl, :] = mul(grad_attn[...], out[sl, :], 1, 1).astype(BF16).T
        return carry

    lax.fori_loop(0, tiles, out_step, 0)

    def attend(h, carry):
        sl = at(h * HEAD, HEAD, 16)
        query, key, grad = q_t[sl, :], k_t[sl, :], do_t[sl, :]
        probs = jnp.exp2(mul(key.T, query) + mask[...] - lse[h])
        delta = jnp.sum(o_t[sl, :].astype(F32) * grad.astype(F32), axis=0, keepdims=True)
        scores = (probs * (mul(v_t[sl, :].T, grad) - delta)).astype(BF16)
        dv_t[sl, :] = mul(grad, probs.astype(BF16), 1, 1).astype(BF16)
        dk_t[sl, :] = (mul(query, scores, 1, 1) * LN2).astype(BF16)
        dq_t[sl, :] = mul(key, scores)
        return carry

    lax.fori_loop(0, width // HEAD, attend, 0)


def backward(cot, mask, gain_two, hidden, inner_t, upper, lower_t, o_t, q_t, k_t, v_t, lse, out, up, down):
    length, width = cot.shape
    total = k_t.shape[1]
    shape = jax.ShapeDtypeStruct
    return pl.pallas_call(
        backward_kernel,
        name="backward_layer",
        out_shape=(
            shape((width, width), BF16),
            shape((width, width), BF16),
            shape((width, width), BF16),
            shape((length, width), F32),
            shape((width, length), F32),
            shape((width, total), BF16),
            shape((width, total), BF16),
            shape((8, width), F32),
        ),
        in_specs=[VM] * 15,
        out_specs=(VM,) * 8,
        scratch_shapes=[
            pltpu.VMEM((length, width), BF16),
            pltpu.VMEM((length, width), BF16),
            pltpu.VMEM((width, length), BF16),
        ],
        compiler_params=pltpu.CompilerParams(vmem_limit_bytes=VMEM_LIMIT),
    )(cot, mask, gain_two, hidden, inner_t, upper, lower_t, o_t, q_t, k_t, v_t, lse, out, up, down)


def project_back_kernel(*refs):
    (dq_t, dk_t, dv_t, q_t, acted_t, qkv, factor, gain_one) = refs[:8]
    (qkv_grad, grad_acted, gain_row, scale_col) = refs[8:12]
    (dq_low,) = refs[12:]
    width, total = acted_t.shape
    length = dq_t.shape[1]
    tiles = width // TILE
    own = pl.ds(total - length, length)
    scale_col[...] = jnp.zeros_like(scale_col)

    def scale_step(h, carry):
        sl = at(h * HEAD, HEAD, 16)
        grad = dq_t[sl, :]
        scale_col[...] += jnp.sum(grad * q_t[sl, :].astype(F32), axis=1, keepdims=True)
        dq_low[sl, :] = (grad * factor[sl, :]).astype(BF16)
        return carry

    lax.fori_loop(0, width // HEAD, scale_step, 0)

    def weight_step(i, carry):
        sl = at(i * TILE, TILE, TILE)
        qkv_grad[:, sl] = mul(acted_t[:, own], dq_low[sl, :], 1, 1).astype(BF16)
        qkv_grad[:, at(width + i * TILE, TILE, TILE)] = mul(acted_t[...], dk_t[sl, :], 1, 1).astype(BF16)
        qkv_grad[:, at(2 * width + i * TILE, TILE, TILE)] = mul(acted_t[...], dv_t[sl, :], 1, 1).astype(BF16)
        return carry

    lax.fori_loop(0, tiles, weight_step, 0)

    def state_step(i, carry):
        sl = at(i * TILE, TILE, TILE)
        wide = mul(qkv[sl, width : 2 * width], dk_t[...]) + mul(qkv[sl, 2 * width : 3 * width], dv_t[...])
        mine = wide[:, total - length :] + mul(qkv[sl, :width], dq_low[...])
        both = jnp.concatenate([wide[:, : total - length], mine], axis=1)
        low = both.astype(BF16)
        sums = jnp.sum(both * acted_t[sl, :].astype(F32), axis=1, keepdims=True)
        gain_row[sl, :] = sums / gain_one[sl, :]
        for j in range(total // length):
            grad_acted[j, :, sl] = low[:, j * length : (j + 1) * length].T
        return carry

    lax.fori_loop(0, tiles, state_step, 0)


def project_back(dq_t, dk_t, dv_t, q_t, acted_t, qkv, factor, gain_one):
    width, total = acted_t.shape
    length = dq_t.shape[1]
    shape = jax.ShapeDtypeStruct
    return pl.pallas_call(
        project_back_kernel,
        name="backward_projection",
        out_shape=(
            shape((width, 3 * width), BF16),
            shape((total // length, length, width), BF16),
            shape((width, 1), F32),
            shape((HEAD, 1), F32),
        ),
        in_specs=[VM] * 8,
        out_specs=(VM,) * 4,
        scratch_shapes=[pltpu.VMEM((width, length), BF16)],
        compiler_params=pltpu.CompilerParams(vmem_limit_bytes=VMEM_LIMIT),
    )(dq_t, dk_t, dv_t, q_t, acted_t, qkv, factor, gain_one)


def reduce_kernel(count, *refs):
    (qkv_grad, out_grad, up_grad, down_grad, grad_acted, small) = refs[:6]
    (qkv_own, out_own, up_own, down_own, acted_own, small_sum) = refs[6:12]
    (acc, core_in, stage_in, result, far_in, near_in, far_out, small_now, small_in, send, recv, lsem) = refs[12:]
    rep, shard = lax.axis_index("rep"), lax.axis_index("shard")
    core, cross = lax.rem(rep, 2), lax.div(rep, 2)
    bits = count.bit_length() - 1
    width = out_grad.shape[1]
    rows = width // count
    half = rows // 2
    cols = width // 2
    length = grad_acted.shape[1]
    sems = Sems(send, recv)

    def block(weight, part_no, core_no):
        if weight == 0:
            return (out_grad, up_grad, down_grad)[part_no].at[:, at(core_no * cols, cols, 128)]
        return qkv_grad.at[:, at(part_no * width + core_no * cols, cols, 128)]

    loads = []
    for weight in (0, 1):
        for part_no in range(3):
            slot = 3 * weight + part_no
            copy = pltpu.make_async_copy(block(weight, part_no, core), acc.at[slot], lsem.at[slot])
            copy.start()
            loads.append(copy)
    fetch = pltpu.make_async_copy(small, small_now.at[0], lsem.at[6])
    fetch.start()
    mine = pltpu.make_async_copy(grad_acted.at[2], acted_own.at[0], lsem.at[7])
    mine.start()
    greet(count)

    pending = []
    exchange = []
    for weight in (0, 1):
        for part_no in range(3):
            copy = sems.remote(block(weight, part_no, 1 - core), core_in.at[3 * weight + part_no], flip(rep, 1), shard)
            copy.start()
            exchange.append(copy)
    pending += exchange

    odd = lax.rem(shard, 2) == 1
    far_ok, far_got = shard >= 2, shard < count - 2
    buddy = flip(shard, 1)
    far_to = lax.rem(shard + count - 2, count)
    give = sems.remote(grad_acted.at[1], near_in, rep, buddy)
    far = sems.remote(far_out, acted_own.at[1], rep, far_to)
    load_far = pltpu.make_async_copy(grad_acted.at[0], far_in, lsem.at[8])
    load_far.start()

    @pl.when(odd | far_ok)
    def _():
        give.start()

    def small_stage(number):
        partner = ("core", "x") + tuple(range(bits))
        what = partner[number]
        to_rep = flip(rep, 1) if what == "core" else flip(rep, 2) if what == "x" else rep
        to_shard = flip(shard, 1 << what) if isinstance(what, int) else shard
        return sems.remote(small_now.at[number], small_in.at[number], to_rep, to_shard)

    fetch.wait()
    small_copy = small_stage(0)
    small_copy.start()
    small_number = 0

    def add_rows(slot, row, size, other):
        sl = at(row, size, 16)
        acc[slot, sl, :] = (acc[slot, sl, :].astype(F32) + other.astype(F32)).astype(BF16)

    def add_core(slot):
        def step(i, carry):
            sl = at(i * TILE, TILE, TILE)
            acc[slot, sl, :] = (acc[slot, sl, :].astype(F32) + core_in[slot, sl, :].astype(F32)).astype(BF16)
            return carry

        lax.fori_loop(0, width // TILE, step, 0)

    orders = stage_orders(bits)
    for weight in (0, 1):
        left = [list(range(bits)) for _ in range(3)]
        done_x = [False] * 3
        arriving = [[] for _ in range(3)]
        base = [0] * 3
        for stage in range(bits + 2):
            for part_no in range(3):
                slot = 3 * weight + part_no
                if stage == 0:
                    loads[slot].wait()
                    exchange[slot].wait_recv()
                    add_core(slot)
                for copy, row, size, spot in arriving[part_no]:
                    copy.wait_recv()
                    add_rows(slot, row, size, stage_in[slot, pl.ds(spot, size), :])
                arriving[part_no] = []
                if stage > bits:
                    continue
                what = orders[part_no][stage]
                if what == "x":
                    for mask in span(left[part_no]):
                        row = flip(shard, mask) * rows
                        spot = base[part_no]
                        copy = sems.remote(
                            acc.at[slot, at(row + (1 - cross) * half, half, 16)],
                            stage_in.at[slot, pl.ds(spot, half)],
                            flip(rep, 2),
                            shard,
                        )
                        copy.start()
                        pending.append(copy)
                        arriving[part_no].append((copy, row + cross * half, half, spot))
                        base[part_no] += half
                    done_x[part_no] = True
                else:
                    left[part_no].remove(what)
                    shift, size = (cross * half, half) if done_x[part_no] else (0, rows)
                    for mask in span(left[part_no]):
                        spot = base[part_no]
                        copy = sems.remote(
                            acc.at[slot, at(flip(shard, mask | (1 << what)) * rows + shift, size, 16)],
                            stage_in.at[slot, pl.ds(spot, size)],
                            rep,
                            flip(shard, 1 << what),
                        )
                        copy.start()
                        pending.append(copy)
                        arriving[part_no].append((copy, flip(shard, mask) * rows + shift, size, spot))
                        base[part_no] += size
            if small_number < bits + 2:
                small_copy.wait()
                small_now[small_number + 1] = small_now[small_number] + small_in[small_number]
                small_number += 1
                if small_number < bits + 2:
                    small_copy = small_stage(small_number)
                    small_copy.start()
            if weight == 0 and stage == 1:

                @pl.when(jnp.logical_not(odd) | far_ok)
                def _():
                    give.wait_recv()

                load_far.wait()

                def far_step(i, carry):
                    sl = at(i * 128, 128, 128)
                    value = far_in[sl, :].astype(F32)
                    value = jnp.where(odd, value + near_in[sl, :].astype(F32), value)
                    far_out[sl, :] = value.astype(BF16)
                    return carry

                @pl.when(far_ok)
                def _():
                    lax.fori_loop(0, length // 128, far_step, 0)
                    far.start()

        crossing = []
        for part_no in range(3):
            slot = 3 * weight + part_no
            src = acc.at[slot, at(shard * rows + cross * half, half, 16)]
            copy = sems.remote(src, result.at[slot, core, at(cross * half, half, 16)], flip(rep, 2), shard)
            copy.start()
            crossing.append(copy)
            result[slot, core, at(cross * half, half, 16), :] = acc[slot, at(shard * rows + cross * half, half, 16), :]
        pending += crossing
        sharing = []
        for part_no in range(3):
            slot = 3 * weight + part_no
            crossing[part_no].wait_recv()
            copy = sems.remote(result.at[slot, core], result.at[slot, core], flip(rep, 1), shard)
            copy.start()
            sharing.append(copy)
        pending += sharing
        for part_no in range(3):
            slot = 3 * weight + part_no
            sharing[part_no].wait_recv()
            for side in range(2):
                value = result[slot, side].astype(F32)
                if weight == 0:
                    (out_own, up_own, down_own)[part_no][:, side * cols : (side + 1) * cols] = value
                else:
                    first = part_no * width + side * cols
                    qkv_own[:, first : first + cols] = value

    small_sum[...] = small_now[bits + 2]

    @pl.when(odd | far_ok)
    def _():
        give.wait_send()

    @pl.when(far_ok)
    def _():
        far.wait_send()

    @pl.when(far_got)
    def _():
        far.wait_recv()

    mine.wait()
    keep_near = pltpu.make_async_copy(near_in, acted_own.at[2], lsem.at[9])

    @pl.when(jnp.logical_not(odd))
    def _():
        keep_near.start()
        keep_near.wait()

    for copy in pending:
        copy.wait_send()


def reduce(count, qkv_grad, out_grad, up_grad, down_grad, grad_acted, small):
    width = out_grad.shape[1]
    rows = width // count
    length = grad_acted.shape[1]
    bits = count.bit_length() - 1
    shape = jax.ShapeDtypeStruct
    cols = width // 2
    return pl.pallas_call(
        functools.partial(reduce_kernel, count),
        name="reduce_gradients",
        out_shape=(
            shape((rows, 3 * width), F32),
            shape((rows, width), F32),
            shape((rows, width), F32),
            shape((rows, width), F32),
            shape((3, length, width), BF16),
            shape(small.shape, F32),
        ),
        in_specs=[ANY] * 6,
        out_specs=(VM, VM, VM, VM, ANY, VM),
        scratch_shapes=[
            pltpu.VMEM((6, width, cols), BF16),
            pltpu.VMEM((6, width, cols), BF16),
            pltpu.VMEM((6, width, cols), BF16),
            pltpu.VMEM((6, 2, rows, cols), BF16),
            pltpu.VMEM((length, width), BF16),
            pltpu.VMEM((length, width), BF16),
            pltpu.VMEM((length, width), BF16),
            pltpu.VMEM((bits + 3,) + small.shape, F32),
            pltpu.VMEM((bits + 2,) + small.shape, F32),
            pltpu.SemaphoreType.DMA((256,)),
            pltpu.SemaphoreType.DMA((256,)),
            pltpu.SemaphoreType.DMA((16,)),
        ],
        compiler_params=pltpu.CompilerParams(collective_id=1, has_side_effects=True, vmem_limit_bytes=VMEM_LIMIT),
    )(qkv_grad, out_grad, up_grad, down_grad, grad_acted, small)


def shifted(value, steps):
    count = lax.axis_size("shard")
    first, last = (max(0, -steps), min(count, count - steps))
    return lax.ppermute(value, "shard", [(source, source + steps) for source in range(first, last)])


def gather_plain(tokens, segs, vec, *weights):
    whole = tuple(lax.all_gather(weight, "shard", axis=0, tiled=True) for weight in weights)
    earlier = jnp.concatenate([shifted(tokens, 2), shifted(tokens, 1)])
    seg_ext = jnp.stack([shifted(segs, 2), shifted(segs, 1), segs])
    return (earlier, seg_ext, lax.all_gather(vec, "shard", axis=0)) + whole


def reduce_plain(qkv_grad, out_grad, up_grad, down_grad, grad_acted, small):
    owned = []
    for grad in (qkv_grad, out_grad, up_grad, down_grad):
        part = lax.psum_scatter(grad, "shard", scatter_dimension=0, tiled=True)
        owned.append(lax.psum(part, "rep").astype(F32))
    parts = jnp.stack([grad_acted[2], shifted(grad_acted[0], -2), shifted(grad_acted[1], -1)])
    return (*owned, parts, lax.psum(small, ("rep", "shard")))


def body(
    tokens,
    segments,
    cotangent,
    gain_one,
    qkv_weight,
    query_scale,
    out_weight,
    gain_two,
    up_weight,
    up_bias,
    down_weight,
    down_bias,
):
    count = lax.axis_size("shard")
    shard = lax.axis_index("shard")
    length, width = tokens.shape[1:]
    rows = qkv_weight.shape[0]
    heads = width // HEAD

    vec = jnp.stack([gain_one, gain_two, up_bias, down_bias])
    vec = jnp.pad(vec, ((0, 12), (0, -rows % 128)))
    segs = jnp.broadcast_to(segments, (8, length))
    whole_tiles = rows % 32 == 0 and count >= 4 and count & (count - 1) == 0 and lax.axis_size("rep") == 4
    reduce_all = functools.partial(reduce, count) if whole_tiles else reduce_plain
    factor = LOG2E / math.sqrt(HEAD) * jax.nn.softplus(query_scale)
    factor_row = jnp.tile(factor, heads)[None]
    weights = (qkv_weight, out_weight, up_weight, down_weight)
    earlier = None
    if not whole_tiles:
        earlier, segs, vec, *weights = gather_plain(tokens[0], segs, vec, *weights)
    output, acted_t, q_t, k_t, v_t, o_t, lse, hidden, inner_t, upper, lower_t, rows_in, qkv, out, up, down, mask = forward(
        count, tokens[0], earlier, segs, vec, factor_row * (1.0 / LN2), *weights
    )
    gain_one_row, gain_two_row = rows_in[0:1], rows_in[1:2]
    down_grad, up_grad, out_grad, grad_hidden, dq_t, dk_t, dv_t, rows_out = backward(
        cotangent[0], mask, gain_two_row, hidden, inner_t, upper, lower_t, o_t, q_t, k_t, v_t, lse, out, up, down
    )
    qkv_grad, grad_acted, gain_col, scale_col = project_back(
        dq_t, dk_t, dv_t, q_t, acted_t, qkv, factor_row.reshape(width, 1), gain_one_row.reshape(width, 1)
    )
    scale_row = jnp.pad(scale_col[:, 0], (0, width - HEAD))
    small_rows = jnp.concatenate([gain_col.reshape(1, width), rows_out[1:4], scale_row[None], rows_out[5:]], 0)
    qkv_own, out_own, up_own, down_own, acted_parts, small_sum = reduce_all(
        qkv_grad, out_grad, up_grad, down_grad, grad_acted, small_rows
    )
    far_got = shard < count - 2
    near_got = (lax.rem(shard, 2) == 0) if whole_tiles else (shard < count - 1)
    total = acted_parts[0].astype(F32)
    total += jnp.where(far_got, acted_parts[1], 0).astype(F32)
    total += jnp.where(near_got, acted_parts[2], 0).astype(F32)
    state = tokens[0].astype(F32)
    inverse = lax.rsqrt(jnp.mean(state * state, axis=-1, keepdims=True) + EPS)
    normed = state * inverse
    weighted = total * gain_one_row
    along = jnp.mean(weighted * normed, axis=-1, keepdims=True)
    input_grad = (grad_hidden + inverse * (weighted - normed * along)).astype(BF16)

    mine = lax.dynamic_slice_in_dim(small_sum[:4], shard * rows, rows, 1)
    scale_grad = (
        small_sum[4, :HEAD]
        * LN2
        / factor
        * (LOG2E / math.sqrt(HEAD))
        * jax.nn.sigmoid(query_scale)
    )
    return (
        output[None],
        input_grad[None],
        mine[0],
        qkv_own,
        scale_grad,
        out_own,
        mine[1],
        up_own,
        mine[2],
        down_own,
        mine[3],
    )


def solution(mesh):
    return jax.shard_map(
        body,
        mesh=mesh,
        in_specs=(
            P("rep", "shard", None),
            P("rep", "shard"),
            P("rep", "shard", None),
            P("shard"),
            P("shard", None),
            P(),
            P("shard", None),
            P("shard"),
            P("shard", None),
            P("shard"),
            P("shard", None),
            P("shard"),
        ),
        out_specs=(
            P("rep", "shard", None),
            P("rep", "shard", None),
            P("shard"),
            P("shard", None),
            P(),
            P("shard", None),
            P("shard"),
            P("shard", None),
            P("shard"),
            P("shard", None),
            P("shard"),
        ),
        check_vma=False,
    )
```

```python
import functools
import math

import jax
import jax.numpy as jnp
from jax import lax
from jax.experimental import pallas as pl
from jax.experimental.pallas import tpu as pltpu
from jax.sharding import PartitionSpec as P

HEAD = 80
WINDOW = 1024
EPS = 1e-06
LOG2E = 1.442695041
LN2 = math.log(2.0)
MASKED = -1e30
TILE = 256
MESH = pl.DeviceIdType.MESH
F32 = jnp.float32
BF16 = jnp.bfloat16
VMEM_LIMIT = 62 * 2**20
ANY = pl.BlockSpec(memory_space=pl.ANY)
VM = pl.BlockSpec(memory_space=pltpu.VMEM)


def mul(a, b, left=1, right=0):
    return lax.dot_general(a, b, (((left,), (right,)), ((), ())), preferred_element_type=F32)


def at(start, size, unit):
    return pl.ds(pl.multiple_of(start, unit), size)


def bit_of(index, bit):
    return lax.rem(lax.div(index, 1 << bit), 2)


def flip(index, mask):
    out = index
    bit = 0
    while mask >> bit:
        if (mask >> bit) & 1:
            out = out + (1 - 2 * bit_of(index, bit)) * (1 << bit)
        bit += 1
    return out


def span(bits):
    masks = [0]
    for bit in bits:
        masks = masks + [mask | (1 << bit) for mask in masks]
    return masks


def stage_orders(bits):
    rest = list(range(2, bits))
    return (["x", 0, 1] + rest, [0, 1, "x"] + rest, [1, "x", 0] + rest)


def cross_orders(bits):
    rest = list(range(2, bits))
    return (["x", 0, 1] + rest, ["x", 1, 0] + rest, [0, "x", 1] + rest)


def greet(count):
    rep, shard = lax.axis_index("rep"), lax.axis_index("shard")
    barrier = pltpu.get_barrier_semaphore()
    for step in range(1, count):
        other = lax.rem(shard + step, count)
        pl.semaphore_signal(barrier, inc=1, device_id={"rep": rep, "shard": other}, device_id_type=MESH)
    for mask in (1, 2):
        pl.semaphore_signal(barrier, inc=1, device_id={"rep": flip(rep, mask), "shard": shard}, device_id_type=MESH)
    pl.semaphore_wait(barrier, count + 1)


class Sems:
    def __init__(self, send, recv):
        self.send, self.recv, self.used = send, recv, 0

    def slot(self):
        self.used += 1
        return self.used - 1

    def remote(self, src, dst, rep, shard, slot=None):
        slot = self.slot() if slot is None else slot
        return pltpu.make_async_remote_copy(
            src_ref=src,
            dst_ref=dst,
            send_sem=self.send.at[slot],
            recv_sem=self.recv.at[slot],
            device_id={"rep": rep, "shard": shard},
            device_id_type=MESH,
        )


class Doubling:
    def __init__(self, sems, count, rows, orders, parts):
        self.sems, self.rows, self.half, self.parts = sems, rows, rows // 2, parts
        bits = count.bit_length() - 1
        self.stages = bits + 1
        self.plan = []
        for order in orders:
            have, whole, stages = [], False, []
            for what in order[::-1]:
                masks = span(have)[1:] if what == "x" else span(have)
                stages.append([(what, mask, whole, sems.slot(), sems.slot()) for mask in masks])
                if what == "x":
                    whole = True
                else:
                    have.append(what)
            self.plan.append(stages)

    def copy(self, part, step):
        what, mask, whole, slot, _ = step
        rep, shard = lax.axis_index("rep"), lax.axis_index("shard")
        core, cross = lax.rem(rep, 2), lax.div(rep, 2)
        src, dst, first, cols = self.parts[part]
        across = at(first + core * cols, cols, 128)
        shift, size = (0, self.rows) if whole else (cross * self.half, self.half)
        row = flip(shard, mask) * self.rows + shift
        to = dst.at[at(row, size, 16), across]
        here = src.at[at(shift, size, 16), across] if mask == 0 else to
        if what == "x":
            return self.sems.remote(here, to, flip(rep, 2), shard, slot)
        return self.sems.remote(here, to, rep, flip(shard, 1 << what), slot)

    def ahead(self, part, step):
        what, mask, whole, _, slot = step
        rep, shard = lax.axis_index("rep"), lax.axis_index("shard")
        core, cross = lax.rem(rep, 2), lax.div(rep, 2)
        _, dst, first, cols = self.parts[part]
        if what == "x":
            row, size = flip(shard, mask) * self.rows + (1 - cross) * self.half, self.half
        else:
            shift, size = (0, self.rows) if whole else (cross * self.half, self.half)
            row = flip(shard, mask | (1 << what)) * self.rows + shift
        spot = dst.at[at(row, size, 16), at(first + core * cols, cols, 128)]
        return self.sems.remote(spot, spot, flip(rep, 1), shard, slot)

    def send(self, stage):
        for part in range(3):
            for step in self.plan[part][stage]:
                self.copy(part, step).start()

    def settle(self, stage):
        for part in range(3):
            for step in self.plan[part][stage]:
                self.copy(part, step).wait_recv()
                self.ahead(part, step).start()

    def move(self, stage):
        for part in range(3):
            for step in self.plan[part][stage]:
                self.copy(part, step).wait_recv()
            for step in self.plan[part][stage + 1]:
                self.copy(part, step).start()
            for step in self.plan[part][stage]:
                self.ahead(part, step).start()

    def finish(self):
        for part in range(3):
            for stage in self.plan[part]:
                for step in stage:
                    self.ahead(part, step).wait_recv()

    def drain(self):
        for part in range(3):
            for stage in self.plan[part]:
                for step in stage:
                    self.copy(part, step).wait_send()
                    self.ahead(part, step).wait_send()


def tail_orders(bits):
    rest = list(range(2, bits))
    return (["x", 0, 1] + rest, ["x", 1, 0] + rest, [0, "x", 1] + rest)


def beside_orders(bits):
    rest = list(range(2, bits))
    return (["x", 0, 1] + rest, [0, 1, "x"] + rest, [1, 0, "x"] + rest)


class Gathered:
    stages = 1

    def send(self, stage):
        pass

    settle = move = send

    def finish(self):
        pass

    drain = finish


def forward_kernel(count, *refs):
    (tokens, earlier, segs, vec, factor, w_qkv, w_out, w_up, w_down) = refs[:9]
    results = refs[9:26]
    alone = earlier is not None
    (
        output_hbm, acted_t_hbm, q_t_hbm, k_t_hbm, v_t_hbm, o_t_hbm, lse, hidden_hbm,
        inner_t_hbm, upper_hbm, lower_t_hbm, rows_out, qkv_hbm, out_hbm, up_hbm, down_hbm, mask_hbm,
    ) = results
    (
        seg_ext, vec_full, qkv, out, up, down, acted, acted_t, q_t, k_t, v_t, o_t, heads, inner,
        hidden, upper, inner_t, lower_t, mask, state_low, send, recv, lsem,
    ) = refs[26:]
    rep, shard = lax.axis_index("rep"), lax.axis_index("shard")
    length, width = tokens.shape
    total = 3 * length
    rows = w_qkv.shape[0]
    tiles = width // TILE
    own = pl.ds(total - length, length)
    sems = Sems(send, recv)
    lower, output = heads, inner
    bits = count.bit_length() - 1

    first_cols = (tiles * 3 // 5) * TILE
    rest_cols = width - first_cols
    groups = (Gathered(),) * 3 if alone else (
        Doubling(sems, count, rows, cross_orders(bits), [(w_qkv, qkv, p * width, first_cols // 2) for p in range(3)]),
        Doubling(sems, count, rows, stage_orders(bits), [(w_qkv, qkv, p * width + first_cols, rest_cols // 2) for p in range(3)]),
        Doubling(sems, count, rows, stage_orders(bits), [(w, full, 0, width // 2) for w, full in ((w_out, out), (w_up, up), (w_down, down))]),
    )

    pairs = [(tokens, acted.at[own]), (tokens, state_low)]
    if alone:
        pairs += [(earlier, acted.at[pl.ds(0, 2 * length)]), (segs, seg_ext), (vec, vec_full)]
        pairs += [(w_qkv, qkv), (w_out, out), (w_up, up), (w_down, down)]
    else:
        mine = at(shard * rows, rows, 16)
        pairs += [(segs, seg_ext.at[2]), (vec, vec_full.at[shard])]
        pairs += [(w_qkv, qkv.at[mine]), (w_out, out.at[mine]), (w_up, up.at[mine]), (w_down, down.at[mine])]
    loads = [pltpu.make_async_copy(src, dst, lsem.at[i]) for i, (src, dst) in enumerate(pairs)]
    for copy in loads:
        copy.start()

    odd = lax.rem(shard, 2) == 1
    even = jnp.logical_not(odd)
    far_ok, far_got = shard < count - 2, shard >= 2
    buddy = flip(shard, 1)
    far_to = lax.rem(shard + 2, count)
    nchunk = 8
    part = length // nchunk
    far, near, relay, vecs = [], [], [], []
    for i in range(0 if alone else nchunk):
        here = pl.ds(i * part, part)
        far_spot, near_spot = acted.at[pl.ds(i * part, part)], acted.at[pl.ds(length + i * part, part)]
        slot = sems.slot()
        far.append(sems.remote(tokens.at[here], far_spot, rep, far_to, sems.slot()))
        near.append(sems.remote(tokens.at[here], near_spot, rep, buddy, slot))
        relay.append(sems.remote(far_spot, near_spot, rep, buddy, slot))
    if not alone:
        slot = sems.slot()
        far.append(sems.remote(segs, seg_ext.at[0], rep, far_to, sems.slot()))
        near.append(sems.remote(segs, seg_ext.at[1], rep, buddy, slot))
        relay.append(sems.remote(seg_ext.at[0], seg_ext.at[1], rep, buddy, slot))
        vecs = [
            sems.remote(vec, vec_full.at[shard], rep, lax.rem(shard + step, count), sems.slot()) for step in range(1, count)
        ]

    def far_start(*which):
        @pl.when(far_ok)
        def _():
            for i in which:
                far[i].start()

    def near_start(*which):
        @pl.when(even)
        def _():
            for i in which:
                near[i].start()

    def far_next(i):
        @pl.when(far_ok)
        def _():
            far[i].wait_send()
            far[i + 2].start()

    def near_next(i):
        @pl.when(even)
        def _():
            near[i].wait_send()
            near[i + 2].start()

    def relay_start(*which):
        @pl.when(far_got)
        def _():
            for i in which:
                far[i].wait_recv()

        @pl.when(odd & far_got)
        def _():
            for i in which:
                relay[i].start()

    if not alone:
        greet(count)
        groups[0].send(0)
        far_start(nchunk, 0, 1)
        near_start(nchunk, 0, 1)
        for copy in vecs:
            copy.start()
        groups[0].move(0)
        relay_start(nchunk)
        for i in range(nchunk):
            relay_start(i)
            if i + 2 < nchunk:
                far_next(i)
                near_next(i)
            if i == 1:
                groups[0].move(1)
            if i == 4:
                groups[0].move(2)

    for copy in loads:
        copy.wait()
    for copy in vecs:
        copy.wait_recv()
    each = width // count
    vectors = jnp.concatenate([vec_full[i][:, :each].astype(F32) for i in range(count)], axis=1)
    rows_out[...] = vectors[:8, :]
    gain_one, gain_two = rows_out[0:1, :], rows_out[1:2, :]

    def norm_rows(i):
        sl = at(i * TILE, TILE, TILE)
        state = acted[sl, :].astype(F32)
        scale = lax.rsqrt(jnp.mean(state * state, axis=-1, keepdims=True) + EPS)
        value = (state * scale * rows_out[0:1, :]).astype(BF16)
        value = jnp.where(shard + i * TILE // length >= 2, value, jnp.zeros_like(value))
        acted[sl, :] = value
        acted_t[:, sl] = value.T

    def norm_step(i, carry):
        norm_rows(i)
        return carry

    per = length // TILE
    lax.fori_loop(2 * per, 3 * per, norm_step, 0)

    if not alone:

        @pl.when(odd)
        def _():
            for copy in near:
                copy.wait_recv()

        @pl.when(even & far_got)
        def _():
            for copy in relay:
                copy.wait_recv()

        @pl.when(odd & far_got)
        def _():
            for copy in relay:
                copy.wait_send()

    lax.fori_loop(0, 2 * per, norm_step, 0)

    mine = seg_ext[2].astype(F32)[0:1, :]
    for j in range(3):
        column = jnp.where(shard + j >= 2, seg_ext[j].astype(F32).T[:, 0:1], -1.0)
        place = lax.broadcasted_iota(jnp.int32, (length, length), 0) + j * length
        lane = lax.broadcasted_iota(jnp.int32, (length, length), 1)
        near_by = (place > lane) & (place <= lane + WINDOW)
        mask[j * length : (j + 1) * length, :] = jnp.where(near_by & (column == mine), 0.0, MASKED)

    groups[1].send(0)
    groups[0].settle(groups[0].stages - 1)
    groups[0].finish()
    groups[1].move(0)

    def project(i, carry):
        sl = at(i * TILE, TILE, TILE)
        q_t[sl, :] = (mul(acted[own, :], qkv[:, sl]) * factor[:, sl]).astype(BF16).T
        k_t[sl, :] = mul(acted[...], qkv[:, at(width + i * TILE, TILE, TILE)]).astype(BF16).T
        v_t[sl, :] = mul(acted[...], qkv[:, at(2 * width + i * TILE, TILE, TILE)]).astype(BF16).T
        return carry

    def project_first(i, carry):
        project(i, carry)

        @pl.when(i == 0)
        def _():
            groups[1].move(1)

        @pl.when(i == 2)
        def _():
            groups[1].move(2)
            groups[2].send(0)

        return carry

    lax.fori_loop(0, first_cols // TILE, project_first, 0)

    def attend(h):
        sl = at(h * HEAD, HEAD, 16)
        scores = mul(k_t[sl, :].T, q_t[sl, :]) + mask[...]
        top = jnp.max(scores, axis=0, keepdims=True)
        probs = jnp.exp2(scores - top)
        norm = jnp.sum(probs, axis=0, keepdims=True)
        o_t[sl, :] = (mul(v_t[sl, :], probs.astype(BF16)) * (1.0 / norm)).astype(BF16)
        lse[h] = top + jnp.log2(norm)

    ready = first_cols // HEAD
    count_heads = width // HEAD

    def attend_first(h, carry):
        attend(h)

        @pl.when(h == 4)
        def _():
            groups[1].settle(groups[1].stages - 1)
            groups[2].move(0)

        @pl.when(h == 7)
        def _():
            groups[2].move(1)

        return carry

    lax.fori_loop(0, ready, attend_first, 0)
    groups[1].finish()
    lax.fori_loop(first_cols // TILE, tiles, project, 0)
    keep = [
        pltpu.make_async_copy(src, dst, lsem.at[8 + i])
        for i, (src, dst) in enumerate(((qkv, qkv_hbm), (acted_t, acted_t_hbm), (q_t, q_t_hbm), (k_t, k_t_hbm), (v_t, v_t_hbm), (mask, mask_hbm)))
    ]
    for copy in keep:
        copy.start()

    def attend_rest(h, carry):
        attend(h)

        @pl.when(h == ready)
        def _():
            groups[2].move(2)

        return carry

    lax.fori_loop(ready, count_heads, attend_rest, 0)

    def keep_more(*pairs):
        for src, dst in pairs:
            copy = pltpu.make_async_copy(src, dst, lsem.at[8 + len(keep)])
            copy.start()
            keep.append(copy)

    keep_more((o_t, o_t_hbm))

    def turn(i, carry):
        sl = at(i * TILE, TILE, TILE)
        heads[:, sl] = o_t[sl, :].T
        return carry

    lax.fori_loop(0, tiles, turn, 0)
    groups[2].settle(groups[2].stages - 1)
    groups[2].finish()
    keep_more((out, out_hbm), (up, up_hbm), (down, down_hbm))

    def out_step(i, carry):
        sl = at(i * TILE, TILE, TILE)
        hidden[:, sl] = state_low[:, sl].astype(F32) + mul(heads[...], out[:, sl])
        return carry

    lax.fori_loop(0, tiles, out_step, 0)
    keep_more((hidden, hidden_hbm))

    def norm_two(i, carry):
        sl = at(i * TILE, TILE, TILE)
        value = hidden[sl, :]
        scale = lax.rsqrt(jnp.mean(value * value, axis=-1, keepdims=True) + EPS)
        normed = (value * scale * rows_out[1:2, :]).astype(BF16)
        inner[sl, :] = normed
        inner_t[:, sl] = normed.T
        return carry

    lax.fori_loop(0, length // TILE, norm_two, 0)
    keep_more((inner_t, inner_t_hbm))

    def up_step(i, carry):
        sl = at(i * TILE, TILE, TILE)
        value = mul(inner[...], up[:, sl]) + rows_out[2:3, sl]
        upper[:, sl] = value
        act = (value / (1.0 + jnp.exp(-value))).astype(BF16)
        lower[:, sl] = act
        lower_t[sl, :] = act.T
        return carry

    lax.fori_loop(0, tiles, up_step, 0)
    keep_more((upper, upper_hbm), (lower_t, lower_t_hbm))

    def down_step(i, carry):
        sl = at(i * TILE, TILE, TILE)
        output[:, sl] = (hidden[:, sl] + (mul(lower[...], down[:, sl]) + rows_out[3:4, sl])).astype(BF16)
        return carry

    lax.fori_loop(0, tiles, down_step, 0)
    keep_more((output, output_hbm))

    if not alone:

        @pl.when(far_ok)
        def _():
            for copy in far[nchunk - 2 :]:
                copy.wait_send()

        @pl.when(even)
        def _():
            for copy in near[nchunk - 2 :]:
                copy.wait_send()

    for copy in vecs:
        copy.wait_send()
    for group in groups:
        group.drain()
    for copy in keep:
        copy.wait()


def forward(count, tokens, earlier, segs, vec, factor, w_qkv, w_out, w_up, w_down):
    length, width = tokens.shape
    total = 3 * length
    heads = width // HEAD
    inputs = [x for x in (tokens, earlier, segs, vec, factor, w_qkv, w_out, w_up, w_down) if x is not None]
    if earlier is None:
        params = pltpu.CompilerParams(collective_id=0, has_side_effects=True, vmem_limit_bytes=VMEM_LIMIT)
    else:
        params = pltpu.CompilerParams(vmem_limit_bytes=VMEM_LIMIT)
    shape = jax.ShapeDtypeStruct
    outs = (
        shape((length, width), BF16),
        shape((width, total), BF16),
        shape((width, length), BF16),
        shape((width, total), BF16),
        shape((width, total), BF16),
        shape((width, length), BF16),
        shape((heads, 1, length), F32),
        shape((length, width), F32),
        shape((width, length), BF16),
        shape((length, width), F32),
        shape((width, length), BF16),
        shape((8, width), F32),
        shape((width, 3 * width), BF16),
        shape((width, width), BF16),
        shape((width, width), BF16),
        shape((width, width), BF16),
        shape((total, length), F32),
    )
    specs = [ANY] * 17
    specs[6] = specs[11] = VM
    buffer = pltpu.VMEM
    return pl.pallas_call(
        functools.partial(forward_kernel, count) if earlier is not None else lambda *refs: forward_kernel(count, refs[0], None, *refs[1:]),
        name="forward_layer",
        out_shape=outs,
        in_specs=[ANY] * (len(inputs) - 5) + [VM] + [ANY] * 4,
        out_specs=tuple(specs),
        scratch_shapes=[
            buffer((3,) + segs.shape[-2:], jnp.int32),
            buffer((count,) + vec.shape[-2:], BF16),
            buffer((width, 3 * width), BF16),
            buffer((width, width), BF16),
            buffer((width, width), BF16),
            buffer((width, width), BF16),
            buffer((total, width), BF16),
            buffer((width, total), BF16),
            buffer((width, length), BF16),
            buffer((width, total), BF16),
            buffer((width, total), BF16),
            buffer((width, length), BF16),
            buffer((length, width), BF16),
            buffer((length, width), BF16),
            buffer((length, width), F32),
            buffer((length, width), F32),
            buffer((width, length), BF16),
            buffer((width, length), BF16),
            buffer((total, length), F32),
            buffer((length, width), BF16),
            pltpu.SemaphoreType.DMA((256,)),
            pltpu.SemaphoreType.DMA((256,)),
            pltpu.SemaphoreType.DMA((32,)),
        ],
        compiler_params=params,
    )(*inputs)


class Halving:
    def __init__(self, sems, credits, count, rows, orders, acc, other, land, result, reused):
        self.sems, self.credits, self.rows, self.half, self.reused = sems, credits, rows, rows // 2, reused
        self.acc, self.other, self.land, self.result = acc, other, land, result
        self.bits = count.bit_length() - 1
        self.plan, self.core_slot, self.cross_slot, self.share_slot = [], [], [], []
        self.at_stage = [0] * 3
        for order in orders:
            left, whole, base, stages = list(range(self.bits)), True, 0, []
            for what in order:
                steps = []
                if what == "x":
                    whole = False
                else:
                    left.remove(what)
                for mask in span(left):
                    size = rows if whole else self.half
                    steps.append((mask, base, size, sems.slot()))
                    base += size
                stages.append((what, whole, steps))
            self.plan.append(stages)
            self.core_slot.append(sems.slot())
            self.cross_slot.append(sems.slot())
            self.share_slot.append(sems.slot())

    def partner(self, what):
        rep, shard = lax.axis_index("rep"), lax.axis_index("shard")
        if what == "core":
            return flip(rep, 1), shard
        if what == "x":
            return flip(rep, 2), shard
        return rep, flip(shard, 1 << what)

    def credit(self, part, what):
        place = 0 if what == "core" else 1 if what == "x" else 2 + what
        return self.credits.at[part * (self.bits + 2) + place]

    def allow(self, part, what):
        rep, shard = self.partner(what)
        pl.semaphore_signal(
            self.credit(part, what), inc=1, device_id={"rep": rep, "shard": shard}, device_id_type=MESH
        )

    def core_copy(self, part):
        return self.sems.remote(self.other[part], self.land[part], *self.partner("core"), self.core_slot[part])

    def core_send(self, part):
        if self.reused:
            pl.semaphore_wait(self.credit(part, "core"), 1)
        self.core_copy(part).start()

    def core_add(self, part):
        self.core_copy(part).wait_recv()
        acc, land = self.acc[part], self.land[part]

        def step(i, carry):
            sl = at(i * TILE, TILE, TILE)
            acc[sl, :] = (acc[sl, :].astype(F32) + land[sl, :].astype(F32)).astype(BF16)
            return carry

        lax.fori_loop(0, acc.shape[0] // TILE, step, 0)
        for what, _, _ in self.plan[part]:
            self.allow(part, what)
        self.send(part, 0)

    def copy(self, part, stage, step):
        what, whole, _ = self.plan[part][stage]
        mask, base, size, slot = step
        shard, cross = lax.axis_index("shard"), lax.div(lax.axis_index("rep"), 2)
        if what == "x":
            row = flip(shard, mask) * self.rows + (1 - cross) * self.half
        else:
            row = flip(shard, mask | (1 << what)) * self.rows
            row = row if whole else row + cross * self.half
        src = self.acc[part].at[at(row, size, 16)]
        return self.sems.remote(src, self.land[part].at[pl.ds(base, size)], *self.partner(what), slot)

    def send(self, part, stage):
        what, _, steps = self.plan[part][stage]
        pl.semaphore_wait(self.credit(part, what), 1)
        for step in steps:
            self.copy(part, stage, step).start()

    def receive(self, part, stage):
        what, whole, steps = self.plan[part][stage]
        shard, cross = lax.axis_index("shard"), lax.div(lax.axis_index("rep"), 2)
        for step in steps:
            mask, base, size, _ = step
            self.copy(part, stage, step).wait_recv()
            row = flip(shard, mask) * self.rows
            row = row if whole else row + cross * self.half
            sl = at(row, size, 16)
            new = self.acc[part][sl, :].astype(F32) + self.land[part][pl.ds(base, size), :].astype(F32)
            self.acc[part][sl, :] = new.astype(BF16)

    def advance(self, part):
        stage = self.at_stage[part]
        self.at_stage[part] += 1
        if stage <= self.bits:
            self.receive(part, stage)
        if stage < self.bits:
            self.send(part, stage + 1)
        elif stage == self.bits:
            core, cross = self.sides()
            shard = lax.axis_index("shard")
            row = shard * self.rows + cross * self.half
            self.result[part].at[core][at(cross * self.half, self.half, 16), :] = self.acc[part][at(row, self.half, 16), :]
            self.cross_copy(part).start()
        elif stage == self.bits + 1:
            self.cross_copy(part).wait_recv()
            self.share_copy(part).start()
        else:
            self.share_copy(part).wait_recv()

    def sides(self):
        rep = lax.axis_index("rep")
        return lax.rem(rep, 2), lax.div(rep, 2)

    def cross_copy(self, part):
        core, cross = self.sides()
        spot = self.result[part].at[core, at(cross * self.half, self.half, 16)]
        return self.sems.remote(spot, spot, *self.partner("x"), self.cross_slot[part])

    def share_copy(self, part):
        core, _ = self.sides()
        spot = self.result[part].at[core]
        return self.sems.remote(spot, spot, *self.partner("core"), self.share_slot[part])

    def drain_other(self, part):
        self.core_copy(part).wait_send()

    def drain_acc(self, part):
        for stage in range(self.bits + 1):
            for step in self.plan[part][stage][2]:
                self.copy(part, stage, step).wait_send()

    def drain_result(self, part):
        self.cross_copy(part).wait_send()
        self.share_copy(part).wait_send()


def backward_kernel(count, alone, *refs):
    (
        cot_hbm, tokens_hbm, hidden_hbm, inner_t_hbm, upper_hbm, lower_t_hbm, o_t_hbm, q_t_hbm, k_t_hbm, v_t_hbm,
        acted_t_hbm, qkv_hbm, out_hbm, up_hbm, down_hbm, mask_hbm, lse, rows_in, factor,
    ) = refs[:19]
    if alone:
        (hidden_out, qkv_out, out_out, up_out, down_out, acted_out, small_out) = refs[19:26]
    else:
        (input_grad, qkv_out, out_out, up_out, down_out, small_out) = refs[19:25]
    scratch = refs[26:] if alone else refs[25:]
    (
        wide, flat, wtile, first_f32, grad_hidden, q_t, k_t, v_t, do_t, delta, mask, scale_sum, acc, other, land,
        result_ff, result_qkv, turned, near_in, far_in, state_low, small_now, small_in, lsem, send, recv, credits,
    ) = scratch
    rep, shard = lax.axis_index("rep"), lax.axis_index("shard")
    core = lax.rem(rep, 2)
    length, width = cot_hbm.shape
    total = 3 * length
    tiles = width // TILE
    rows = width // count
    cols = width // 2
    heads = width // HEAD
    own = pl.ds(total - length, length)
    bits = count.bit_length() - 1
    sems = Sems(send, recv)
    lower_t, inner_t, o_t = (wide.at[:, pl.ds(i * length, length)] for i in range(3))
    cot, grad_upper, grad_attn = (flat.at[i] for i in range(3))
    parts = [[ref.at[i] for i in range(3)] for ref in (acc, other, land, result_ff, result_qkv)]

    def local(src, dst, slot):
        return pltpu.make_async_copy(src, dst, lsem.at[slot])

    loads = {
        "cot": local(cot_hbm, cot, 0),
        "lower": local(lower_t_hbm, lower_t, 1),
        "upper": local(upper_hbm, first_f32, 2),
        "inner": local(inner_t_hbm, inner_t, 3),
        "o": local(o_t_hbm, o_t, 4),
        "q": local(q_t_hbm, q_t, 5),
        "k": local(k_t_hbm, k_t, 6),
        "v": local(v_t_hbm, v_t, 7),
        "mask": local(mask_hbm, mask, 8),
        "state": local(tokens_hbm, state_low, 9),
    }
    load_hidden = local(hidden_hbm, first_f32, 10)
    load_acted = local(acted_t_hbm, wide, 11)

    def tile_copy(src, i, slot):
        return local(src.at[at(i * TILE, TILE, TILE)], wtile.at[slot, :, pl.ds(0, src.shape[1])], 12 + slot)

    def tile_next(src, after, i, slot):
        tile_copy(src, i, slot).wait()

        @pl.when(i < tiles - 1)
        def _():
            tile_copy(src, i + 1, 1 - slot).start()

        if after is not None:

            @pl.when(i == tiles - 1)
            def _():
                tile_copy(after, 0, 1 - slot).start()

    for name in ("lower", "cot"):
        loads[name].start()
    tile_copy(down_hbm, 0, 0).start()
    for name in ("upper", "inner", "o", "q", "k", "v", "mask", "state"):
        loads[name].start()
    if alone:
        ff = qkv = None
    else:
        greet(count)
        ff = Halving(sems, credits.at[0], count, rows, beside_orders(bits), *parts[:4], False)
        back = [refs[::-1] for refs in parts[:3]]
        qkv = Halving(sems, credits.at[1], count, rows, tail_orders(bits), *back, parts[4], True)
    copies_out = []

    def weight_side(group, part, left, right, side_core, first_use=False):
        theirs = side_core is not core
        dest = (other if theirs else acc).at[part if first_use else 2 - part]

        def step(i, carry):
            sl = at(i * cols, cols, 16)
            dest[sl, :] = right(left(sl), side_core * cols).astype(BF16)
            return carry

        lax.fori_loop(0, 2, step, 0)
        if theirs and group is not None:
            group.core_send(part)

    def weight_out(part, target, first, first_use=False):
        for ref, side_core in ((other, 1 - core), (acc, core)):
            copy = local(ref.at[part if first_use else 2 - part], target.at[:, at(first + side_core * cols, cols, 128)], 20 + len(copies_out))
            copy.start()
            copies_out.append(copy)

    def weight_grad(group, part, left, right, target):
        weight_side(group, part, left, right, 1 - core, True)
        weight_side(group, part, left, right, core, True)
        if alone:
            weight_out(part, target, 0, True)

    small_now[0] = jnp.zeros_like(small_now[0])
    loads["lower"].wait()
    loads["cot"].wait()
    weight_grad(
        ff, 2, lambda sl: lower_t[sl, :], lambda left, col: mul(left, cot[:, at(col, cols, 128)]), down_out
    )
    loads["upper"].wait()

    def down_step(i, carry):
        sl = at(i * TILE, TILE, TILE)
        slot = lax.rem(i, 2)
        tile_next(down_hbm, up_hbm, i, slot)
        grad_lower = mul(cot[...], wtile[slot, :, :width], 1, 1)
        value = first_f32[:, sl]
        gate = 1.0 / (1.0 + jnp.exp(-value))
        grad = (grad_lower * (gate + value * gate * (1.0 - gate))).astype(BF16)
        grad_upper[:, sl] = grad
        small_now[0, 2:3, sl] = jnp.sum(grad.astype(F32), axis=0, keepdims=True)
        small_now[0, 3:4, sl] = jnp.sum(cot[:, sl].astype(F32), axis=0, keepdims=True)
        return carry

    lax.fori_loop(0, tiles, down_step, 0)
    load_hidden.start()
    loads["inner"].wait()
    weight_grad(
        ff, 1, lambda sl: inner_t[sl, :], lambda left, col: mul(left, grad_upper[:, at(col, cols, 128)]), up_out
    )
    if not alone:
        ff.core_add(2)

    def up_step(i, carry):
        sl = at(i * TILE, TILE, TILE)
        slot = lax.rem(i + tiles, 2)
        tile_next(up_hbm, out_hbm, i, slot)
        grad_hidden[:, sl] = mul(grad_upper[...], wtile[slot, :, :width], 1, 1)
        return carry

    lax.fori_loop(0, tiles, up_step, 0)
    load_hidden.wait()
    if not alone:
        ff.core_add(1)

    def norm_step(i, carry):
        sl = at(i * TILE, TILE, TILE)
        value = first_f32[sl, :]
        scale = lax.rsqrt(jnp.mean(value * value, axis=-1, keepdims=True) + EPS)
        normed = value * scale
        grad = grad_hidden[sl, :]
        small_now[0, 1:2, :] += jnp.sum(grad * normed, axis=0, keepdims=True)
        weighted = grad * rows_in[1:2, :]
        along = jnp.mean(weighted * normed, axis=-1, keepdims=True)
        whole = cot[sl, :].astype(F32) + scale * (weighted - normed * along)
        grad_hidden[sl, :] = whole
        grad_attn[sl, :] = whole.astype(BF16)
        return carry

    lax.fori_loop(0, length // TILE, norm_step, 0)
    loads["o"].wait()
    weight_grad(
        ff, 0, lambda sl: o_t[sl, :], lambda left, col: mul(left, grad_attn[:, at(col, cols, 128)]), out_out
    )

    def out_step(i, carry):
        sl = at(i * TILE, TILE, TILE)
        slot = lax.rem(i, 2)
        tile_next(out_hbm, qkv_hbm, i, slot)
        do_t[sl, :] = mul(grad_attn[...], wtile[slot, :, :width], 1, 1).astype(BF16).T
        return carry

    lax.fori_loop(0, tiles, out_step, 0)
    if not alone:
        ff.core_add(0)

    def delta_step(h, carry):
        sl = at(h * HEAD, HEAD, 16)
        delta[h] = jnp.sum(o_t[sl, :].astype(F32) * do_t[sl, :].astype(F32), axis=0, keepdims=True)
        return carry

    lax.fori_loop(0, heads, delta_step, 0)
    load_acted.start()
    for name in ("q", "k", "v", "mask"):
        loads[name].wait()
    scale_sum[...] = jnp.zeros_like(scale_sum)
    chunk = total // 2

    def attend(h, carry):
        sl = at(h * HEAD, HEAD, 16)
        query, grad = q_t[sl, :], do_t[sl, :]
        dq = jnp.zeros((HEAD, length), F32)
        for c in range(2):
            ks = pl.ds(c * chunk, chunk)
            key, value = k_t[sl, ks], v_t[sl, ks]
            probs = jnp.exp2(mul(key.T, query) + mask[ks, :] - lse[h])
            scores = (probs * (mul(value.T, grad) - delta[h])).astype(BF16)
            v_t[sl, ks] = mul(grad, probs.astype(BF16), 1, 1).astype(BF16)
            k_t[sl, ks] = (mul(query, scores, 1, 1) * LN2).astype(BF16)
            dq += mul(key, scores)
        scale_sum[...] += dq * query.astype(F32)
        q_t[sl, :] = (dq * factor[...]).astype(BF16)
        if not alone:
            for head in sorted({step[0] for step in FF_STEPS}):

                @pl.when(h == head)
                def _():
                    for _, part, stage in [step for step in FF_STEPS if step[0] == head]:
                        ff.at_stage[part] = stage
                        ff.advance(part)
                        if stage == bits:
                            qkv.allow(2 - part, "core")

        return carry

    lax.fori_loop(0, heads, attend, 0)

    def give_result(group, part, target, first):
        for side in range(2):
            slot = side
            turned[slot] = (result_ff if group is ff else result_qkv)[part, side].astype(F32)
            copy = local(turned.at[slot], target.at[:, pl.ds(first + side * cols, cols)], 14 + slot)
            copy.start()
        for side in range(2):
            local(turned.at[side], target.at[:, pl.ds(first + side * cols, cols)], 14 + side).wait()

    load_acted.wait()
    odd = lax.rem(shard, 2) == 1
    even = jnp.logical_not(odd)
    far_ok, far_got = shard >= 2, shard < count - 2
    buddy = flip(shard, 1)
    far_to = lax.rem(shard + count - 2, count)
    give_slots = [sems.slot() for _ in range(tiles)]
    far_slots = [sems.slot() for _ in range(tiles)]

    def give(i):
        sl = pl.ds(i * TILE, TILE)
        return sems.remote(flat.at[1, :, sl], near_in.at[:, sl], rep, buddy, give_slots[i])

    def far(i):
        sl = pl.ds(i * TILE, TILE)
        return sems.remote(flat.at[0, :, sl], far_in.at[:, sl], rep, far_to, far_slots[i])

    def state_step(i):
        sl = pl.ds(i * TILE, TILE)
        slot = (i + 3 * tiles) % 2
        tile_copy(qkv_hbm, i, slot).wait()
        if i < tiles - 1:
            tile_copy(qkv_hbm, i + 1, 1 - slot).start()
        both = mul(wtile[slot, :, width : 2 * width], k_t[...]) + mul(wtile[slot, :, 2 * width :], v_t[...])
        mine = both[:, total - length :] + mul(wtile[slot, :, :width], q_t[...])
        both = jnp.concatenate([both[:, : total - length], mine], axis=1)
        low = both.astype(BF16)
        sums = jnp.sum(both * wide[sl, :].astype(F32), axis=1, keepdims=True)
        small_now[0, 0:1, sl] = jnp.broadcast_to(sums, (TILE, 128)).T[0:1, :] / rows_in[0:1, sl]
        for j in range(3):
            flat[j, :, sl] = low[:, j * length : (j + 1) * length].T

    def give_start(i):
        @pl.when(odd | far_ok)
        def _():
            give(i).start()

    def far_start(i):
        @pl.when(even | far_ok)
        def _():
            give(i).wait_recv()

        @pl.when(odd & far_ok)
        def _():
            sl = pl.ds(i * TILE, TILE)
            flat[0, :, sl] = (flat[0, :, sl].astype(F32) + near_in[:, sl].astype(F32)).astype(BF16)

        @pl.when(far_ok)
        def _():
            far(i).start()

    if alone:
        for copy in copies_out:
            copy.wait()
    else:
        ff.at_stage = [max([step[2] + 1 for step in FF_STEPS if step[1] == part]) for part in range(3)]
        for part in (1, 2):
            ff.drain_other(part)
            ff.drain_acc(part)
    for side_core in (1 - core, core):
        weight_side(
            qkv, 0, lambda sl: wide[sl, own], lambda left, col: mul(left, q_t[at(col, cols, 16), :], 1, 1), side_core
        )
    for i in range(tiles):
        state_step(i)
        if alone:
            continue
        give_start(i)
        if i == 0:
            ff.advance(0)
            qkv.core_add(0)
        if i == 2:
            far_start(0)
        if i == 3:
            ff.advance(0)
            qkv.allow(2, "core")
            far_start(1)
    spread = jnp.sum(scale_sum[...], axis=1, keepdims=True)
    small_now[0, 4:5, 0:HEAD] = jnp.broadcast_to(spread, (HEAD, 128)).T[0:1, :]
    partners = ("core", "x") + tuple(range(bits))
    small_slots = [sems.slot() for _ in partners]

    def small_copy(number):
        return sems.remote(
            small_now.at[number], small_in.at[number], *ff.partner(partners[number]), small_slots[number]
        )

    def small_step(number):
        small_copy(number).wait()
        small_now[number + 1] = small_now[number] + small_in[number]
        if number + 1 < len(partners):
            small_copy(number + 1).start()

    if not alone:
        small_copy(0).start()
        far_start(2)
        ff.advance(0)
    weight_side(qkv, 1, lambda sl: wide[sl, :], lambda left, col: mul(left, k_t[at(col, cols, 16), :], 1, 1), 1 - core)
    if not alone:
        far_start(3)
        small_step(0)
    weight_side(qkv, 1, lambda sl: wide[sl, :], lambda left, col: mul(left, k_t[at(col, cols, 16), :], 1, 1), core)
    if not alone:
        ff.drain_other(0)
        ff.drain_acc(0)
        qkv.core_add(1)
        small_step(1)
    weight_side(qkv, 2, lambda sl: wide[sl, :], lambda left, col: mul(left, v_t[at(col, cols, 16), :], 1, 1), 1 - core)
    if not alone:
        far_start(4)
        qkv.advance(0)
        small_step(2)
    weight_side(qkv, 2, lambda sl: wide[sl, :], lambda left, col: mul(left, v_t[at(col, cols, 16), :], 1, 1), core)
    if alone:
        for part in range(3):
            weight_out(part, qkv_out, part * width)
    if alone:
        small_out[...] = small_now[0]
        tail = [local(grad_hidden, hidden_out, 12), local(flat, acted_out, 13)]
        for copy in tail:
            copy.start()
        loads["state"].wait()
        for copy in tail + copies_out[6:]:
            copy.wait()
        return

    qkv.core_add(2)
    small_step(3)
    for part, target in enumerate((out_out, up_out, down_out)):
        ff.advance(part)
        give_result(ff, part, target, 0)
        ff.drain_result(part)
    qkv.advance(0)
    for number in range(4, len(partners)):
        small_step(number)
    small_out[...] = small_now[len(partners)]
    qkv.advance(1)

    loads["state"].wait()
    for i in range(tiles):

        @pl.when(far_got)
        def _():
            far(i).wait_recv()


    def final_step(i, carry):
        sl = at(i * 128, 128, 128)
        state = state_low[sl, :].astype(F32)
        inverse = lax.rsqrt(jnp.mean(state * state, axis=-1, keepdims=True) + EPS)
        normed = state * inverse
        grad = flat[2, sl, :].astype(F32)
        grad += jnp.where(even, near_in[sl, :].astype(F32), 0.0)
        grad += jnp.where(far_got, far_in[sl, :].astype(F32), 0.0)
        weighted = grad * rows_in[0:1, :]
        along = jnp.mean(weighted * normed, axis=-1, keepdims=True)
        state_low[sl, :] = (grad_hidden[sl, :] + inverse * (weighted - normed * along)).astype(BF16)
        return carry

    lax.fori_loop(0, length // 128, final_step, 0)
    write = local(state_low, input_grad, 12)
    write.start()
    qkv.advance(0)
    qkv.advance(2)
    qkv.advance(1)
    qkv.advance(0)
    qkv.advance(2)
    qkv.advance(1)
    qkv.advance(2)
    qkv.advance(1)
    while min(qkv.at_stage) <= bits:
        for part in range(3):
            if qkv.at_stage[part] <= bits:
                qkv.advance(part)
    for part in range(3):
        qkv.advance(part)
    for part in range(3):
        qkv.advance(part)
        give_result(qkv, part, qkv_out, part * width)

    for i in range(tiles):

        @pl.when(odd | far_ok)
        def _():
            give(i).wait_send()

        @pl.when(far_ok)
        def _():
            far(i).wait_send()

    for part in range(3):
        qkv.drain_other(part)
        qkv.drain_acc(part)
        qkv.drain_result(part)
    write.wait()


FF_STEPS = (
    (0, 2, 0), (2, 1, 0), (6, 2, 1), (7, 1, 1), (9, 2, 2), (10, 0, 0),
    (11, 1, 2), (12, 2, 3), (13, 1, 3), (14, 0, 1), (15, 2, 4), (15, 1, 4),
)


def backward(count, alone, *inputs):
    length, width = inputs[0].shape
    total = 3 * length
    rows = width // count
    cols = width // 2
    heads = width // HEAD
    bits = count.bit_length() - 1
    shape = jax.ShapeDtypeStruct
    if alone:
        outs = (
            shape((length, width), F32),
            shape((width, 3 * width), BF16),
            shape((width, width), BF16),
            shape((width, width), BF16),
            shape((width, width), BF16),
            shape((3, length, width), BF16),
            shape((8, width), F32),
        )
        params = pltpu.CompilerParams(vmem_limit_bytes=VMEM_LIMIT)
    else:
        outs = (
            shape((length, width), BF16),
            shape((rows, 3 * width), F32),
            shape((rows, width), F32),
            shape((rows, width), F32),
            shape((rows, width), F32),
            shape((8, width), F32),
        )
        params = pltpu.CompilerParams(collective_id=1, has_side_effects=True, vmem_limit_bytes=VMEM_LIMIT)
    buffer = pltpu.VMEM
    return pl.pallas_call(
        functools.partial(backward_kernel, count, alone),
        name="backward_layer",
        out_shape=outs,
        in_specs=[ANY] * 16 + [VM] * 3,
        out_specs=(ANY,) * (len(outs) - 1) + (VM,),
        scratch_shapes=[
            buffer((width, total), BF16),
            buffer((3, length, width), BF16),
            buffer((2, TILE, 3 * width), BF16),
            buffer((length, width), F32),
            buffer((length, width), F32),
            buffer((width, length), BF16),
            buffer((width, total), BF16),
            buffer((width, total), BF16),
            buffer((width, length), BF16),
            buffer((heads, 1, length), F32),
            buffer((total, length), F32),
            buffer((HEAD, length), F32),
            buffer((3, width, cols), BF16),
            buffer((3, width, cols), BF16),
            buffer((3, width, cols), BF16),
            buffer((3, 2, rows, cols), BF16),
            buffer((3, 2, rows, cols), BF16),
            buffer((2, rows, cols), F32),
            buffer((length, width), BF16),
            buffer((length, width), BF16),
            buffer((length, width), BF16),
            buffer((bits + 3, 8, width), F32),
            buffer((bits + 2, 8, width), F32),
            pltpu.SemaphoreType.DMA((40,)),
            pltpu.SemaphoreType.DMA((192,)),
            pltpu.SemaphoreType.DMA((192,)),
            pltpu.SemaphoreType.REGULAR((2, 3 * (bits + 2))),
        ],
        compiler_params=params,
    )(*inputs)


def shifted(value, steps):
    count = lax.axis_size("shard")
    first, last = (max(0, -steps), min(count, count - steps))
    return lax.ppermute(value, "shard", [(source, source + steps) for source in range(first, last)])


def gather_plain(tokens, segs, vec, *weights):
    whole = tuple(lax.all_gather(weight, "shard", axis=0, tiled=True) for weight in weights)
    earlier = jnp.concatenate([shifted(tokens, 2), shifted(tokens, 1)])
    seg_ext = jnp.stack([shifted(segs, 2), shifted(segs, 1), segs])
    return (earlier, seg_ext, lax.all_gather(vec, "shard", axis=0)) + whole


def reduce_plain(qkv_grad, out_grad, up_grad, down_grad, grad_acted, small):
    owned = []
    for grad in (qkv_grad, out_grad, up_grad, down_grad):
        part = lax.psum_scatter(grad, "shard", scatter_dimension=0, tiled=True)
        owned.append(lax.psum(part, "rep").astype(F32))
    parts = [grad_acted[2], shifted(grad_acted[0], -2), shifted(grad_acted[1], -1)]
    return (*owned, sum(part.astype(F32) for part in parts), lax.psum(small, ("rep", "shard")))


def body(
    tokens,
    segments,
    cotangent,
    gain_one,
    qkv_weight,
    query_scale,
    out_weight,
    gain_two,
    up_weight,
    up_bias,
    down_weight,
    down_bias,
):
    count = lax.axis_size("shard")
    shard = lax.axis_index("shard")
    length, width = tokens.shape[1:]
    rows = qkv_weight.shape[0]
    heads = width // HEAD

    vec = jnp.stack([gain_one, gain_two, up_bias, down_bias])
    vec = jnp.pad(vec, ((0, 12), (0, -rows % 128)))
    segs = jnp.broadcast_to(segments, (8, length))
    whole_tiles = rows % 32 == 0 and count >= 4 and count & (count - 1) == 0 and lax.axis_size("rep") == 4
    factor = LOG2E / math.sqrt(HEAD) * jax.nn.softplus(query_scale)
    factor_row = jnp.tile(factor, heads)[None]
    weights = (qkv_weight, out_weight, up_weight, down_weight)
    earlier = None
    if not whole_tiles:
        earlier, segs, vec, *weights = gather_plain(tokens[0], segs, vec, *weights)
    output, acted_t, q_t, k_t, v_t, o_t, lse, hidden, inner_t, upper, lower_t, rows_in, qkv, out, up, down, mask = forward(
        count, tokens[0], earlier, segs, vec, factor_row * (1.0 / LN2), *weights
    )
    results = backward(
        count, not whole_tiles, cotangent[0], tokens[0], hidden, inner_t, upper, lower_t, o_t, q_t, k_t, v_t, acted_t,
        qkv, out, up, down, mask, lse, rows_in, factor[:, None],
    )
    if whole_tiles:
        input_grad, qkv_own, out_own, up_own, down_own, small_sum = results
    else:
        grad_hidden, *partial = results
        qkv_own, out_own, up_own, down_own, grad_acted, small_sum = reduce_plain(*partial)
        state = tokens[0].astype(F32)
        inverse = lax.rsqrt(jnp.mean(state * state, axis=-1, keepdims=True) + EPS)
        normed = state * inverse
        weighted = grad_acted * rows_in[0:1]
        along = jnp.mean(weighted * normed, axis=-1, keepdims=True)
        input_grad = (grad_hidden + inverse * (weighted - normed * along)).astype(BF16)

    mine = lax.dynamic_slice_in_dim(small_sum[:4], shard * rows, rows, 1)
    scale_grad = (
        small_sum[4, :HEAD]
        * LN2
        / factor
        * (LOG2E / math.sqrt(HEAD))
        * jax.nn.sigmoid(query_scale)
    )
    return (
        output[None],
        input_grad[None],
        mine[0],
        qkv_own,
        scale_grad,
        out_own,
        mine[1],
        up_own,
        mine[2],
        down_own,
        mine[3],
    )


def solution(mesh):
    return jax.shard_map(
        body,
        mesh=mesh,
        in_specs=(
            P("rep", "shard", None),
            P("rep", "shard"),
            P("rep", "shard", None),
            P("shard"),
            P("shard", None),
            P(),
            P("shard", None),
            P("shard"),
            P("shard", None),
            P("shard"),
            P("shard", None),
            P("shard"),
        ),
        out_specs=(
            P("rep", "shard", None),
            P("rep", "shard", None),
            P("shard"),
            P("shard", None),
            P(),
            P("shard", None),
            P("shard"),
            P("shard", None),
            P("shard"),
            P("shard", None),
            P("shard"),
        ),
        check_vma=False,
    )
```

```python
import functools
import math

import jax
import jax.numpy as jnp
from jax import lax
from jax.experimental import pallas as pl
from jax.experimental.pallas import tpu as pltpu
from jax.sharding import PartitionSpec as P

HEAD = 80
WINDOW = 1024
EPS = 1e-06
LOG2E = 1.442695041
LN2 = math.log(2.0)
MASKED = -1e30
TILE = 256
MESH = pl.DeviceIdType.MESH
F32 = jnp.float32
BF16 = jnp.bfloat16
VMEM_LIMIT = 62 * 2**20
ANY = pl.BlockSpec(memory_space=pl.ANY)
VM = pl.BlockSpec(memory_space=pltpu.VMEM)


def mul(a, b, left=1, right=0):
    return lax.dot_general(a, b, (((left,), (right,)), ((), ())), preferred_element_type=F32)


def at(start, size, unit):
    return pl.ds(pl.multiple_of(start, unit), size)


def bit_of(index, bit):
    return lax.rem(lax.div(index, 1 << bit), 2)


def flip(index, mask):
    out = index
    bit = 0
    while mask >> bit:
        if (mask >> bit) & 1:
            out = out + (1 - 2 * bit_of(index, bit)) * (1 << bit)
        bit += 1
    return out


def span(bits):
    masks = [0]
    for bit in bits:
        masks = masks + [mask | (1 << bit) for mask in masks]
    return masks


def stage_orders(bits):
    rest = list(range(2, bits))
    return (["x", 0, 1] + rest, [0, 1, "x"] + rest, [1, "x", 0] + rest)


def cross_orders(bits):
    rest = list(range(2, bits))
    return (["x", 0, 1] + rest, ["x", 1, 0] + rest, ["x", 0, 1] + rest)


def greet(count):
    rep, shard = lax.axis_index("rep"), lax.axis_index("shard")
    barrier = pltpu.get_barrier_semaphore()
    for step in range(1, count):
        other = lax.rem(shard + step, count)
        pl.semaphore_signal(barrier, inc=1, device_id={"rep": rep, "shard": other}, device_id_type=MESH)
    for mask in (1, 2):
        pl.semaphore_signal(barrier, inc=1, device_id={"rep": flip(rep, mask), "shard": shard}, device_id_type=MESH)
    pl.semaphore_wait(barrier, count + 1)


class Sems:
    def __init__(self, send, recv):
        self.send, self.recv, self.used = send, recv, 0

    def slot(self):
        self.used += 1
        return self.used - 1

    def remote(self, src, dst, rep, shard, slot=None):
        slot = self.slot() if slot is None else slot
        return pltpu.make_async_remote_copy(
            src_ref=src,
            dst_ref=dst,
            send_sem=self.send.at[slot],
            recv_sem=self.recv.at[slot],
            device_id={"rep": rep, "shard": shard},
            device_id_type=MESH,
        )


class Doubling:
    def __init__(self, sems, count, rows, orders, parts):
        self.sems, self.rows, self.half, self.parts = sems, rows, rows // 2, parts
        bits = count.bit_length() - 1
        self.stages = bits + 1
        self.plan = []
        for order in orders:
            have, whole, stages = [], False, []
            for what in order[::-1]:
                masks = span(have)[1:] if what == "x" else span(have)
                stages.append([(what, mask, whole, sems.slot(), sems.slot()) for mask in masks])
                if what == "x":
                    whole = True
                else:
                    have.append(what)
            self.plan.append(stages)

    def copy(self, part, step):
        what, mask, whole, slot, _ = step
        rep, shard = lax.axis_index("rep"), lax.axis_index("shard")
        core, cross = lax.rem(rep, 2), lax.div(rep, 2)
        src, dst, first, cols = self.parts[part]
        across = at(first + core * cols, cols, 128)
        shift, size = (0, self.rows) if whole else (cross * self.half, self.half)
        row = flip(shard, mask) * self.rows + shift
        to = dst.at[at(row, size, 16), across]
        here = src.at[at(shift, size, 16), across] if mask == 0 else to
        if what == "x":
            return self.sems.remote(here, to, flip(rep, 2), shard, slot)
        return self.sems.remote(here, to, rep, flip(shard, 1 << what), slot)

    def ahead(self, part, step):
        what, mask, whole, _, slot = step
        rep, shard = lax.axis_index("rep"), lax.axis_index("shard")
        core, cross = lax.rem(rep, 2), lax.div(rep, 2)
        _, dst, first, cols = self.parts[part]
        if what == "x":
            row, size = flip(shard, mask) * self.rows + (1 - cross) * self.half, self.half
        else:
            shift, size = (0, self.rows) if whole else (cross * self.half, self.half)
            row = flip(shard, mask | (1 << what)) * self.rows + shift
        spot = dst.at[at(row, size, 16), at(first + core * cols, cols, 128)]
        return self.sems.remote(spot, spot, flip(rep, 1), shard, slot)

    def send(self, stage):
        for part in range(3):
            for step in self.plan[part][stage]:
                self.copy(part, step).start()

    def settle(self, stage):
        for part in range(3):
            for step in self.plan[part][stage]:
                self.copy(part, step).wait_recv()
                self.ahead(part, step).start()

    def move(self, stage):
        for part in range(3):
            for step in self.plan[part][stage]:
                self.copy(part, step).wait_recv()
            for step in self.plan[part][stage + 1]:
                self.copy(part, step).start()
            for step in self.plan[part][stage]:
                self.ahead(part, step).start()

    def finish(self):
        for part in range(3):
            for stage in self.plan[part]:
                for step in stage:
                    self.ahead(part, step).wait_recv()

    def drain(self):
        for part in range(3):
            for stage in self.plan[part]:
                for step in stage:
                    self.copy(part, step).wait_send()
                    self.ahead(part, step).wait_send()


def tail_orders(bits):
    rest = list(range(2, bits))
    return (["x", 0, 1] + rest, ["x", 1, 0] + rest, [0, "x", 1] + rest)


def beside_orders(bits):
    rest = list(range(2, bits))
    return (["x", 0, 1] + rest, [0, 1, "x"] + rest, [1, 0, "x"] + rest)


class Gathered:
    stages = 1

    def send(self, stage):
        pass

    settle = move = send

    def finish(self):
        pass

    drain = finish


def forward_kernel(count, *refs):
    (tokens, earlier, segs, vec, factor, w_qkv, w_out, w_up, w_down) = refs[:9]
    results = refs[9:26]
    alone = earlier is not None
    (
        output_hbm, acted_t_hbm, q_t_hbm, k_t_hbm, v_t_hbm, o_t_hbm, lse, hidden_hbm,
        inner_t_hbm, upper_hbm, lower_t_hbm, rows_out, qkv_hbm, out_hbm, up_hbm, down_hbm, mask_hbm,
    ) = results
    (
        seg_ext, vec_full, qkv, out, up, down, acted, acted_t, q_t, k_t, v_t, o_t, heads, inner,
        hidden, upper, inner_t, lower_t, mask, state_low, send, recv, lsem,
    ) = refs[26:]
    rep, shard = lax.axis_index("rep"), lax.axis_index("shard")
    length, width = tokens.shape
    total = 3 * length
    rows = w_qkv.shape[0]
    tiles = width // TILE
    own = pl.ds(total - length, length)
    sems = Sems(send, recv)
    lower, output = heads, inner
    bits = count.bit_length() - 1

    first_cols = (tiles * 2 // 5) * TILE
    rest_cols = width - first_cols
    groups = (Gathered(),) * 3 if alone else (
        Doubling(sems, count, rows, cross_orders(bits), [(w_qkv, qkv, p * width, first_cols // 2) for p in range(3)]),
        Doubling(sems, count, rows, stage_orders(bits), [(w_qkv, qkv, p * width + first_cols, rest_cols // 2) for p in range(3)]),
        Doubling(sems, count, rows, stage_orders(bits), [(w, full, 0, width // 2) for w, full in ((w_out, out), (w_up, up), (w_down, down))]),
    )

    pairs = [(tokens, acted.at[own]), (tokens, state_low)]
    if alone:
        pairs += [(earlier, acted.at[pl.ds(0, 2 * length)]), (segs, seg_ext), (vec, vec_full)]
        pairs += [(w_qkv, qkv), (w_out, out), (w_up, up), (w_down, down)]
    else:
        mine = at(shard * rows, rows, 16)
        pairs += [(segs, seg_ext.at[2]), (vec, vec_full.at[shard])]
        pairs += [(w_qkv, qkv.at[mine]), (w_out, out.at[mine]), (w_up, up.at[mine]), (w_down, down.at[mine])]
    loads = [pltpu.make_async_copy(src, dst, lsem.at[i]) for i, (src, dst) in enumerate(pairs)]
    for copy in loads:
        copy.start()

    odd = lax.rem(shard, 2) == 1
    even = jnp.logical_not(odd)
    far_ok, far_got = shard < count - 2, shard >= 2
    buddy = flip(shard, 1)
    far_to = lax.rem(shard + 2, count)
    nchunk = 8
    part = length // nchunk
    far, near, relay, vecs = [], [], [], []
    for i in range(0 if alone else nchunk):
        here = pl.ds(i * part, part)
        far_spot, near_spot = acted.at[pl.ds(i * part, part)], acted.at[pl.ds(length + i * part, part)]
        slot = sems.slot()
        far.append(sems.remote(tokens.at[here], far_spot, rep, far_to, sems.slot()))
        near.append(sems.remote(tokens.at[here], near_spot, rep, buddy, slot))
        relay.append(sems.remote(far_spot, near_spot, rep, buddy, slot))
    if not alone:
        slot = sems.slot()
        far.append(sems.remote(segs, seg_ext.at[0], rep, far_to, sems.slot()))
        near.append(sems.remote(segs, seg_ext.at[1], rep, buddy, slot))
        relay.append(sems.remote(seg_ext.at[0], seg_ext.at[1], rep, buddy, slot))
        vecs = [
            sems.remote(vec, vec_full.at[shard], rep, lax.rem(shard + step, count), sems.slot()) for step in range(1, count)
        ]

    def far_start(*which):
        @pl.when(far_ok)
        def _():
            for i in which:
                far[i].start()

    def near_start(*which):
        @pl.when(even)
        def _():
            for i in which:
                near[i].start()

    def far_next(i):
        @pl.when(far_ok)
        def _():
            far[i].wait_send()
            far[i + 2].start()

    def near_next(i):
        @pl.when(even)
        def _():
            near[i].wait_send()
            near[i + 2].start()

    def relay_start(*which):
        @pl.when(far_got)
        def _():
            for i in which:
                far[i].wait_recv()

        @pl.when(odd & far_got)
        def _():
            for i in which:
                relay[i].start()

    if not alone:
        greet(count)
        groups[0].send(0)
        far_start(nchunk, 0, 1)
        near_start(nchunk, 0, 1)
        for copy in vecs:
            copy.start()
        groups[0].move(0)
        relay_start(nchunk)
        for i in range(nchunk):
            relay_start(i)
            if i + 2 < nchunk:
                far_next(i)
                near_next(i)
            if i == 0:
                groups[0].move(1)
            if i == 2:
                groups[0].move(2)
            if i == 6:
                groups[1].send(0)

    for copy in loads:
        copy.wait()
    for copy in vecs:
        copy.wait_recv()
    each = width // count
    vectors = jnp.concatenate([vec_full[i][:, :each].astype(F32) for i in range(count)], axis=1)
    rows_out[...] = vectors[:8, :]
    gain_one, gain_two = rows_out[0:1, :], rows_out[1:2, :]

    def norm_rows(i):
        sl = at(i * TILE, TILE, TILE)
        state = acted[sl, :].astype(F32)
        scale = lax.rsqrt(jnp.mean(state * state, axis=-1, keepdims=True) + EPS)
        value = (state * scale * rows_out[0:1, :]).astype(BF16)
        value = jnp.where(shard + i * TILE // length >= 2, value, jnp.zeros_like(value))
        acted[sl, :] = value
        acted_t[:, sl] = value.T

    def norm_step(i, carry):
        norm_rows(i)
        return carry

    per = length // TILE
    lax.fori_loop(2 * per, 3 * per, norm_step, 0)

    groups[0].settle(groups[0].stages - 1)
    groups[0].finish()

    def project_own(i, carry):
        sl = at(i * TILE, TILE, TILE)
        q_t[sl, :] = (mul(acted[own, :], qkv[:, sl]) * factor[:, sl]).astype(BF16).T
        k_t[sl, own] = mul(acted[own, :], qkv[:, at(width + i * TILE, TILE, TILE)]).astype(BF16).T
        v_t[sl, own] = mul(acted[own, :], qkv[:, at(2 * width + i * TILE, TILE, TILE)]).astype(BF16).T
        return carry

    def project_earlier(i, carry):
        sl = at(i * TILE, TILE, TILE)
        k_t[sl, before] = mul(acted[before, :], qkv[:, at(width + i * TILE, TILE, TILE)]).astype(BF16).T
        v_t[sl, before] = mul(acted[before, :], qkv[:, at(2 * width + i * TILE, TILE, TILE)]).astype(BF16).T
        return carry

    def project(i, carry):
        sl = at(i * TILE, TILE, TILE)
        q_t[sl, :] = (mul(acted[own, :], qkv[:, sl]) * factor[:, sl]).astype(BF16).T
        k_t[sl, :] = mul(acted[...], qkv[:, at(width + i * TILE, TILE, TILE)]).astype(BF16).T
        v_t[sl, :] = mul(acted[...], qkv[:, at(2 * width + i * TILE, TILE, TILE)]).astype(BF16).T
        return carry

    before = pl.ds(0, total - length)
    lax.fori_loop(0, first_cols // TILE, project_own, 0)
    if not alone:

        @pl.when(odd)
        def _():
            for copy in near:
                copy.wait_recv()

        @pl.when(even & far_got)
        def _():
            for copy in relay:
                copy.wait_recv()

        @pl.when(odd & far_got)
        def _():
            for copy in relay:
                copy.wait_send()

    groups[1].move(0)
    groups[2].send(0)
    lax.fori_loop(0, 2 * per, norm_step, 0)

    mine = seg_ext[2].astype(F32)[0:1, :]
    for j in range(3):
        column = jnp.where(shard + j >= 2, seg_ext[j].astype(F32).T[:, 0:1], -1.0)
        place = lax.broadcasted_iota(jnp.int32, (length, length), 0) + j * length
        lane = lax.broadcasted_iota(jnp.int32, (length, length), 1)
        near_by = (place > lane) & (place <= lane + WINDOW)
        mask[j * length : (j + 1) * length, :] = jnp.where(near_by & (column == mine), 0.0, MASKED)

    groups[1].move(1)
    lax.fori_loop(0, first_cols // TILE, project_earlier, 0)
    groups[1].move(2)

    half = length // 2

    def attend(h):
        sl = at(h * HEAD, HEAD, 16)
        key, query = k_t[sl, :].T, q_t[sl, :]
        first, last = pl.ds(0, half), pl.ds(total - half, half)
        middle = pl.ds(half, total - length)
        score_m = mul(key[half : total - half], query) + mask[middle, :]
        score_f = mul(key[:half], query[:, :half]) + mask[first, :half]
        score_l = mul(key[total - half :], query[:, half:]) + mask[last, half:]
        ends = [jnp.max(score, axis=0, keepdims=True) for score in (score_f, score_l)]
        top = jnp.maximum(jnp.max(score_m, axis=0, keepdims=True), jnp.concatenate(ends, axis=1))
        prob_m = jnp.exp2(score_m - top)
        prob_f = jnp.exp2(score_f - top[:, :half])
        prob_l = jnp.exp2(score_l - top[:, half:])
        ends = [jnp.sum(prob, axis=0, keepdims=True) for prob in (prob_f, prob_l)]
        norm = jnp.sum(prob_m, axis=0, keepdims=True) + jnp.concatenate(ends, axis=1)
        ends = [mul(v_t[sl, first], prob_f.astype(BF16)), mul(v_t[sl, last], prob_l.astype(BF16))]
        mixed = mul(v_t[sl, middle], prob_m.astype(BF16)) + jnp.concatenate(ends, axis=1)
        o_t[sl, :] = (mixed * (1.0 / norm)).astype(BF16)
        lse[h] = top + jnp.log2(norm)

    ready = first_cols // HEAD // 2 * 2
    count_heads = width // HEAD

    def attend_first(pair, carry):
        attend(2 * pair)
        attend(2 * pair + 1)

        @pl.when(pair == ready // 2 - 1)
        def _():
            groups[1].settle(groups[1].stages - 1)
            groups[2].move(0)

        return carry

    lax.fori_loop(0, ready // 2, attend_first, 0)
    groups[1].finish()

    def project_rest(i, carry):
        project(i, carry)

        @pl.when(i == tiles - 2)
        def _():
            groups[2].move(1)

        return carry

    lax.fori_loop(first_cols // TILE, tiles, project_rest, 0)
    keep = [
        pltpu.make_async_copy(src, dst, lsem.at[8 + i])
        for i, (src, dst) in enumerate(((qkv, qkv_hbm), (acted_t, acted_t_hbm), (q_t, q_t_hbm), (k_t, k_t_hbm), (v_t, v_t_hbm), (mask, mask_hbm)))
    ]
    for copy in keep:
        copy.start()

    def attend_rest(pair, carry):
        attend(2 * pair)
        attend(2 * pair + 1)

        @pl.when(pair == ready // 2 + 1)
        def _():
            groups[2].move(2)

        return carry

    lax.fori_loop(ready // 2, count_heads // 2, attend_rest, 0)

    def keep_more(*pairs):
        for src, dst in pairs:
            copy = pltpu.make_async_copy(src, dst, lsem.at[8 + len(keep)])
            copy.start()
            keep.append(copy)

    keep_more((o_t, o_t_hbm))

    def turn(i, carry):
        sl = at(i * TILE, TILE, TILE)
        heads[:, sl] = o_t[sl, :].T
        return carry

    lax.fori_loop(0, tiles, turn, 0)
    groups[2].settle(groups[2].stages - 1)
    groups[2].finish()
    keep_more((out, out_hbm), (up, up_hbm), (down, down_hbm))

    def out_step(i, carry):
        sl = at(i * TILE, TILE, TILE)
        hidden[:, sl] = state_low[:, sl].astype(F32) + mul(heads[...], out[:, sl])
        return carry

    lax.fori_loop(0, tiles, out_step, 0)
    keep_more((hidden, hidden_hbm))

    def norm_two(i, carry):
        sl = at(i * TILE, TILE, TILE)
        value = hidden[sl, :]
        scale = lax.rsqrt(jnp.mean(value * value, axis=-1, keepdims=True) + EPS)
        normed = (value * scale * rows_out[1:2, :]).astype(BF16)
        inner[sl, :] = normed
        inner_t[:, sl] = normed.T
        return carry

    lax.fori_loop(0, length // TILE, norm_two, 0)
    keep_more((inner_t, inner_t_hbm))

    def up_step(i, carry):
        sl = at(i * TILE, TILE, TILE)
        value = mul(inner[...], up[:, sl]) + rows_out[2:3, sl]
        upper[:, sl] = value
        act = (value / (1.0 + jnp.exp(-value))).astype(BF16)
        lower[:, sl] = act
        lower_t[sl, :] = act.T
        return carry

    lax.fori_loop(0, tiles, up_step, 0)
    keep_more((upper, upper_hbm), (lower_t, lower_t_hbm))

    def down_step(i, carry):
        sl = at(i * TILE, TILE, TILE)
        output[:, sl] = (hidden[:, sl] + (mul(lower[...], down[:, sl]) + rows_out[3:4, sl])).astype(BF16)
        return carry

    lax.fori_loop(0, tiles, down_step, 0)
    keep_more((output, output_hbm))

    if not alone:

        @pl.when(far_ok)
        def _():
            for copy in far[nchunk - 2 :]:
                copy.wait_send()

        @pl.when(even)
        def _():
            for copy in near[nchunk - 2 :]:
                copy.wait_send()

    for copy in vecs:
        copy.wait_send()
    for group in groups:
        group.drain()
    for copy in keep:
        copy.wait()


def forward(count, tokens, earlier, segs, vec, factor, w_qkv, w_out, w_up, w_down):
    length, width = tokens.shape
    total = 3 * length
    heads = width // HEAD
    inputs = [x for x in (tokens, earlier, segs, vec, factor, w_qkv, w_out, w_up, w_down) if x is not None]
    if earlier is None:
        params = pltpu.CompilerParams(collective_id=0, has_side_effects=True, vmem_limit_bytes=VMEM_LIMIT)
    else:
        params = pltpu.CompilerParams(vmem_limit_bytes=VMEM_LIMIT)
    shape = jax.ShapeDtypeStruct
    outs = (
        shape((length, width), BF16),
        shape((width, total), BF16),
        shape((width, length), BF16),
        shape((width, total), BF16),
        shape((width, total), BF16),
        shape((width, length), BF16),
        shape((heads, 1, length), F32),
        shape((length, width), F32),
        shape((width, length), BF16),
        shape((length, width), F32),
        shape((width, length), BF16),
        shape((8, width), F32),
        shape((width, 3 * width), BF16),
        shape((width, width), BF16),
        shape((width, width), BF16),
        shape((width, width), BF16),
        shape((total, length), F32),
    )
    specs = [ANY] * 17
    specs[6] = specs[11] = VM
    buffer = pltpu.VMEM
    return pl.pallas_call(
        functools.partial(forward_kernel, count) if earlier is not None else lambda *refs: forward_kernel(count, refs[0], None, *refs[1:]),
        name="forward_layer",
        out_shape=outs,
        in_specs=[ANY] * (len(inputs) - 5) + [VM] + [ANY] * 4,
        out_specs=tuple(specs),
        scratch_shapes=[
            buffer((3,) + segs.shape[-2:], jnp.int32),
            buffer((count,) + vec.shape[-2:], BF16),
            buffer((width, 3 * width), BF16),
            buffer((width, width), BF16),
            buffer((width, width), BF16),
            buffer((width, width), BF16),
            buffer((total, width), BF16),
            buffer((width, total), BF16),
            buffer((width, length), BF16),
            buffer((width, total), BF16),
            buffer((width, total), BF16),
            buffer((width, length), BF16),
            buffer((length, width), BF16),
            buffer((length, width), BF16),
            buffer((length, width), F32),
            buffer((length, width), F32),
            buffer((width, length), BF16),
            buffer((width, length), BF16),
            buffer((total, length), F32),
            buffer((length, width), BF16),
            pltpu.SemaphoreType.DMA((256,)),
            pltpu.SemaphoreType.DMA((256,)),
            pltpu.SemaphoreType.DMA((32,)),
        ],
        compiler_params=params,
    )(*inputs)


class Halving:
    def __init__(self, sems, credits, count, rows, orders, acc, other, land, result, reused):
        self.sems, self.credits, self.rows, self.half, self.reused = sems, credits, rows, rows // 2, reused
        self.acc, self.other, self.land, self.result = acc, other, land, result
        self.bits = count.bit_length() - 1
        self.plan, self.core_slot, self.cross_slot, self.share_slot = [], [], [], []
        self.at_stage = [0] * 3
        for order in orders:
            left, whole, base, stages = list(range(self.bits)), True, 0, []
            for what in order:
                steps = []
                if what == "x":
                    whole = False
                else:
                    left.remove(what)
                for mask in span(left):
                    size = rows if whole else self.half
                    steps.append((mask, base, size, sems.slot()))
                    base += size
                stages.append((what, whole, steps))
            self.plan.append(stages)
            self.core_slot.append(sems.slot())
            self.cross_slot.append(sems.slot())
            self.share_slot.append(sems.slot())

    def partner(self, what):
        rep, shard = lax.axis_index("rep"), lax.axis_index("shard")
        if what == "core":
            return flip(rep, 1), shard
        if what == "x":
            return flip(rep, 2), shard
        return rep, flip(shard, 1 << what)

    def credit(self, part, what):
        place = 0 if what == "core" else 1 if what == "x" else 2 + what
        return self.credits.at[part * (self.bits + 2) + place]

    def allow(self, part, what):
        rep, shard = self.partner(what)
        pl.semaphore_signal(
            self.credit(part, what), inc=1, device_id={"rep": rep, "shard": shard}, device_id_type=MESH
        )

    def core_copy(self, part):
        return self.sems.remote(self.other[part], self.land[part], *self.partner("core"), self.core_slot[part])

    def core_send(self, part):
        if self.reused:
            pl.semaphore_wait(self.credit(part, "core"), 1)
        self.core_copy(part).start()

    def core_add(self, part):
        self.core_copy(part).wait_recv()
        acc, land = self.acc[part], self.land[part]

        def step(i, carry):
            sl = at(i * TILE, TILE, TILE)
            acc[sl, :] = (acc[sl, :].astype(F32) + land[sl, :].astype(F32)).astype(BF16)
            return carry

        lax.fori_loop(0, acc.shape[0] // TILE, step, 0)
        for what, _, _ in self.plan[part]:
            self.allow(part, what)
        self.send(part, 0)

    def copy(self, part, stage, step):
        what, whole, _ = self.plan[part][stage]
        mask, base, size, slot = step
        shard, cross = lax.axis_index("shard"), lax.div(lax.axis_index("rep"), 2)
        if what == "x":
            row = flip(shard, mask) * self.rows + (1 - cross) * self.half
        else:
            row = flip(shard, mask | (1 << what)) * self.rows
            row = row if whole else row + cross * self.half
        src = self.acc[part].at[at(row, size, 16)]
        return self.sems.remote(src, self.land[part].at[pl.ds(base, size)], *self.partner(what), slot)

    def send(self, part, stage):
        what, _, steps = self.plan[part][stage]
        pl.semaphore_wait(self.credit(part, what), 1)
        for step in steps:
            self.copy(part, stage, step).start()

    def receive(self, part, stage):
        what, whole, steps = self.plan[part][stage]
        shard, cross = lax.axis_index("shard"), lax.div(lax.axis_index("rep"), 2)
        for step in steps:
            mask, base, size, _ = step
            self.copy(part, stage, step).wait_recv()
            row = flip(shard, mask) * self.rows
            row = row if whole else row + cross * self.half
            sl = at(row, size, 16)
            new = self.acc[part][sl, :].astype(F32) + self.land[part][pl.ds(base, size), :].astype(F32)
            self.acc[part][sl, :] = new.astype(BF16)

    def advance(self, part):
        stage = self.at_stage[part]
        self.at_stage[part] += 1
        if stage <= self.bits:
            self.receive(part, stage)
        if stage < self.bits:
            self.send(part, stage + 1)
        elif stage == self.bits:
            core, cross = self.sides()
            shard = lax.axis_index("shard")
            row = shard * self.rows + cross * self.half
            self.result[part].at[core][at(cross * self.half, self.half, 16), :] = self.acc[part][at(row, self.half, 16), :]
            self.cross_copy(part).start()
        elif stage == self.bits + 1:
            self.cross_copy(part).wait_recv()
            self.share_copy(part).start()
        else:
            self.share_copy(part).wait_recv()

    def sides(self):
        rep = lax.axis_index("rep")
        return lax.rem(rep, 2), lax.div(rep, 2)

    def cross_copy(self, part):
        core, cross = self.sides()
        spot = self.result[part].at[core, at(cross * self.half, self.half, 16)]
        return self.sems.remote(spot, spot, *self.partner("x"), self.cross_slot[part])

    def share_copy(self, part):
        core, _ = self.sides()
        spot = self.result[part].at[core]
        return self.sems.remote(spot, spot, *self.partner("core"), self.share_slot[part])

    def drain_other(self, part):
        self.core_copy(part).wait_send()

    def drain_acc(self, part):
        for stage in range(self.bits + 1):
            for step in self.plan[part][stage][2]:
                self.copy(part, stage, step).wait_send()

    def drain_result(self, part):
        self.cross_copy(part).wait_send()
        self.share_copy(part).wait_send()


def backward_kernel(count, alone, *refs):
    (
        cot_hbm, tokens_hbm, hidden_hbm, inner_t_hbm, upper_hbm, lower_t_hbm, o_t_hbm, q_t_hbm, k_t_hbm, v_t_hbm,
        acted_t_hbm, qkv_hbm, out_hbm, up_hbm, down_hbm, mask_hbm, lse, rows_in, factor,
    ) = refs[:19]
    if alone:
        (hidden_out, qkv_out, out_out, up_out, down_out, acted_out, small_out) = refs[19:26]
    else:
        (input_grad, qkv_out, out_out, up_out, down_out, small_out) = refs[19:25]
    scratch = refs[26:] if alone else refs[25:]
    (
        wide, flat, wtile, first_f32, grad_hidden, q_t, k_t, v_t, do_t, delta, mask, scale_sum, acc, other, land,
        result_ff, result_qkv, turned, near_in, far_in, state_low, small_now, small_in, lsem, send, recv, credits,
    ) = scratch
    rep, shard = lax.axis_index("rep"), lax.axis_index("shard")
    core = lax.rem(rep, 2)
    length, width = cot_hbm.shape
    total = 3 * length
    tiles = width // TILE
    rows = width // count
    cols = width // 2
    heads = width // HEAD
    own = pl.ds(total - length, length)
    bits = count.bit_length() - 1
    sems = Sems(send, recv)
    lower_t, inner_t, o_t = (wide.at[:, pl.ds(i * length, length)] for i in range(3))
    cot, grad_upper, grad_attn = (flat.at[i] for i in range(3))
    parts = [[ref.at[i] for i in range(3)] for ref in (acc, other, land, result_ff, result_qkv)]

    def local(src, dst, slot):
        return pltpu.make_async_copy(src, dst, lsem.at[slot])

    loads = {
        "cot": local(cot_hbm, cot, 0),
        "lower": local(lower_t_hbm, lower_t, 1),
        "upper": local(upper_hbm, first_f32, 2),
        "inner": local(inner_t_hbm, inner_t, 3),
        "o": local(o_t_hbm, o_t, 4),
        "q": local(q_t_hbm, q_t, 5),
        "k": local(k_t_hbm, k_t, 6),
        "v": local(v_t_hbm, v_t, 7),
        "mask": local(mask_hbm, mask, 8),
        "state": local(tokens_hbm, state_low, 9),
    }
    load_hidden = local(hidden_hbm, first_f32, 10)
    load_acted = local(acted_t_hbm, wide, 11)

    def tile_copy(src, order, i):
        slot = lax.rem(order * tiles + i, 6)
        return local(src.at[at(i * TILE, TILE, TILE)], wtile.at[slot], 12 + slot)

    def wide_copies(i):
        first = 3 * (i % 2)
        return [
            local(qkv_hbm.at[pl.ds(i * TILE, TILE), pl.ds(k * width, width)], wtile.at[first + k], 12 + first + k)
            for k in range(3)
        ]

    def tile_next(src, after, order, i):
        tile_copy(src, order, i).wait()
        if after is not None:
            tile_copy(after, order + 1, i).start()
        return lax.rem(order * tiles + i, 6)

    for name in ("lower", "cot"):
        loads[name].start()
    loads["upper"].start()
    for i in range(tiles):
        tile_copy(down_hbm, 0, i).start()
    for name in ("inner", "o"):
        loads[name].start()
    if alone:
        ff = qkv = None
    else:
        greet(count)
        ff = Halving(sems, credits.at[0], count, rows, beside_orders(bits), *parts[:4], False)
        back = [refs[::-1] for refs in parts[:3]]
        qkv = Halving(sems, credits.at[1], count, rows, tail_orders(bits), *back, parts[4], True)
    copies_out = []

    def weight_side(group, part, left, right, side_core, first_use=False):
        theirs = side_core is not core
        dest = (other if theirs else acc).at[part if first_use else 2 - part]

        def step(i, carry):
            sl = at(i * cols, cols, 16)
            dest[sl, :] = right(left(sl), side_core * cols).astype(BF16)
            return carry

        lax.fori_loop(0, 2, step, 0)
        if theirs and group is not None:
            group.core_send(part)

    def weight_out(part, target, first, first_use=False):
        for ref, side_core in ((other, 1 - core), (acc, core)):
            copy = local(ref.at[part if first_use else 2 - part], target.at[:, at(first + side_core * cols, cols, 128)], 20 + len(copies_out))
            copy.start()
            copies_out.append(copy)

    def weight_grad(group, part, left, right, target):
        weight_side(group, part, left, right, 1 - core, True)
        weight_side(group, part, left, right, core, True)
        if alone:
            weight_out(part, target, 0, True)

    small_now[0] = jnp.zeros_like(small_now[0])
    loads["lower"].wait()
    loads["cot"].wait()
    weight_grad(
        ff, 2, lambda sl: lower_t[sl, :], lambda left, col: mul(left, cot[:, at(col, cols, 128)]), down_out
    )
    loads["upper"].wait()

    def down_step(i, carry):
        sl = at(i * TILE, TILE, TILE)
        slot = tile_next(down_hbm, up_hbm, 0, i)
        grad_lower = mul(cot[...], wtile[slot], 1, 1)
        value = first_f32[:, sl]
        gate = 1.0 / (1.0 + jnp.exp(-value))
        grad = (grad_lower * (gate + value * gate * (1.0 - gate))).astype(BF16)
        grad_upper[:, sl] = grad
        small_now[0, 2:3, sl] = jnp.sum(grad.astype(F32), axis=0, keepdims=True)
        small_now[0, 3:4, sl] = jnp.sum(cot[:, sl].astype(F32), axis=0, keepdims=True)
        return carry

    lax.fori_loop(0, tiles, down_step, 0)
    load_hidden.start()
    for name in ("q", "k", "v", "mask", "state"):
        loads[name].start()
    loads["inner"].wait()
    weight_grad(
        ff, 1, lambda sl: inner_t[sl, :], lambda left, col: mul(left, grad_upper[:, at(col, cols, 128)]), up_out
    )
    if not alone:
        ff.core_add(2)

    def up_step(i, carry):
        sl = at(i * TILE, TILE, TILE)
        slot = tile_next(up_hbm, out_hbm, 1, i)
        grad_hidden[:, sl] = mul(grad_upper[...], wtile[slot], 1, 1)
        return carry

    lax.fori_loop(0, tiles, up_step, 0)
    load_hidden.wait()
    if not alone:
        ff.core_add(1)

    def norm_step(i, carry):
        sl = at(i * TILE, TILE, TILE)
        value = first_f32[sl, :]
        scale = lax.rsqrt(jnp.mean(value * value, axis=-1, keepdims=True) + EPS)
        normed = value * scale
        grad = grad_hidden[sl, :]
        small_now[0, 1:2, :] += jnp.sum(grad * normed, axis=0, keepdims=True)
        weighted = grad * rows_in[1:2, :]
        along = jnp.mean(weighted * normed, axis=-1, keepdims=True)
        whole = cot[sl, :].astype(F32) + scale * (weighted - normed * along)
        grad_hidden[sl, :] = whole
        grad_attn[sl, :] = whole.astype(BF16)
        return carry

    lax.fori_loop(0, length // TILE, norm_step, 0)
    loads["o"].wait()
    weight_grad(
        ff, 0, lambda sl: o_t[sl, :], lambda left, col: mul(left, grad_attn[:, at(col, cols, 128)]), out_out
    )

    def out_step(i, carry):
        sl = at(i * TILE, TILE, TILE)
        slot = tile_next(out_hbm, None, 2, i)
        do_t[sl, :] = mul(grad_attn[...], wtile[slot], 1, 1).astype(BF16).T
        return carry

    lax.fori_loop(0, tiles, out_step, 0)
    if not alone:
        ff.core_add(0)

    def delta_step(h, carry):
        sl = at(h * HEAD, HEAD, 16)
        delta[h] = jnp.sum(o_t[sl, :].astype(F32) * do_t[sl, :].astype(F32), axis=0, keepdims=True)
        return carry

    lax.fori_loop(0, heads, delta_step, 0)
    load_acted.start()
    for i in range(2):
        for copy in wide_copies(i):
            copy.start()
    for name in ("q", "k", "v", "mask"):
        loads[name].wait()
    scale_sum[...] = jnp.zeros_like(scale_sum)
    half = length // 2
    pieces = (
        (0, half, (0,)),
        (half, length, (0, 1)),
        (half + length, length, (0, 1)),
        (total - half, half, (1,)),
    )

    def attend(h, carry):
        sl = at(h * HEAD, HEAD, 16)
        query, grad = q_t[sl, :], do_t[sl, :]
        parts_dq = [jnp.zeros((HEAD, half), F32)] * 2
        for first, size, sides in pieces:
            ks, qs = pl.ds(first, size), slice(sides[0] * half, (sides[-1] + 1) * half)
            key, value = k_t[sl, ks], v_t[sl, ks]
            query_part, grad_part = query[:, qs], grad[:, qs]
            probs = jnp.exp2(mul(key.T, query_part) + mask[ks, qs] - lse[h][:, qs])
            scores = (probs * (mul(value.T, grad_part) - delta[h][:, qs])).astype(BF16)
            v_t[sl, ks] = mul(grad_part, probs.astype(BF16), 1, 1).astype(BF16)
            k_t[sl, ks] = (mul(query_part, scores, 1, 1) * LN2).astype(BF16)
            term = mul(key, scores)
            for place, side in enumerate(sides):
                parts_dq[side] = parts_dq[side] + term[:, place * half : (place + 1) * half]
        dq = jnp.concatenate(parts_dq, axis=1)
        scale_sum[...] += dq * query.astype(F32)
        q_t[sl, :] = (dq * factor[...]).astype(BF16)
        if not alone:
            for head in sorted({step[0] for step in FF_STEPS}):

                @pl.when(h == head)
                def _():
                    for _, part, stage in [step for step in FF_STEPS if step[0] == head]:
                        ff.at_stage[part] = stage
                        ff.advance(part)
                        if stage == bits:
                            qkv.allow(2 - part, "core")

        return carry

    lax.fori_loop(0, heads, attend, 0)

    def give_result(group, part, target, first):
        for side in range(2):
            src = (result_ff if group is ff else result_qkv).at[part, side]
            copy = local(src, target.at[:, pl.ds(first + side * cols, cols)], 20 + len(copies_out))
            copy.start()
            copies_out.append(copy)

    load_acted.wait()
    odd = lax.rem(shard, 2) == 1
    even = jnp.logical_not(odd)
    far_ok, far_got = shard >= 2, shard < count - 2
    buddy = flip(shard, 1)
    far_to = lax.rem(shard + count - 2, count)
    give_slots = [sems.slot() for _ in range(tiles)]
    far_slots = [sems.slot() for _ in range(tiles)]

    def give(i):
        sl = pl.ds(i * TILE, TILE)
        return sems.remote(flat.at[1, :, sl], near_in.at[:, sl], rep, buddy, give_slots[i])

    def far(i):
        sl = pl.ds(i * TILE, TILE)
        return sems.remote(flat.at[0, :, sl], far_in.at[:, sl], rep, far_to, far_slots[i])

    def state_step(i):
        sl = pl.ds(i * TILE, TILE)
        for copy in wide_copies(i):
            copy.wait()
        slot = 3 * (i % 2)
        both = mul(wtile[slot + 1], k_t[...]) + mul(wtile[slot + 2], v_t[...])
        mine = both[:, total - length :] + mul(wtile[slot], q_t[...])
        both = jnp.concatenate([both[:, : total - length], mine], axis=1)
        low = both.astype(BF16)
        sums = jnp.sum(both * wide[sl, :].astype(F32), axis=1, keepdims=True)
        small_now[0, 0:1, sl] = jnp.broadcast_to(sums, (TILE, 128)).T[0:1, :] / rows_in[0:1, sl]
        for j in range(3):
            flat[j, :, sl] = low[:, j * length : (j + 1) * length].T
        if i + 2 < tiles:
            for copy in wide_copies(i + 2):
                copy.start()

    def give_start(i):
        @pl.when(odd | far_ok)
        def _():
            give(i).start()

    def far_start(i):
        @pl.when(even | far_ok)
        def _():
            give(i).wait_recv()

        @pl.when(odd & far_ok)
        def _():
            sl = pl.ds(i * TILE, TILE)
            flat[0, :, sl] = (flat[0, :, sl].astype(F32) + near_in[:, sl].astype(F32)).astype(BF16)

        @pl.when(far_ok)
        def _():
            far(i).start()

    if alone:
        for copy in copies_out:
            copy.wait()
    else:
        ff.at_stage = [max([step[2] + 1 for step in FF_STEPS if step[1] == part]) for part in range(3)]
        for part in (1, 2):
            ff.drain_other(part)
            ff.drain_acc(part)
    for side_core in (1 - core, core):
        weight_side(
            qkv, 0, lambda sl: wide[sl, own], lambda left, col: mul(left, q_t[at(col, cols, 16), :], 1, 1), side_core
        )
    for i in range(tiles):
        state_step(i)
        if alone:
            continue
        give_start(i)
        if i == 0:
            qkv.core_add(0)
            ff.advance(0)
        if i == 4:
            far_start(0)
    spread = jnp.sum(scale_sum[...], axis=1, keepdims=True)
    small_now[0, 4:5, 0:HEAD] = jnp.broadcast_to(spread, (HEAD, 128)).T[0:1, :]
    partners = ("core", "x") + tuple(range(bits))
    small_slots = [sems.slot() for _ in partners]

    def small_copy(number):
        return sems.remote(
            small_now.at[number], small_in.at[number], *ff.partner(partners[number]), small_slots[number]
        )

    def small_step(number):
        small_copy(number).wait()
        small_now[number + 1] = small_now[number] + small_in[number]
        if number + 1 < len(partners):
            small_copy(number + 1).start()

    if not alone:
        small_copy(0).start()
        ff.advance(0)
        qkv.allow(2, "core")
        far_start(1)
    weight_side(qkv, 1, lambda sl: wide[sl, :], lambda left, col: mul(left, k_t[at(col, cols, 16), :], 1, 1), 1 - core)
    if not alone:
        far_start(2)
        small_step(0)
    weight_side(qkv, 1, lambda sl: wide[sl, :], lambda left, col: mul(left, k_t[at(col, cols, 16), :], 1, 1), core)
    if not alone:
        ff.drain_other(0)
        ff.drain_acc(0)
        qkv.core_add(1)
        far_start(3)
        small_step(1)
    weight_side(qkv, 2, lambda sl: wide[sl, :], lambda left, col: mul(left, v_t[at(col, cols, 16), :], 1, 1), 1 - core)
    if not alone:
        qkv.advance(0)
        far_start(4)
        small_step(2)
    weight_side(qkv, 2, lambda sl: wide[sl, :], lambda left, col: mul(left, v_t[at(col, cols, 16), :], 1, 1), core)
    if alone:
        for part in range(3):
            weight_out(part, qkv_out, part * width)
    if alone:
        small_out[...] = small_now[0]
        tail = [local(grad_hidden, hidden_out, 18), local(flat, acted_out, 19)]
        for copy in tail:
            copy.start()
        loads["state"].wait()
        for copy in tail + copies_out[6:]:
            copy.wait()
        return

    qkv.core_add(2)
    small_step(3)
    qkv.advance(0)
    qkv.advance(1)
    ff.advance(0)
    for part, target in enumerate((out_out, up_out, down_out)):
        ff.advance(part)
        give_result(ff, part, target, 0)
    for number in range(4, len(partners)):
        small_step(number)
    small_out[...] = small_now[len(partners)]
    qkv.advance(0)
    qkv.advance(2)
    qkv.advance(1)
    qkv.advance(0)

    loads["state"].wait()
    for i in range(tiles):

        @pl.when(far_got)
        def _():
            far(i).wait_recv()


    def final_step(i, carry):
        sl = at(i * 128, 128, 128)
        state = state_low[sl, :].astype(F32)
        inverse = lax.rsqrt(jnp.mean(state * state, axis=-1, keepdims=True) + EPS)
        normed = state * inverse
        grad = flat[2, sl, :].astype(F32)
        grad += jnp.where(even, near_in[sl, :].astype(F32), 0.0)
        grad += jnp.where(far_got, far_in[sl, :].astype(F32), 0.0)
        weighted = grad * rows_in[0:1, :]
        along = jnp.mean(weighted * normed, axis=-1, keepdims=True)
        state_low[sl, :] = (grad_hidden[sl, :] + inverse * (weighted - normed * along)).astype(BF16)
        return carry

    lax.fori_loop(0, length // 128, final_step, 0)
    write = local(state_low, input_grad, 18)
    write.start()
    qkv.advance(2)
    qkv.advance(1)
    qkv.advance(2)
    qkv.advance(1)

    while min(qkv.at_stage) <= bits:
        for part in range(3):
            if qkv.at_stage[part] <= bits:
                qkv.advance(part)
    for part in range(3):
        qkv.advance(part)
    for part in range(3):
        qkv.advance(part)
        give_result(qkv, part, qkv_out, part * width)

    for i in range(tiles):

        @pl.when(odd | far_ok)
        def _():
            give(i).wait_send()

        @pl.when(far_ok)
        def _():
            far(i).wait_send()

    for part in range(3):
        qkv.drain_other(part)
        qkv.drain_acc(part)
        qkv.drain_result(part)
        ff.drain_result(part)
    for copy in copies_out:
        copy.wait()
    write.wait()


FF_STEPS = (
    (0, 2, 0), (2, 1, 0), (6, 2, 1), (7, 1, 1), (9, 2, 2), (10, 0, 0),
    (11, 1, 2), (12, 2, 3), (13, 1, 3), (14, 0, 1), (15, 2, 4), (15, 1, 4),
)


def backward(count, alone, *inputs):
    length, width = inputs[0].shape
    total = 3 * length
    rows = width // count
    cols = width // 2
    heads = width // HEAD
    bits = count.bit_length() - 1
    shape = jax.ShapeDtypeStruct
    if alone:
        outs = (
            shape((length, width), F32),
            shape((width, 3 * width), BF16),
            shape((width, width), BF16),
            shape((width, width), BF16),
            shape((width, width), BF16),
            shape((3, length, width), BF16),
            shape((8, width), F32),
        )
        params = pltpu.CompilerParams(vmem_limit_bytes=VMEM_LIMIT)
    else:
        outs = (
            shape((length, width), BF16),
            shape((rows, 3 * width), BF16),
            shape((rows, width), BF16),
            shape((rows, width), BF16),
            shape((rows, width), BF16),
            shape((8, width), F32),
        )
        params = pltpu.CompilerParams(collective_id=1, has_side_effects=True, vmem_limit_bytes=VMEM_LIMIT)
    buffer = pltpu.VMEM
    return pl.pallas_call(
        functools.partial(backward_kernel, count, alone),
        name="backward_layer",
        out_shape=outs,
        in_specs=[ANY] * 16 + [VM] * 3,
        out_specs=(ANY,) * (len(outs) - 1) + (VM,),
        scratch_shapes=[
            buffer((width, total), BF16),
            buffer((3, length, width), BF16),
            buffer((6, TILE, width), BF16),
            buffer((length, width), F32),
            buffer((length, width), F32),
            buffer((width, length), BF16),
            buffer((width, total), BF16),
            buffer((width, total), BF16),
            buffer((width, length), BF16),
            buffer((heads, 1, length), F32),
            buffer((total, length), F32),
            buffer((HEAD, length), F32),
            buffer((3, width, cols), BF16),
            buffer((3, width, cols), BF16),
            buffer((3, width, cols), BF16),
            buffer((3, 2, rows, cols), BF16),
            buffer((3, 2, rows, cols), BF16),
            buffer((8, 128), F32),
            buffer((length, width), BF16),
            buffer((length, width), BF16),
            buffer((length, width), BF16),
            buffer((bits + 3, 8, width), F32),
            buffer((bits + 2, 8, width), F32),
            pltpu.SemaphoreType.DMA((40,)),
            pltpu.SemaphoreType.DMA((192,)),
            pltpu.SemaphoreType.DMA((192,)),
            pltpu.SemaphoreType.REGULAR((2, 3 * (bits + 2))),
        ],
        compiler_params=params,
    )(*inputs)


def shifted(value, steps):
    count = lax.axis_size("shard")
    first, last = (max(0, -steps), min(count, count - steps))
    return lax.ppermute(value, "shard", [(source, source + steps) for source in range(first, last)])


def gather_plain(tokens, segs, vec, *weights):
    whole = tuple(lax.all_gather(weight, "shard", axis=0, tiled=True) for weight in weights)
    earlier = jnp.concatenate([shifted(tokens, 2), shifted(tokens, 1)])
    seg_ext = jnp.stack([shifted(segs, 2), shifted(segs, 1), segs])
    return (earlier, seg_ext, lax.all_gather(vec, "shard", axis=0)) + whole


def reduce_plain(qkv_grad, out_grad, up_grad, down_grad, grad_acted, small):
    owned = []
    for grad in (qkv_grad, out_grad, up_grad, down_grad):
        part = lax.psum_scatter(grad, "shard", scatter_dimension=0, tiled=True)
        owned.append(lax.psum(part, "rep").astype(F32))
    parts = [grad_acted[2], shifted(grad_acted[0], -2), shifted(grad_acted[1], -1)]
    return (*owned, sum(part.astype(F32) for part in parts), lax.psum(small, ("rep", "shard")))


def body(
    tokens,
    segments,
    cotangent,
    gain_one,
    qkv_weight,
    query_scale,
    out_weight,
    gain_two,
    up_weight,
    up_bias,
    down_weight,
    down_bias,
):
    count = lax.axis_size("shard")
    shard = lax.axis_index("shard")
    length, width = tokens.shape[1:]
    rows = qkv_weight.shape[0]
    heads = width // HEAD

    vec = jnp.stack([gain_one, gain_two, up_bias, down_bias])
    vec = jnp.pad(vec, ((0, 12), (0, -rows % 128)))
    segs = jnp.broadcast_to(segments, (8, length))
    whole_tiles = rows % 32 == 0 and count >= 4 and count & (count - 1) == 0 and lax.axis_size("rep") == 4
    factor = LOG2E / math.sqrt(HEAD) * jax.nn.softplus(query_scale)
    factor_row = jnp.tile(factor, heads)[None]
    weights = (qkv_weight, out_weight, up_weight, down_weight)
    earlier = None
    if not whole_tiles:
        earlier, segs, vec, *weights = gather_plain(tokens[0], segs, vec, *weights)
    output, acted_t, q_t, k_t, v_t, o_t, lse, hidden, inner_t, upper, lower_t, rows_in, qkv, out, up, down, mask = forward(
        count, tokens[0], earlier, segs, vec, factor_row * (1.0 / LN2), *weights
    )
    results = backward(
        count, not whole_tiles, cotangent[0], tokens[0], hidden, inner_t, upper, lower_t, o_t, q_t, k_t, v_t, acted_t,
        qkv, out, up, down, mask, lse, rows_in, factor[:, None],
    )
    if whole_tiles:
        input_grad, qkv_own, out_own, up_own, down_own, small_sum = results
        qkv_own, out_own, up_own, down_own = (part.astype(F32) for part in (qkv_own, out_own, up_own, down_own))
    else:
        grad_hidden, *partial = results
        qkv_own, out_own, up_own, down_own, grad_acted, small_sum = reduce_plain(*partial)
        state = tokens[0].astype(F32)
        inverse = lax.rsqrt(jnp.mean(state * state, axis=-1, keepdims=True) + EPS)
        normed = state * inverse
        weighted = grad_acted * rows_in[0:1]
        along = jnp.mean(weighted * normed, axis=-1, keepdims=True)
        input_grad = (grad_hidden + inverse * (weighted - normed * along)).astype(BF16)

    mine = lax.dynamic_slice_in_dim(small_sum[:4], shard * rows, rows, 1)
    scale_grad = (
        small_sum[4, :HEAD]
        * LN2
        / factor
        * (LOG2E / math.sqrt(HEAD))
        * jax.nn.sigmoid(query_scale)
    )
    return (
        output[None],
        input_grad[None],
        mine[0],
        qkv_own,
        scale_grad,
        out_own,
        mine[1],
        up_own,
        mine[2],
        down_own,
        mine[3],
    )


def solution(mesh):
    return jax.shard_map(
        body,
        mesh=mesh,
        in_specs=(
            P("rep", "shard", None),
            P("rep", "shard"),
            P("rep", "shard", None),
            P("shard"),
            P("shard", None),
            P(),
            P("shard", None),
            P("shard"),
            P("shard", None),
            P("shard"),
            P("shard", None),
            P("shard"),
        ),
        out_specs=(
            P("rep", "shard", None),
            P("rep", "shard", None),
            P("shard"),
            P("shard", None),
            P(),
            P("shard", None),
            P("shard"),
            P("shard", None),
            P("shard"),
            P("shard", None),
            P("shard"),
        ),
        check_vma=False,
    )
```

```python
import functools
import math

import jax
import jax.numpy as jnp
from jax import lax
from jax.experimental import pallas as pl
from jax.experimental.pallas import tpu as pltpu
from jax.sharding import PartitionSpec as P

HEAD = 80
WINDOW = 1024
EPS = 1e-06
LOG2E = 1.442695041
LN2 = math.log(2.0)
MASKED = -1e30
TILE = 256
MESH = pl.DeviceIdType.MESH
F32 = jnp.float32
BF16 = jnp.bfloat16
VMEM_LIMIT = 62 * 2**20
ANY = pl.BlockSpec(memory_space=pl.ANY)
VM = pl.BlockSpec(memory_space=pltpu.VMEM)


def mul(a, b, left=1, right=0):
    return lax.dot_general(a, b, (((left,), (right,)), ((), ())), preferred_element_type=F32)


def at(start, size, unit):
    return pl.ds(pl.multiple_of(start, unit), size)


def bit_of(index, bit):
    return lax.rem(lax.div(index, 1 << bit), 2)


def flip(index, mask):
    out = index
    bit = 0
    while mask >> bit:
        if (mask >> bit) & 1:
            out = out + (1 - 2 * bit_of(index, bit)) * (1 << bit)
        bit += 1
    return out


def span(bits):
    masks = [0]
    for bit in bits:
        masks = masks + [mask | (1 << bit) for mask in masks]
    return masks


def stage_orders(bits):
    rest = list(range(2, bits))
    return (["x", 0, 1] + rest, [0, 1, "x"] + rest, [1, "x", 0] + rest)


def cross_orders(bits):
    rest = list(range(2, bits))
    return (["x", 0, 1] + rest, ["x", 1, 0] + rest, ["x", 0, 1] + rest)


def greet(count):
    rep, shard = lax.axis_index("rep"), lax.axis_index("shard")
    barrier = pltpu.get_barrier_semaphore()
    for step in range(1, count):
        other = lax.rem(shard + step, count)
        pl.semaphore_signal(barrier, inc=1, device_id={"rep": rep, "shard": other}, device_id_type=MESH)
    for mask in (1, 2):
        pl.semaphore_signal(barrier, inc=1, device_id={"rep": flip(rep, mask), "shard": shard}, device_id_type=MESH)
    pl.semaphore_wait(barrier, count + 1)


class Sems:
    def __init__(self, send, recv):
        self.send, self.recv, self.used = send, recv, 0

    def slot(self):
        self.used += 1
        return self.used - 1

    def remote(self, src, dst, rep, shard, slot=None):
        slot = self.slot() if slot is None else slot
        return pltpu.make_async_remote_copy(
            src_ref=src,
            dst_ref=dst,
            send_sem=self.send.at[slot],
            recv_sem=self.recv.at[slot],
            device_id={"rep": rep, "shard": shard},
            device_id_type=MESH,
        )


class Doubling:
    def __init__(self, sems, count, rows, orders, parts):
        self.sems, self.rows, self.half, self.parts = sems, rows, rows // 2, parts
        bits = count.bit_length() - 1
        self.stages = bits + 1
        self.plan = []
        for order in orders:
            have, whole, stages = [], False, []
            for what in order[::-1]:
                masks = span(have)[1:] if what == "x" else span(have)
                stages.append([(what, mask, whole, sems.slot(), sems.slot()) for mask in masks])
                if what == "x":
                    whole = True
                else:
                    have.append(what)
            self.plan.append(stages)

    def copy(self, part, step):
        what, mask, whole, slot, _ = step
        rep, shard = lax.axis_index("rep"), lax.axis_index("shard")
        core, cross = lax.rem(rep, 2), lax.div(rep, 2)
        src, dst, first, cols = self.parts[part]
        across = at(first + core * cols, cols, 128)
        shift, size = (0, self.rows) if whole else (cross * self.half, self.half)
        row = flip(shard, mask) * self.rows + shift
        to = dst.at[at(row, size, 16), across]
        here = src.at[at(shift, size, 16), across] if mask == 0 else to
        if what == "x":
            return self.sems.remote(here, to, flip(rep, 2), shard, slot)
        return self.sems.remote(here, to, rep, flip(shard, 1 << what), slot)

    def ahead(self, part, step):
        what, mask, whole, _, slot = step
        rep, shard = lax.axis_index("rep"), lax.axis_index("shard")
        core, cross = lax.rem(rep, 2), lax.div(rep, 2)
        _, dst, first, cols = self.parts[part]
        if what == "x":
            row, size = flip(shard, mask) * self.rows + (1 - cross) * self.half, self.half
        else:
            shift, size = (0, self.rows) if whole else (cross * self.half, self.half)
            row = flip(shard, mask | (1 << what)) * self.rows + shift
        spot = dst.at[at(row, size, 16), at(first + core * cols, cols, 128)]
        return self.sems.remote(spot, spot, flip(rep, 1), shard, slot)

    def send(self, stage):
        for part in range(3):
            for step in self.plan[part][stage]:
                self.copy(part, step).start()

    def settle(self, stage):
        for part in range(3):
            for step in self.plan[part][stage]:
                self.copy(part, step).wait_recv()
                self.ahead(part, step).start()

    def move(self, stage):
        for part in range(3):
            for step in self.plan[part][stage]:
                self.copy(part, step).wait_recv()
            for step in self.plan[part][stage + 1]:
                self.copy(part, step).start()
            for step in self.plan[part][stage]:
                self.ahead(part, step).start()

    def finish(self):
        for part in range(3):
            for stage in self.plan[part]:
                for step in stage:
                    self.ahead(part, step).wait_recv()

    def drain(self):
        for part in range(3):
            for stage in self.plan[part]:
                for step in stage:
                    self.copy(part, step).wait_send()
                    self.ahead(part, step).wait_send()


def tail_orders(bits):
    rest = list(range(2, bits))
    cross = ["x", 0, 1] + rest
    return (cross, cross, ["x", 1, 0] + rest, [0, "x", 1] + rest, cross)


def beside_orders(bits):
    rest = list(range(2, bits))
    return (["x", 0, 1] + rest, [0, 1, "x"] + rest, [1, 0, "x"] + rest)


class Gathered:
    stages = 1

    def send(self, stage):
        pass

    settle = move = send

    def finish(self):
        pass

    drain = finish


def forward_kernel(count, *refs):
    (tokens, earlier, segs, vec, factor, w_qkv, w_out, w_up, w_down) = refs[:9]
    results = refs[9:26]
    alone = earlier is not None
    (
        output_hbm, acted_t_hbm, q_t_hbm, k_t_hbm, v_t_hbm, o_t_hbm, lse, hidden_hbm,
        inner_t_hbm, upper_hbm, lower_t_hbm, rows_out, qkv_hbm, out_hbm, up_hbm, down_hbm, mask_hbm,
    ) = results
    (
        seg_ext, vec_full, qkv, out, up, down, acted, acted_t, q_t, k_t, v_t, o_t, heads, inner,
        hidden, upper, inner_t, lower_t, mask, state_low, send, recv, lsem,
    ) = refs[26:]
    rep, shard = lax.axis_index("rep"), lax.axis_index("shard")
    length, width = tokens.shape
    total = 3 * length
    rows = w_qkv.shape[0]
    tiles = width // TILE
    own = pl.ds(total - length, length)
    sems = Sems(send, recv)
    lower, output = heads, inner
    bits = count.bit_length() - 1

    runs = [tiles * 2 // 5, tiles - tiles * 2 // 5]
    starts = [0, runs[0], tiles]
    wide_part = width // 5 // 128 * 128
    last_part = width // 2 - 2 * wide_part
    if alone:
        groups = [Gathered()] * 5
    else:
        groups = []
        for run, start in zip(runs, starts):
            parts = [(w_qkv, qkv, p * width + start * TILE, run * TILE // 2) for p in range(3)]
            groups.append(Doubling(sems, count, rows, stage_orders(bits) if start else cross_orders(bits), parts))
        for w, full in ((w_out, out), (w_up, up), (w_down, down)):
            parts = [(w, full, 0, wide_part), (w, full, 2 * wide_part, wide_part), (w, full, 4 * wide_part, last_part)]
            groups.append(Doubling(sems, count, rows, stage_orders(bits), parts))

    pairs = [(tokens, acted.at[own]), (tokens, state_low)]
    if alone:
        pairs += [(earlier, acted.at[pl.ds(0, 2 * length)]), (segs, seg_ext), (vec, vec_full)]
        pairs += [(w_qkv, qkv), (w_out, out), (w_up, up), (w_down, down)]
    else:
        mine = at(shard * rows, rows, 16)
        pairs += [(segs, seg_ext.at[2]), (vec, vec_full.at[shard])]
        pairs += [(w_qkv, qkv.at[mine]), (w_out, out.at[mine]), (w_up, up.at[mine]), (w_down, down.at[mine])]
    loads = [pltpu.make_async_copy(src, dst, lsem.at[i]) for i, (src, dst) in enumerate(pairs)]
    for copy in loads:
        copy.start()

    odd = lax.rem(shard, 2) == 1
    even = jnp.logical_not(odd)
    far_ok, far_got = shard < count - 2, shard >= 2
    buddy = flip(shard, 1)
    far_to = lax.rem(shard + 2, count)
    nchunk = 8
    part = length // nchunk
    far, near, relay, vecs = [], [], [], []
    for i in range(0 if alone else nchunk):
        here = pl.ds(i * part, part)
        far_spot, near_spot = acted.at[pl.ds(i * part, part)], acted.at[pl.ds(length + i * part, part)]
        slot = sems.slot()
        far.append(sems.remote(tokens.at[here], far_spot, rep, far_to, sems.slot()))
        near.append(sems.remote(tokens.at[here], near_spot, rep, buddy, slot))
        relay.append(sems.remote(far_spot, near_spot, rep, buddy, slot))
    if not alone:
        slot = sems.slot()
        far.append(sems.remote(segs, seg_ext.at[0], rep, far_to, sems.slot()))
        near.append(sems.remote(segs, seg_ext.at[1], rep, buddy, slot))
        relay.append(sems.remote(seg_ext.at[0], seg_ext.at[1], rep, buddy, slot))
        vecs = [
            sems.remote(vec, vec_full.at[shard], rep, lax.rem(shard + step, count), sems.slot()) for step in range(1, count)
        ]

    def far_start(*which):
        @pl.when(far_ok)
        def _():
            for i in which:
                far[i].start()

    def near_start(*which):
        @pl.when(even)
        def _():
            for i in which:
                near[i].start()

    def far_next(i):
        @pl.when(far_ok)
        def _():
            far[i].wait_send()
            far[i + 2].start()

    def near_next(i):
        @pl.when(even)
        def _():
            near[i].wait_send()
            near[i + 2].start()

    def relay_start(*which):
        @pl.when(far_got)
        def _():
            for i in which:
                far[i].wait_recv()

        @pl.when(odd & far_got)
        def _():
            for i in which:
                relay[i].start()

    if not alone:
        greet(count)
        groups[0].send(0)
        far_start(nchunk, 0, 1)
        near_start(nchunk, 0, 1)
        for copy in vecs:
            copy.start()
        groups[0].move(0)
        relay_start(nchunk)
        for i in range(nchunk):
            relay_start(i)
            if i + 2 < nchunk:
                far_next(i)
                near_next(i)
            if i == 0:
                groups[0].move(1)
            if i == 2:
                groups[0].move(2)
            if i == 6:
                groups[1].send(0)

    for copy in loads:
        copy.wait()
    for copy in vecs:
        copy.wait_recv()
    each = width // count
    vectors = jnp.concatenate([vec_full[i][:, :each].astype(F32) for i in range(count)], axis=1)
    rows_out[...] = vectors[:8, :]
    gain_one, gain_two = rows_out[0:1, :], rows_out[1:2, :]

    def norm_rows(i):
        sl = at(i * TILE, TILE, TILE)
        state = acted[sl, :].astype(F32)
        scale = lax.rsqrt(jnp.mean(state * state, axis=-1, keepdims=True) + EPS)
        value = (state * scale * rows_out[0:1, :]).astype(BF16)
        value = jnp.where(shard + i * TILE // length >= 2, value, jnp.zeros_like(value))
        acted[sl, :] = value
        acted_t[:, sl] = value.T

    def norm_step(i, carry):
        norm_rows(i)
        return carry

    per = length // TILE
    lax.fori_loop(2 * per, 3 * per, norm_step, 0)

    groups[0].settle(groups[0].stages - 1)
    groups[0].finish()

    def project_own(i, carry):
        sl = at(i * TILE, TILE, TILE)
        q_t[sl, :] = (mul(acted[own, :], qkv[:, sl]) * factor[:, sl]).astype(BF16).T
        k_t[sl, own] = mul(acted[own, :], qkv[:, at(width + i * TILE, TILE, TILE)]).astype(BF16).T
        v_t[sl, own] = mul(acted[own, :], qkv[:, at(2 * width + i * TILE, TILE, TILE)]).astype(BF16).T
        return carry

    def project_earlier(i, carry):
        sl = at(i * TILE, TILE, TILE)
        k_t[sl, before] = mul(acted[before, :], qkv[:, at(width + i * TILE, TILE, TILE)]).astype(BF16).T
        v_t[sl, before] = mul(acted[before, :], qkv[:, at(2 * width + i * TILE, TILE, TILE)]).astype(BF16).T
        return carry

    def project(i, carry):
        sl = at(i * TILE, TILE, TILE)
        q_t[sl, :] = (mul(acted[own, :], qkv[:, sl]) * factor[:, sl]).astype(BF16).T
        k_t[sl, :] = mul(acted[...], qkv[:, at(width + i * TILE, TILE, TILE)]).astype(BF16).T
        v_t[sl, :] = mul(acted[...], qkv[:, at(2 * width + i * TILE, TILE, TILE)]).astype(BF16).T
        return carry

    before = pl.ds(0, total - length)
    lax.fori_loop(0, runs[0], project_own, 0)
    if not alone:

        @pl.when(odd)
        def _():
            for copy in near:
                copy.wait_recv()

        @pl.when(even & far_got)
        def _():
            for copy in relay:
                copy.wait_recv()

        @pl.when(odd & far_got)
        def _():
            for copy in relay:
                copy.wait_send()

    groups[1].move(0)
    lax.fori_loop(0, 2 * per, norm_step, 0)

    mine = seg_ext[2].astype(F32)[0:1, :]
    for j in range(3):
        column = jnp.where(shard + j >= 2, seg_ext[j].astype(F32).T[:, 0:1], -1.0)
        place = lax.broadcasted_iota(jnp.int32, (length, length), 0) + j * length
        lane = lax.broadcasted_iota(jnp.int32, (length, length), 1)
        near_by = (place > lane) & (place <= lane + WINDOW)
        mask[j * length : (j + 1) * length, :] = jnp.where(near_by & (column == mine), 0.0, MASKED)

    groups[1].move(1)
    for group in groups[2:]:
        group.send(0)
    lax.fori_loop(0, runs[0], project_earlier, 0)
    groups[1].move(2)

    half = length // 2

    def attend(h):
        sl = at(h * HEAD, HEAD, 16)
        key, query = k_t[sl, :].T, q_t[sl, :]
        first, last = pl.ds(0, half), pl.ds(total - half, half)
        middle = pl.ds(half, total - length)
        score_m = mul(key[half : total - half], query) + mask[middle, :]
        score_f = mul(key[:half], query[:, :half]) + mask[first, :half]
        score_l = mul(key[total - half :], query[:, half:]) + mask[last, half:]
        ends = [jnp.max(score, axis=0, keepdims=True) for score in (score_f, score_l)]
        top = jnp.maximum(jnp.max(score_m, axis=0, keepdims=True), jnp.concatenate(ends, axis=1))
        prob_m = jnp.exp2(score_m - top)
        prob_f = jnp.exp2(score_f - top[:, :half])
        prob_l = jnp.exp2(score_l - top[:, half:])
        ends = [jnp.sum(prob, axis=0, keepdims=True) for prob in (prob_f, prob_l)]
        norm = jnp.sum(prob_m, axis=0, keepdims=True) + jnp.concatenate(ends, axis=1)
        ends = [mul(v_t[sl, first], prob_f.astype(BF16)), mul(v_t[sl, last], prob_l.astype(BF16))]
        mixed = mul(v_t[sl, middle], prob_m.astype(BF16)) + jnp.concatenate(ends, axis=1)
        o_t[sl, :] = (mixed * (1.0 / norm)).astype(BF16)
        lse[h] = top + jnp.log2(norm)

    pairs = [start * TILE // HEAD // 2 for start in starts]
    last = groups[0].stages - 1

    def steps(index, table):
        for number, actions in table.items():

            @pl.when(index == number)
            def _():
                for group, what in actions:
                    if what == "send":
                        groups[group].send(0)
                    elif what == "settle":
                        groups[group].settle(last)
                    else:
                        groups[group].move(what)

    def attend_run(first, stop, table):
        def attend_pair(pair, carry):
            attend(2 * pair)
            attend(2 * pair + 1)
            steps(pair, table)
            return carry

        lax.fori_loop(first, stop, attend_pair, 0)

    def project_run(first, stop, table):
        def project_step(i, carry):
            project(i, carry)
            steps(i, table)
            return carry

        lax.fori_loop(first, stop, project_step, 0)

    attend_run(0, pairs[1], {pairs[1] - 2: [(2, 0), (3, 0), (4, 0)], pairs[1] - 1: [(1, "settle")]})
    groups[1].finish()
    project_run(starts[1], starts[2], {starts[1]: [(2, 1), (3, 1), (4, 1)]})
    keep = [
        pltpu.make_async_copy(src, dst, lsem.at[8 + i])
        for i, (src, dst) in enumerate(((qkv, qkv_hbm), (acted_t, acted_t_hbm), (q_t, q_t_hbm), (k_t, k_t_hbm), (v_t, v_t_hbm), (mask, mask_hbm)))
    ]
    for copy in keep:
        copy.start()

    attend_run(
        pairs[1], pairs[2],
        {pairs[1]: [(2, 2), (3, 2)], pairs[2] - 2: [(2, "settle"), (4, 2)]},
    )

    def keep_more(*more):
        for src, dst in more:
            copy = pltpu.make_async_copy(src, dst, lsem.at[8 + len(keep)])
            copy.start()
            keep.append(copy)

    keep_more((o_t, o_t_hbm))

    def turn(i, carry):
        sl = at(i * TILE, TILE, TILE)
        heads[:, sl] = o_t[sl, :].T
        return carry

    lax.fori_loop(0, tiles, turn, 0)
    groups[2].finish()
    keep_more((out, out_hbm))

    def out_step(i, carry):
        sl = at(i * TILE, TILE, TILE)
        hidden[:, sl] = state_low[:, sl].astype(F32) + mul(heads[...], out[:, sl])
        return carry

    lax.fori_loop(0, tiles, out_step, 0)
    keep_more((hidden, hidden_hbm))

    def norm_two(i, carry):
        sl = at(i * TILE, TILE, TILE)
        value = hidden[sl, :]
        scale = lax.rsqrt(jnp.mean(value * value, axis=-1, keepdims=True) + EPS)
        normed = (value * scale * rows_out[1:2, :]).astype(BF16)
        inner[sl, :] = normed
        inner_t[:, sl] = normed.T
        return carry

    lax.fori_loop(0, length // TILE, norm_two, 0)
    keep_more((inner_t, inner_t_hbm))

    groups[3].settle(last)
    groups[3].finish()
    keep_more((up, up_hbm))

    def up_step(i, carry):
        sl = at(i * TILE, TILE, TILE)
        value = mul(inner[...], up[:, sl]) + rows_out[2:3, sl]
        upper[:, sl] = value
        act = (value / (1.0 + jnp.exp(-value))).astype(BF16)
        lower[:, sl] = act
        lower_t[sl, :] = act.T
        return carry

    lax.fori_loop(0, tiles, up_step, 0)
    keep_more((upper, upper_hbm), (lower_t, lower_t_hbm))

    groups[4].settle(last)
    groups[4].finish()
    keep_more((down, down_hbm))

    def down_step(i, carry):
        sl = at(i * TILE, TILE, TILE)
        output[:, sl] = (hidden[:, sl] + (mul(lower[...], down[:, sl]) + rows_out[3:4, sl])).astype(BF16)
        return carry

    lax.fori_loop(0, tiles, down_step, 0)
    keep_more((output, output_hbm))

    if not alone:

        @pl.when(far_ok)
        def _():
            for copy in far[nchunk - 2 :]:
                copy.wait_send()

        @pl.when(even)
        def _():
            for copy in near[nchunk - 2 :]:
                copy.wait_send()

    for copy in vecs:
        copy.wait_send()
    for group in groups:
        group.drain()
    for copy in keep:
        copy.wait()


def forward(count, tokens, earlier, segs, vec, factor, w_qkv, w_out, w_up, w_down):
    length, width = tokens.shape
    total = 3 * length
    heads = width // HEAD
    inputs = [x for x in (tokens, earlier, segs, vec, factor, w_qkv, w_out, w_up, w_down) if x is not None]
    if earlier is None:
        params = pltpu.CompilerParams(collective_id=0, has_side_effects=True, vmem_limit_bytes=VMEM_LIMIT)
    else:
        params = pltpu.CompilerParams(vmem_limit_bytes=VMEM_LIMIT)
    shape = jax.ShapeDtypeStruct
    outs = (
        shape((length, width), BF16),
        shape((width, total), BF16),
        shape((width, length), BF16),
        shape((width, total), BF16),
        shape((width, total), BF16),
        shape((width, length), BF16),
        shape((heads, 1, length), F32),
        shape((length, width), F32),
        shape((width, length), BF16),
        shape((length, width), F32),
        shape((width, length), BF16),
        shape((8, width), F32),
        shape((width, 3 * width), BF16),
        shape((width, width), BF16),
        shape((width, width), BF16),
        shape((width, width), BF16),
        shape((total, length), F32),
    )
    specs = [ANY] * 17
    specs[6] = specs[11] = VM
    buffer = pltpu.VMEM
    return pl.pallas_call(
        functools.partial(forward_kernel, count) if earlier is not None else lambda *refs: forward_kernel(count, refs[0], None, *refs[1:]),
        name="forward_layer",
        out_shape=outs,
        in_specs=[ANY] * (len(inputs) - 5) + [VM] + [ANY] * 4,
        out_specs=tuple(specs),
        scratch_shapes=[
            buffer((3,) + segs.shape[-2:], jnp.int32),
            buffer((count,) + vec.shape[-2:], BF16),
            buffer((width, 3 * width), BF16),
            buffer((width, width), BF16),
            buffer((width, width), BF16),
            buffer((width, width), BF16),
            buffer((total, width), BF16),
            buffer((width, total), BF16),
            buffer((width, length), BF16),
            buffer((width, total), BF16),
            buffer((width, total), BF16),
            buffer((width, length), BF16),
            buffer((length, width), BF16),
            buffer((length, width), BF16),
            buffer((length, width), F32),
            buffer((length, width), F32),
            buffer((width, length), BF16),
            buffer((width, length), BF16),
            buffer((total, length), F32),
            buffer((length, width), BF16),
            pltpu.SemaphoreType.DMA((448,)),
            pltpu.SemaphoreType.DMA((448,)),
            pltpu.SemaphoreType.DMA((32,)),
        ],
        compiler_params=params,
    )(*inputs)


class Halving:
    def __init__(self, sems, credits, count, rows, orders, acc, other, land, result, reused):
        self.sems, self.credits, self.rows, self.half, self.reused = sems, credits, rows, rows // 2, reused
        self.acc, self.other, self.land, self.result = acc, other, land, result
        self.bits = count.bit_length() - 1
        self.plan, self.core_slot, self.cross_slot, self.share_slot = [], [], [], []
        self.at_stage = [0] * len(orders)
        for order in orders:
            left, whole, base, stages = list(range(self.bits)), True, 0, []
            for what in order:
                steps = []
                if what == "x":
                    whole = False
                else:
                    left.remove(what)
                for mask in span(left):
                    size = rows if whole else self.half
                    steps.append((mask, base, size, sems.slot()))
                    base += size
                stages.append((what, whole, steps))
            self.plan.append(stages)
            self.core_slot.append(sems.slot())
            self.cross_slot.append(sems.slot())
            self.share_slot.append(sems.slot())

    def partner(self, what):
        rep, shard = lax.axis_index("rep"), lax.axis_index("shard")
        if what == "core":
            return flip(rep, 1), shard
        if what == "x":
            return flip(rep, 2), shard
        return rep, flip(shard, 1 << what)

    def credit(self, part, what):
        place = 0 if what == "core" else 1 if what == "x" else 2 + what
        return self.credits.at[part * (self.bits + 2) + place]

    def allow(self, part, what):
        rep, shard = self.partner(what)
        pl.semaphore_signal(
            self.credit(part, what), inc=1, device_id={"rep": rep, "shard": shard}, device_id_type=MESH
        )

    def core_copy(self, part):
        return self.sems.remote(self.other[part], self.land[part], *self.partner("core"), self.core_slot[part])

    def core_send(self, part):
        if self.reused:
            pl.semaphore_wait(self.credit(part, "core"), 1)
        self.core_copy(part).start()

    def core_add(self, part):
        self.core_copy(part).wait_recv()
        acc, land = self.acc[part], self.land[part]

        def step(i, carry):
            sl = at(i * TILE, TILE, TILE)
            acc[sl, :] = (acc[sl, :].astype(F32) + land[sl, :].astype(F32)).astype(BF16)
            return carry

        lax.fori_loop(0, acc.shape[0] // TILE, step, 0)
        for what, _, _ in self.plan[part]:
            self.allow(part, what)
        self.send(part, 0)

    def copy(self, part, stage, step):
        what, whole, _ = self.plan[part][stage]
        mask, base, size, slot = step
        shard, cross = lax.axis_index("shard"), lax.div(lax.axis_index("rep"), 2)
        if what == "x":
            row = flip(shard, mask) * self.rows + (1 - cross) * self.half
        else:
            row = flip(shard, mask | (1 << what)) * self.rows
            row = row if whole else row + cross * self.half
        src = self.acc[part].at[at(row, size, 16)]
        return self.sems.remote(src, self.land[part].at[pl.ds(base, size)], *self.partner(what), slot)

    def send(self, part, stage):
        what, _, steps = self.plan[part][stage]
        pl.semaphore_wait(self.credit(part, what), 1)
        for step in steps:
            self.copy(part, stage, step).start()

    def receive(self, part, stage):
        what, whole, steps = self.plan[part][stage]
        shard, cross = lax.axis_index("shard"), lax.div(lax.axis_index("rep"), 2)
        for step in steps:
            mask, base, size, _ = step
            self.copy(part, stage, step).wait_recv()
            row = flip(shard, mask) * self.rows
            row = row if whole else row + cross * self.half
            sl = at(row, size, 16)
            new = self.acc[part][sl, :].astype(F32) + self.land[part][pl.ds(base, size), :].astype(F32)
            self.acc[part][sl, :] = new.astype(BF16)

    def advance(self, part):
        stage = self.at_stage[part]
        self.at_stage[part] += 1
        if stage <= self.bits:
            self.receive(part, stage)
        if stage < self.bits:
            self.send(part, stage + 1)
        elif stage == self.bits:
            core, cross = self.sides()
            shard = lax.axis_index("shard")
            row = shard * self.rows + cross * self.half
            self.result[part].at[core][at(cross * self.half, self.half, 16), :] = self.acc[part][at(row, self.half, 16), :]
            self.cross_copy(part).start()
        elif stage == self.bits + 1:
            self.cross_copy(part).wait_recv()
            self.share_copy(part).start()
        else:
            self.share_copy(part).wait_recv()

    def sides(self):
        rep = lax.axis_index("rep")
        return lax.rem(rep, 2), lax.div(rep, 2)

    def cross_copy(self, part):
        core, cross = self.sides()
        spot = self.result[part].at[core, at(cross * self.half, self.half, 16)]
        return self.sems.remote(spot, spot, *self.partner("x"), self.cross_slot[part])

    def share_copy(self, part):
        core, _ = self.sides()
        spot = self.result[part].at[core]
        return self.sems.remote(spot, spot, *self.partner("core"), self.share_slot[part])

    def drain_other(self, part):
        self.core_copy(part).wait_send()

    def drain_acc(self, part):
        for stage in range(self.bits + 1):
            for step in self.plan[part][stage][2]:
                self.copy(part, stage, step).wait_send()

    def drain_result(self, part):
        self.cross_copy(part).wait_send()
        self.share_copy(part).wait_send()


def backward_kernel(count, alone, *refs):
    (
        cot_hbm, tokens_hbm, hidden_hbm, inner_t_hbm, upper_hbm, lower_t_hbm, o_t_hbm, q_t_hbm, k_t_hbm, v_t_hbm,
        acted_t_hbm, qkv_hbm, out_hbm, up_hbm, down_hbm, mask_hbm, lse, rows_in, factor,
    ) = refs[:19]
    if alone:
        (hidden_out, qkv_out, out_out, up_out, down_out, acted_out, small_out) = refs[19:26]
    else:
        (input_grad, qkv_out, out_out, up_out, down_out, small_out) = refs[19:25]
    scratch = refs[26:] if alone else refs[25:]
    (
        wide, flat, wtile, first_f32, grad_hidden, q_t, k_t, v_t, do_t, delta, mask, scale_sum, acc, other, land,
        result_ff, result_qkv, turned, near_in, far_in, state_low, small_now, small_in, lsem, send, recv, credits,
    ) = scratch
    rep, shard = lax.axis_index("rep"), lax.axis_index("shard")
    core = lax.rem(rep, 2)
    length, width = cot_hbm.shape
    total = 3 * length
    tiles = width // TILE
    rows = width // count
    cols = width // 2
    heads = width // HEAD
    own = pl.ds(total - length, length)
    bits = count.bit_length() - 1
    sems = Sems(send, recv)
    lower_t, inner_t, o_t = (wide.at[:, pl.ds(i * length, length)] for i in range(3))
    cot, grad_upper, grad_attn = (flat.at[i] for i in range(3))
    parts = [[ref.at[i] for i in range(3)] for ref in (acc, other, land, result_ff, result_qkv)]

    def local(src, dst, slot):
        return pltpu.make_async_copy(src, dst, lsem.at[slot])

    loads = {
        "cot": local(cot_hbm, cot, 0),
        "lower": local(lower_t_hbm, lower_t, 1),
        "upper": local(upper_hbm, first_f32, 2),
        "inner": local(inner_t_hbm, inner_t, 3),
        "o": local(o_t_hbm, o_t, 4),
        "q": local(q_t_hbm, q_t, 5),
        "k": local(k_t_hbm, k_t, 6),
        "v": local(v_t_hbm, v_t, 7),
        "mask": local(mask_hbm, mask, 8),
        "state": local(tokens_hbm, state_low, 9),
    }
    load_hidden = local(hidden_hbm, first_f32, 10)
    load_acted = local(acted_t_hbm, wide, 11)

    def tile_copy(src, order, i):
        slot = lax.rem(order * tiles + i, 6)
        return local(src.at[at(i * TILE, TILE, TILE)], wtile.at[slot], 12 + slot)

    def wide_copies(i):
        first = 3 * (i % 2)
        return [
            local(qkv_hbm.at[pl.ds(i * TILE, TILE), pl.ds(k * width, width)], wtile.at[first + k], 12 + first + k)
            for k in range(3)
        ]

    def tile_next(src, after, order, i):
        tile_copy(src, order, i).wait()
        if after is not None:
            tile_copy(after, order + 1, i).start()
        return lax.rem(order * tiles + i, 6)

    for name in ("lower", "cot"):
        loads[name].start()
    loads["upper"].start()
    for i in range(tiles):
        tile_copy(down_hbm, 0, i).start()
    for name in ("inner", "o"):
        loads[name].start()
    if alone:
        ff = qkv = None
    else:
        greet(count)
        ff = Halving(sems, credits.at[0], count, rows, beside_orders(bits), *parts[:4], False)
        cut = cols * 3 // 5 // 128 * 128
        runs = ((0, 0, cols), (1, 0, cut), (1, cut, cols - cut), (2, 0, cut), (2, cut, cols - cut))
        back = [[ref.at[2 - m, :, pl.ds(at_col, size)] for m, at_col, size in runs] for ref in (acc, other, land)]
        ends = [result_qkv.at[m, :, :, pl.ds(at_col, size)] for m, at_col, size in runs]
        qkv = Halving(sems, credits.at[1], count, rows, tail_orders(bits), *back, ends, True)
    copies_out = []

    def group_parts(first_use, part):
        return (part,) if first_use else ((0,), (1, 2), (3, 4))[part]

    def weight_side(group, part, left, right, side_core, first_use=False):
        theirs = side_core is not core
        dest = (other if theirs else acc).at[part if first_use else 2 - part]

        def step(i, carry):
            sl = at(i * cols, cols, 16)
            dest[sl, :] = right(left(sl), side_core * cols).astype(BF16)
            return carry

        lax.fori_loop(0, 2, step, 0)
        if theirs and group is not None:
            for run in group_parts(first_use, part):
                group.core_send(run)

    def weight_out(part, target, first, first_use=False):
        for ref, side_core in ((other, 1 - core), (acc, core)):
            copy = local(ref.at[part if first_use else 2 - part], target.at[:, at(first + side_core * cols, cols, 128)], 20 + len(copies_out))
            copy.start()
            copies_out.append(copy)

    def weight_grad(group, part, left, right, target):
        weight_side(group, part, left, right, 1 - core, True)
        weight_side(group, part, left, right, core, True)
        if alone:
            weight_out(part, target, 0, True)

    small_now[0] = jnp.zeros_like(small_now[0])
    loads["lower"].wait()
    loads["cot"].wait()
    weight_grad(
        ff, 2, lambda sl: lower_t[sl, :], lambda left, col: mul(left, cot[:, at(col, cols, 128)]), down_out
    )
    loads["upper"].wait()

    def down_step(i, carry):
        sl = at(i * TILE, TILE, TILE)
        slot = tile_next(down_hbm, up_hbm, 0, i)
        grad_lower = mul(cot[...], wtile[slot], 1, 1)
        value = first_f32[:, sl]
        gate = 1.0 / (1.0 + jnp.exp(-value))
        grad = (grad_lower * (gate + value * gate * (1.0 - gate))).astype(BF16)
        grad_upper[:, sl] = grad
        small_now[0, 2:3, sl] = jnp.sum(grad.astype(F32), axis=0, keepdims=True)
        small_now[0, 3:4, sl] = jnp.sum(cot[:, sl].astype(F32), axis=0, keepdims=True)
        return carry

    lax.fori_loop(0, tiles, down_step, 0)
    load_hidden.start()
    for name in ("q", "k", "v", "mask", "state"):
        loads[name].start()
    loads["inner"].wait()
    weight_grad(
        ff, 1, lambda sl: inner_t[sl, :], lambda left, col: mul(left, grad_upper[:, at(col, cols, 128)]), up_out
    )
    if not alone:
        ff.core_add(2)

    def up_step(i, carry):
        sl = at(i * TILE, TILE, TILE)
        slot = tile_next(up_hbm, out_hbm, 1, i)
        grad_hidden[:, sl] = mul(grad_upper[...], wtile[slot], 1, 1)
        return carry

    lax.fori_loop(0, tiles, up_step, 0)
    load_hidden.wait()
    if not alone:
        ff.core_add(1)

    def norm_step(i, carry):
        sl = at(i * TILE, TILE, TILE)
        value = first_f32[sl, :]
        scale = lax.rsqrt(jnp.mean(value * value, axis=-1, keepdims=True) + EPS)
        normed = value * scale
        grad = grad_hidden[sl, :]
        small_now[0, 1:2, :] += jnp.sum(grad * normed, axis=0, keepdims=True)
        weighted = grad * rows_in[1:2, :]
        along = jnp.mean(weighted * normed, axis=-1, keepdims=True)
        whole = cot[sl, :].astype(F32) + scale * (weighted - normed * along)
        grad_hidden[sl, :] = whole
        grad_attn[sl, :] = whole.astype(BF16)
        return carry

    lax.fori_loop(0, length // TILE, norm_step, 0)
    loads["o"].wait()
    weight_grad(
        ff, 0, lambda sl: o_t[sl, :], lambda left, col: mul(left, grad_attn[:, at(col, cols, 128)]), out_out
    )

    def out_step(i, carry):
        sl = at(i * TILE, TILE, TILE)
        slot = tile_next(out_hbm, None, 2, i)
        do_t[sl, :] = mul(grad_attn[...], wtile[slot], 1, 1).astype(BF16).T
        return carry

    lax.fori_loop(0, tiles, out_step, 0)
    if not alone:
        ff.core_add(0)

    def delta_step(h, carry):
        sl = at(h * HEAD, HEAD, 16)
        delta[h] = jnp.sum(o_t[sl, :].astype(F32) * do_t[sl, :].astype(F32), axis=0, keepdims=True)
        return carry

    lax.fori_loop(0, heads, delta_step, 0)
    load_acted.start()
    for i in range(2):
        for copy in wide_copies(i):
            copy.start()
    for name in ("q", "k", "v", "mask"):
        loads[name].wait()
    scale_sum[...] = jnp.zeros_like(scale_sum)
    half = length // 2
    pieces = (
        (0, half, (0,)),
        (half, length, (0, 1)),
        (half + length, length, (0, 1)),
        (total - half, half, (1,)),
    )

    def attend(h, carry):
        sl = at(h * HEAD, HEAD, 16)
        query, grad = q_t[sl, :], do_t[sl, :]
        parts_dq = [jnp.zeros((HEAD, half), F32)] * 2
        for first, size, sides in pieces:
            ks, qs = pl.ds(first, size), slice(sides[0] * half, (sides[-1] + 1) * half)
            key, value = k_t[sl, ks], v_t[sl, ks]
            query_part, grad_part = query[:, qs], grad[:, qs]
            probs = jnp.exp2(mul(key.T, query_part) + mask[ks, qs] - lse[h][:, qs])
            scores = (probs * (mul(value.T, grad_part) - delta[h][:, qs])).astype(BF16)
            v_t[sl, ks] = mul(grad_part, probs.astype(BF16), 1, 1).astype(BF16)
            k_t[sl, ks] = (mul(query_part, scores, 1, 1) * LN2).astype(BF16)
            term = mul(key, scores)
            for place, side in enumerate(sides):
                parts_dq[side] = parts_dq[side] + term[:, place * half : (place + 1) * half]
        dq = jnp.concatenate(parts_dq, axis=1)
        scale_sum[...] += dq * query.astype(F32)
        q_t[sl, :] = (dq * factor[...]).astype(BF16)
        if not alone:
            for head in sorted({step[0] for step in FF_STEPS}):

                @pl.when(h == head)
                def _():
                    for _, part, stage in [step for step in FF_STEPS if step[0] == head]:
                        ff.at_stage[part] = stage
                        ff.advance(part)
                        if stage == bits:
                            for run in group_parts(False, 2 - part):
                                qkv.allow(run, "core")

        return carry

    lax.fori_loop(0, heads, attend, 0)

    def give_result(group, part, target, first):
        for side in range(2):
            src = (result_ff if group is ff else result_qkv).at[part, side]
            copy = local(src, target.at[:, pl.ds(first + side * cols, cols)], 20 + len(copies_out))
            copy.start()
            copies_out.append(copy)

    load_acted.wait()
    odd = lax.rem(shard, 2) == 1
    even = jnp.logical_not(odd)
    far_ok, far_got = shard >= 2, shard < count - 2
    buddy = flip(shard, 1)
    far_to = lax.rem(shard + count - 2, count)
    give_slots = [sems.slot() for _ in range(tiles)]
    far_slots = [sems.slot() for _ in range(tiles)]

    def give(i):
        sl = pl.ds(i * TILE, TILE)
        return sems.remote(flat.at[1, :, sl], near_in.at[:, sl], rep, buddy, give_slots[i])

    def far(i):
        sl = pl.ds(i * TILE, TILE)
        return sems.remote(flat.at[0, :, sl], far_in.at[:, sl], rep, far_to, far_slots[i])

    def state_step(i):
        sl = pl.ds(i * TILE, TILE)
        for copy in wide_copies(i):
            copy.wait()
        slot = 3 * (i % 2)
        both = mul(wtile[slot + 1], k_t[...]) + mul(wtile[slot + 2], v_t[...])
        mine = both[:, total - length :] + mul(wtile[slot], q_t[...])
        both = jnp.concatenate([both[:, : total - length], mine], axis=1)
        low = both.astype(BF16)
        sums = jnp.sum(both * wide[sl, :].astype(F32), axis=1, keepdims=True)
        small_now[0, 0:1, sl] = jnp.broadcast_to(sums, (TILE, 128)).T[0:1, :] / rows_in[0:1, sl]
        for j in range(3):
            flat[j, :, sl] = low[:, j * length : (j + 1) * length].T
        if i + 2 < tiles:
            for copy in wide_copies(i + 2):
                copy.start()

    def give_start(i):
        @pl.when(odd | far_ok)
        def _():
            give(i).start()

    def far_start(i):
        @pl.when(even | far_ok)
        def _():
            give(i).wait_recv()

        @pl.when(odd & far_ok)
        def _():
            sl = pl.ds(i * TILE, TILE)
            flat[0, :, sl] = (flat[0, :, sl].astype(F32) + near_in[:, sl].astype(F32)).astype(BF16)

        @pl.when(far_ok)
        def _():
            far(i).start()

    if alone:
        for copy in copies_out:
            copy.wait()
    else:
        ff.at_stage = [max([step[2] + 1 for step in FF_STEPS if step[1] == part]) for part in range(3)]
        for part in (1, 2):
            ff.drain_other(part)
            ff.drain_acc(part)
    for side_core in (1 - core, core):
        weight_side(
            qkv, 0, lambda sl: wide[sl, own], lambda left, col: mul(left, q_t[at(col, cols, 16), :], 1, 1), side_core
        )
    for i in range(tiles):
        state_step(i)
        if alone:
            continue
        give_start(i)
        if i == 0:
            qkv.core_add(0)
            ff.advance(0)
        if i == 4:
            far_start(0)
    spread = jnp.sum(scale_sum[...], axis=1, keepdims=True)
    small_now[0, 4:5, 0:HEAD] = jnp.broadcast_to(spread, (HEAD, 128)).T[0:1, :]
    partners = ("core", "x") + tuple(range(bits))
    small_slots = [sems.slot() for _ in partners]

    def small_copy(number):
        return sems.remote(
            small_now.at[number], small_in.at[number], *ff.partner(partners[number]), small_slots[number]
        )

    def small_step(number):
        small_copy(number).wait()
        small_now[number + 1] = small_now[number] + small_in[number]
        if number + 1 < len(partners):
            small_copy(number + 1).start()

    if not alone:
        small_copy(0).start()
        ff.advance(0)
        for run in group_parts(False, 2):
            qkv.allow(run, "core")
        far_start(1)
    weight_side(qkv, 1, lambda sl: wide[sl, :], lambda left, col: mul(left, k_t[at(col, cols, 16), :], 1, 1), 1 - core)
    if not alone:
        far_start(2)
        small_step(0)
    weight_side(qkv, 1, lambda sl: wide[sl, :], lambda left, col: mul(left, k_t[at(col, cols, 16), :], 1, 1), core)
    if not alone:
        ff.drain_other(0)
        ff.drain_acc(0)
        qkv.core_add(1)
        qkv.core_add(2)
        qkv.advance(0)
        far_start(3)
        small_step(1)
    weight_side(qkv, 2, lambda sl: wide[sl, :], lambda left, col: mul(left, v_t[at(col, cols, 16), :], 1, 1), 1 - core)
    if not alone:
        far_start(4)
    weight_side(qkv, 2, lambda sl: wide[sl, :], lambda left, col: mul(left, v_t[at(col, cols, 16), :], 1, 1), core)
    if alone:
        for part in range(3):
            weight_out(part, qkv_out, part * width)
    if alone:
        small_out[...] = small_now[0]
        tail = [local(grad_hidden, hidden_out, 18), local(flat, acted_out, 19)]
        for copy in tail:
            copy.start()
        loads["state"].wait()
        for copy in tail + copies_out[6:]:
            copy.wait()
        return

    qkv.core_add(3)
    qkv.core_add(4)
    small_step(2)

    def round_robin(*order):
        for part in order:
            qkv.advance(part)

    round_robin(0, 2, 1)
    round_robin(4, 3)
    ff.advance(0)
    for part, target in enumerate((out_out, up_out, down_out)):
        ff.advance(part)
        give_result(ff, part, target, 0)
    small_step(3)
    round_robin(0, 2, 1)
    round_robin(4, 3)

    loads["state"].wait()
    for i in range(tiles):

        @pl.when(far_got)
        def _():
            far(i).wait_recv()


    def final_step(i, carry):
        sl = at(i * 128, 128, 128)
        state = state_low[sl, :].astype(F32)
        inverse = lax.rsqrt(jnp.mean(state * state, axis=-1, keepdims=True) + EPS)
        normed = state * inverse
        grad = flat[2, sl, :].astype(F32)
        grad += jnp.where(even, near_in[sl, :].astype(F32), 0.0)
        grad += jnp.where(far_got, far_in[sl, :].astype(F32), 0.0)
        weighted = grad * rows_in[0:1, :]
        along = jnp.mean(weighted * normed, axis=-1, keepdims=True)
        state_low[sl, :] = (grad_hidden[sl, :] + inverse * (weighted - normed * along)).astype(BF16)
        return carry

    lax.fori_loop(0, length // 128, final_step, 0)
    write = local(state_low, input_grad, 18)
    write.start()
    for number in range(4, len(partners)):
        small_step(number)
    small_out[...] = small_now[len(partners)]
    while min(qkv.at_stage) <= bits + 2:
        round_robin(*[part for part in (0, 2, 1, 4, 3) if qkv.at_stage[part] <= bits + 2])
    for part in range(3):
        give_result(qkv, part, qkv_out, part * width)

    for i in range(tiles):

        @pl.when(odd | far_ok)
        def _():
            give(i).wait_send()

        @pl.when(far_ok)
        def _():
            far(i).wait_send()

    for part in range(5):
        qkv.drain_other(part)
        qkv.drain_acc(part)
        qkv.drain_result(part)
    for part in range(3):
        ff.drain_result(part)
    for copy in copies_out:
        copy.wait()
    write.wait()


FF_STEPS = (
    (2, 2, 0), (4, 1, 0), (7, 2, 1), (8, 1, 1), (9, 2, 2), (10, 0, 0),
    (11, 1, 2), (12, 2, 3), (13, 1, 3), (14, 0, 1), (15, 2, 4), (15, 1, 4),
)


def backward(count, alone, *inputs):
    length, width = inputs[0].shape
    total = 3 * length
    rows = width // count
    cols = width // 2
    heads = width // HEAD
    bits = count.bit_length() - 1
    shape = jax.ShapeDtypeStruct
    if alone:
        outs = (
            shape((length, width), F32),
            shape((width, 3 * width), BF16),
            shape((width, width), BF16),
            shape((width, width), BF16),
            shape((width, width), BF16),
            shape((3, length, width), BF16),
            shape((8, width), F32),
        )
        params = pltpu.CompilerParams(vmem_limit_bytes=VMEM_LIMIT)
    else:
        outs = (
            shape((length, width), BF16),
            shape((rows, 3 * width), BF16),
            shape((rows, width), BF16),
            shape((rows, width), BF16),
            shape((rows, width), BF16),
            shape((8, width), F32),
        )
        params = pltpu.CompilerParams(collective_id=1, has_side_effects=True, vmem_limit_bytes=VMEM_LIMIT)
    buffer = pltpu.VMEM
    return pl.pallas_call(
        functools.partial(backward_kernel, count, alone),
        name="backward_layer",
        out_shape=outs,
        in_specs=[ANY] * 16 + [VM] * 3,
        out_specs=(ANY,) * (len(outs) - 1) + (VM,),
        scratch_shapes=[
            buffer((width, total), BF16),
            buffer((3, length, width), BF16),
            buffer((6, TILE, width), BF16),
            buffer((length, width), F32),
            buffer((length, width), F32),
            buffer((width, length), BF16),
            buffer((width, total), BF16),
            buffer((width, total), BF16),
            buffer((width, length), BF16),
            buffer((heads, 1, length), F32),
            buffer((total, length), F32),
            buffer((HEAD, length), F32),
            buffer((3, width, cols), BF16),
            buffer((3, width, cols), BF16),
            buffer((3, width, cols), BF16),
            buffer((3, 2, rows, cols), BF16),
            buffer((3, 2, rows, cols), BF16),
            buffer((8, 128), F32),
            buffer((length, width), BF16),
            buffer((length, width), BF16),
            buffer((length, width), BF16),
            buffer((bits + 3, 8, width), F32),
            buffer((bits + 2, 8, width), F32),
            pltpu.SemaphoreType.DMA((40,)),
            pltpu.SemaphoreType.DMA((192,)),
            pltpu.SemaphoreType.DMA((192,)),
            pltpu.SemaphoreType.REGULAR((2, 5 * (bits + 2))),
        ],
        compiler_params=params,
    )(*inputs)


def shifted(value, steps):
    count = lax.axis_size("shard")
    first, last = (max(0, -steps), min(count, count - steps))
    return lax.ppermute(value, "shard", [(source, source + steps) for source in range(first, last)])


def gather_plain(tokens, segs, vec, *weights):
    whole = tuple(lax.all_gather(weight, "shard", axis=0, tiled=True) for weight in weights)
    earlier = jnp.concatenate([shifted(tokens, 2), shifted(tokens, 1)])
    seg_ext = jnp.stack([shifted(segs, 2), shifted(segs, 1), segs])
    return (earlier, seg_ext, lax.all_gather(vec, "shard", axis=0)) + whole


def reduce_plain(qkv_grad, out_grad, up_grad, down_grad, grad_acted, small):
    owned = []
    for grad in (qkv_grad, out_grad, up_grad, down_grad):
        part = lax.psum_scatter(grad, "shard", scatter_dimension=0, tiled=True)
        owned.append(lax.psum(part, "rep").astype(F32))
    parts = [grad_acted[2], shifted(grad_acted[0], -2), shifted(grad_acted[1], -1)]
    return (*owned, sum(part.astype(F32) for part in parts), lax.psum(small, ("rep", "shard")))


def body(
    tokens,
    segments,
    cotangent,
    gain_one,
    qkv_weight,
    query_scale,
    out_weight,
    gain_two,
    up_weight,
    up_bias,
    down_weight,
    down_bias,
):
    count = lax.axis_size("shard")
    shard = lax.axis_index("shard")
    length, width = tokens.shape[1:]
    rows = qkv_weight.shape[0]
    heads = width // HEAD

    vec = jnp.stack([gain_one, gain_two, up_bias, down_bias])
    vec = jnp.pad(vec, ((0, 12), (0, -rows % 128)))
    segs = jnp.broadcast_to(segments, (8, length))
    whole_tiles = rows % 32 == 0 and count >= 4 and count & (count - 1) == 0 and lax.axis_size("rep") == 4
    factor = LOG2E / math.sqrt(HEAD) * jax.nn.softplus(query_scale)
    factor_row = jnp.tile(factor, heads)[None]
    weights = (qkv_weight, out_weight, up_weight, down_weight)
    earlier = None
    if not whole_tiles:
        earlier, segs, vec, *weights = gather_plain(tokens[0], segs, vec, *weights)
    output, acted_t, q_t, k_t, v_t, o_t, lse, hidden, inner_t, upper, lower_t, rows_in, qkv, out, up, down, mask = forward(
        count, tokens[0], earlier, segs, vec, factor_row * (1.0 / LN2), *weights
    )
    results = backward(
        count, not whole_tiles, cotangent[0], tokens[0], hidden, inner_t, upper, lower_t, o_t, q_t, k_t, v_t, acted_t,
        qkv, out, up, down, mask, lse, rows_in, factor[:, None],
    )
    if whole_tiles:
        input_grad, qkv_own, out_own, up_own, down_own, small_sum = results
        qkv_own, out_own, up_own, down_own = (part.astype(F32) for part in (qkv_own, out_own, up_own, down_own))
    else:
        grad_hidden, *partial = results
        qkv_own, out_own, up_own, down_own, grad_acted, small_sum = reduce_plain(*partial)
        state = tokens[0].astype(F32)
        inverse = lax.rsqrt(jnp.mean(state * state, axis=-1, keepdims=True) + EPS)
        normed = state * inverse
        weighted = grad_acted * rows_in[0:1]
        along = jnp.mean(weighted * normed, axis=-1, keepdims=True)
        input_grad = (grad_hidden + inverse * (weighted - normed * along)).astype(BF16)

    mine = lax.dynamic_slice_in_dim(small_sum[:4], shard * rows, rows, 1)
    scale_grad = (
        small_sum[4, :HEAD]
        * LN2
        / factor
        * (LOG2E / math.sqrt(HEAD))
        * jax.nn.sigmoid(query_scale)
    )
    return (
        output[None],
        input_grad[None],
        mine[0],
        qkv_own,
        scale_grad,
        out_own,
        mine[1],
        up_own,
        mine[2],
        down_own,
        mine[3],
    )


def solution(mesh):
    return jax.shard_map(
        body,
        mesh=mesh,
        in_specs=(
            P("rep", "shard", None),
            P("rep", "shard"),
            P("rep", "shard", None),
            P("shard"),
            P("shard", None),
            P(),
            P("shard", None),
            P("shard"),
            P("shard", None),
            P("shard"),
            P("shard", None),
            P("shard"),
        ),
        out_specs=(
            P("rep", "shard", None),
            P("rep", "shard", None),
            P("shard"),
            P("shard", None),
            P(),
            P("shard", None),
            P("shard"),
            P("shard", None),
            P("shard"),
            P("shard", None),
            P("shard"),
        ),
        check_vma=False,
    )
```

```python
import functools
import math

import jax
import jax.numpy as jnp
from jax import lax
from jax.experimental import pallas as pl
from jax.experimental.pallas import tpu as pltpu
from jax.sharding import PartitionSpec as P

HEAD = 80
WINDOW = 1024
EPS = 1e-06
LOG2E = 1.442695041
LN2 = math.log(2.0)
MASKED = -1e30
TILE = 256
MESH = pl.DeviceIdType.MESH
F32 = jnp.float32
BF16 = jnp.bfloat16
VMEM_LIMIT = 62 * 2**20
ANY = pl.BlockSpec(memory_space=pl.ANY)
VM = pl.BlockSpec(memory_space=pltpu.VMEM)


def mul(a, b, left=1, right=0):
    return lax.dot_general(a, b, (((left,), (right,)), ((), ())), preferred_element_type=F32)


def at(start, size, unit):
    return pl.ds(pl.multiple_of(start, unit), size)


def bit_of(index, bit):
    return lax.rem(lax.div(index, 1 << bit), 2)


def flip(index, mask):
    out = index
    bit = 0
    while mask >> bit:
        if (mask >> bit) & 1:
            out = out + (1 - 2 * bit_of(index, bit)) * (1 << bit)
        bit += 1
    return out


def span(bits):
    masks = [0]
    for bit in bits:
        masks = masks + [mask | (1 << bit) for mask in masks]
    return masks


def stage_orders(bits):
    rest = list(range(2, bits))
    return (["x", 0, 1] + rest, [0, 1, "x"] + rest, [1, "x", 0] + rest)


def cross_orders(bits):
    rest = list(range(2, bits))
    return (["x", 0, 1] + rest, ["x", 1, 0] + rest, ["x", 0, 1] + rest)


def greet(count):
    rep, shard = lax.axis_index("rep"), lax.axis_index("shard")
    barrier = pltpu.get_barrier_semaphore()
    for step in range(1, count):
        other = lax.rem(shard + step, count)
        pl.semaphore_signal(barrier, inc=1, device_id={"rep": rep, "shard": other}, device_id_type=MESH)
    for mask in (1, 2):
        pl.semaphore_signal(barrier, inc=1, device_id={"rep": flip(rep, mask), "shard": shard}, device_id_type=MESH)
    pl.semaphore_wait(barrier, count + 1)


class Sems:
    def __init__(self, send, recv):
        self.send, self.recv, self.used = send, recv, 0

    def slot(self):
        self.used += 1
        return self.used - 1

    def remote(self, src, dst, rep, shard, slot=None):
        slot = self.slot() if slot is None else slot
        return pltpu.make_async_remote_copy(
            src_ref=src,
            dst_ref=dst,
            send_sem=self.send.at[slot],
            recv_sem=self.recv.at[slot],
            device_id={"rep": rep, "shard": shard},
            device_id_type=MESH,
        )


class Doubling:
    def __init__(self, sems, count, rows, orders, parts):
        self.sems, self.rows, self.half, self.parts = sems, rows, rows // 2, parts
        bits = count.bit_length() - 1
        self.stages = bits + 1
        self.plan = []
        for order in orders:
            have, whole, stages = [], False, []
            for what in order[::-1]:
                masks = span(have)[1:] if what == "x" else span(have)
                stages.append([(what, mask, whole, sems.slot(), sems.slot()) for mask in masks])
                if what == "x":
                    whole = True
                else:
                    have.append(what)
            self.plan.append(stages)

    def copy(self, part, step):
        what, mask, whole, slot, _ = step
        rep, shard = lax.axis_index("rep"), lax.axis_index("shard")
        core, cross = lax.rem(rep, 2), lax.div(rep, 2)
        src, dst, first, cols = self.parts[part]
        across = at(first + core * cols, cols, 128)
        shift, size = (0, self.rows) if whole else (cross * self.half, self.half)
        row = flip(shard, mask) * self.rows + shift
        to = dst.at[at(row, size, 16), across]
        here = src.at[at(shift, size, 16), across] if mask == 0 else to
        if what == "x":
            return self.sems.remote(here, to, flip(rep, 2), shard, slot)
        return self.sems.remote(here, to, rep, flip(shard, 1 << what), slot)

    def ahead(self, part, step):
        what, mask, whole, _, slot = step
        rep, shard = lax.axis_index("rep"), lax.axis_index("shard")
        core, cross = lax.rem(rep, 2), lax.div(rep, 2)
        _, dst, first, cols = self.parts[part]
        if what == "x":
            row, size = flip(shard, mask) * self.rows + (1 - cross) * self.half, self.half
        else:
            shift, size = (0, self.rows) if whole else (cross * self.half, self.half)
            row = flip(shard, mask | (1 << what)) * self.rows + shift
        spot = dst.at[at(row, size, 16), at(first + core * cols, cols, 128)]
        return self.sems.remote(spot, spot, flip(rep, 1), shard, slot)

    def send(self, stage):
        for part in range(3):
            for step in self.plan[part][stage]:
                self.copy(part, step).start()

    def settle(self, stage):
        for part in range(3):
            for step in self.plan[part][stage]:
                self.copy(part, step).wait_recv()
                self.ahead(part, step).start()

    def move(self, stage):
        for part in range(3):
            for step in self.plan[part][stage]:
                self.copy(part, step).wait_recv()
            for step in self.plan[part][stage + 1]:
                self.copy(part, step).start()
            for step in self.plan[part][stage]:
                self.ahead(part, step).start()

    def finish(self):
        for part in range(3):
            for stage in self.plan[part]:
                for step in stage:
                    self.ahead(part, step).wait_recv()

    def drain(self):
        for part in range(3):
            for stage in self.plan[part]:
                for step in stage:
                    self.copy(part, step).wait_send()
                    self.ahead(part, step).wait_send()


def tail_orders(bits):
    rest = list(range(2, bits))
    cross = ["x", 0, 1] + rest
    return (cross, cross, ["x", 1, 0] + rest, [0, "x", 1] + rest, cross)


def beside_orders(bits):
    rest = list(range(2, bits))
    return (["x", 0, 1] + rest, [0, 1, "x"] + rest, [1, 0, "x"] + rest)


class Gathered:
    stages = 1

    def send(self, stage):
        pass

    settle = move = send

    def finish(self):
        pass

    drain = finish


def forward_kernel(count, *refs):
    (tokens, earlier, segs, vec, query_scale, w_qkv, w_out, w_up, w_down) = refs[:9]
    results = refs[9:26]
    alone = earlier is not None
    (
        output_hbm, acted_t_hbm, q_t_hbm, k_t_hbm, v_t_hbm, o_t_hbm, lse, hidden_hbm,
        inner_t_hbm, upper_hbm, lower_t_hbm, rows_out, qkv_hbm, out_hbm, up_hbm, down_hbm, mask_hbm,
    ) = results
    (
        seg_ext, vec_full, qkv, out, up, down, acted, acted_t, q_t, k_t, v_t, o_t, heads, inner,
        hidden, upper, inner_t, lower_t, mask, state_low, send, recv, lsem,
    ) = refs[26:]
    rep, shard = lax.axis_index("rep"), lax.axis_index("shard")
    length, width = tokens.shape
    total = 3 * length
    rows = w_qkv.shape[0]
    tiles = width // TILE
    own = pl.ds(total - length, length)
    sems = Sems(send, recv)
    lower, output = heads, inner
    bits = count.bit_length() - 1

    runs = [tiles * 2 // 5, tiles - tiles * 2 // 5]
    starts = [0, runs[0], tiles]
    wide_part = width // 5 // 128 * 128
    last_part = width // 2 - 2 * wide_part
    if alone:
        groups = [Gathered()] * 5
    else:
        groups = []
        for run, start in zip(runs, starts):
            parts = [(w_qkv, qkv, p * width + start * TILE, run * TILE // 2) for p in range(3)]
            groups.append(Doubling(sems, count, rows, stage_orders(bits) if start else cross_orders(bits), parts))
        for w, full in ((w_out, out), (w_up, up), (w_down, down)):
            parts = [(w, full, 0, wide_part), (w, full, 2 * wide_part, wide_part), (w, full, 4 * wide_part, last_part)]
            groups.append(Doubling(sems, count, rows, stage_orders(bits), parts))

    pairs = [(tokens, acted.at[own]), (tokens, state_low)]
    if alone:
        pairs += [(earlier, acted.at[pl.ds(0, 2 * length)]), (segs, seg_ext), (vec, vec_full)]
        pairs += [(w_qkv, qkv), (w_out, out), (w_up, up), (w_down, down)]
    else:
        mine = at(shard * rows, rows, 16)
        pairs += [(segs, seg_ext.at[2]), (vec, vec_full.at[shard])]
        pairs += [(w_qkv, qkv.at[mine]), (w_out, out.at[mine]), (w_up, up.at[mine]), (w_down, down.at[mine])]
    loads = [pltpu.make_async_copy(src, dst, lsem.at[i]) for i, (src, dst) in enumerate(pairs)]
    for copy in loads:
        copy.start()

    odd = lax.rem(shard, 2) == 1
    even = jnp.logical_not(odd)
    far_ok, far_got = shard < count - 2, shard >= 2
    buddy = flip(shard, 1)
    far_to = lax.rem(shard + 2, count)
    nchunk = 8
    part = length // nchunk
    far, near, relay, vecs = [], [], [], []
    for i in range(0 if alone else nchunk):
        here = pl.ds(i * part, part)
        far_spot, near_spot = acted.at[pl.ds(i * part, part)], acted.at[pl.ds(length + i * part, part)]
        slot = sems.slot()
        far.append(sems.remote(tokens.at[here], far_spot, rep, far_to, sems.slot()))
        near.append(sems.remote(tokens.at[here], near_spot, rep, buddy, slot))
        relay.append(sems.remote(far_spot, near_spot, rep, buddy, slot))
    if not alone:
        slot = sems.slot()
        far.append(sems.remote(segs, seg_ext.at[0], rep, far_to, sems.slot()))
        near.append(sems.remote(segs, seg_ext.at[1], rep, buddy, slot))
        relay.append(sems.remote(seg_ext.at[0], seg_ext.at[1], rep, buddy, slot))
        vecs = [
            sems.remote(vec, vec_full.at[shard], rep, lax.rem(shard + step, count), sems.slot()) for step in range(1, count)
        ]

    def far_start(*which):
        @pl.when(far_ok)
        def _():
            for i in which:
                far[i].start()

    def near_start(*which):
        @pl.when(even)
        def _():
            for i in which:
                near[i].start()

    def far_next(i):
        @pl.when(far_ok)
        def _():
            far[i].wait_send()
            far[i + 2].start()

    def near_next(i):
        @pl.when(even)
        def _():
            near[i].wait_send()
            near[i + 2].start()

    def relay_start(*which):
        @pl.when(far_got)
        def _():
            for i in which:
                far[i].wait_recv()

        @pl.when(odd & far_got)
        def _():
            for i in which:
                relay[i].start()

    if not alone:
        greet(count)
        groups[0].send(0)
        far_start(nchunk, 0, 1)
        near_start(nchunk, 0, 1)
        for copy in vecs:
            copy.start()
        groups[0].move(0)
        relay_start(nchunk)
        for i in range(nchunk):
            relay_start(i)
            if i + 2 < nchunk:
                far_next(i)
                near_next(i)
            if i == 0:
                groups[0].move(1)
            if i == 2:
                groups[0].move(2)
            if i == 6:
                groups[1].send(0)

    for copy in loads:
        copy.wait()
    for copy in vecs:
        copy.wait_recv()
    each = width // count
    lines = [jnp.concatenate([vec_full[i][j : j + 1, :] for j in range(-(-4 * each // 128))], axis=1) for i in range(count)]
    rows_out[...] = jnp.zeros_like(rows_out)
    for k in range(4):
        rows_out[k : k + 1, :] = jnp.concatenate([line[:, k * each : (k + 1) * each] for line in lines], axis=1)
    value = query_scale[...]
    soft = jnp.maximum(value, 0.0) + jnp.log(1.0 + jnp.exp(-jnp.abs(value)))
    rows_out[4:5, :] = jnp.concatenate([soft * (LOG2E / math.sqrt(HEAD) / LN2)] * (width // HEAD), axis=1)
    rows_out[5:6, 0:HEAD] = LN2 / (soft * (1.0 + jnp.exp(-value)))

    def norm_rows(i):
        sl = at(i * TILE, TILE, TILE)
        state = acted[sl, :].astype(F32)
        scale = lax.rsqrt(jnp.mean(state * state, axis=-1, keepdims=True) + EPS)
        value = (state * scale * rows_out[0:1, :]).astype(BF16)
        value = jnp.where(shard + i * TILE // length >= 2, value, jnp.zeros_like(value))
        acted[sl, :] = value
        acted_t[:, sl] = value.T

    def norm_step(i, carry):
        norm_rows(i)
        return carry

    per = length // TILE
    lax.fori_loop(2 * per, 3 * per, norm_step, 0)

    groups[0].settle(groups[0].stages - 1)
    groups[0].finish()

    def project_own(i, carry):
        sl = at(i * TILE, TILE, TILE)
        q_t[sl, :] = (mul(acted[own, :], qkv[:, sl]) * rows_out[4:5, sl]).astype(BF16).T
        k_t[sl, own] = mul(acted[own, :], qkv[:, at(width + i * TILE, TILE, TILE)]).astype(BF16).T
        v_t[sl, own] = mul(acted[own, :], qkv[:, at(2 * width + i * TILE, TILE, TILE)]).astype(BF16).T
        return carry

    def project_earlier(i, carry):
        sl = at(i * TILE, TILE, TILE)
        k_t[sl, before] = mul(acted[before, :], qkv[:, at(width + i * TILE, TILE, TILE)]).astype(BF16).T
        v_t[sl, before] = mul(acted[before, :], qkv[:, at(2 * width + i * TILE, TILE, TILE)]).astype(BF16).T
        return carry

    def project(i, carry):
        sl = at(i * TILE, TILE, TILE)
        q_t[sl, :] = (mul(acted[own, :], qkv[:, sl]) * rows_out[4:5, sl]).astype(BF16).T
        k_t[sl, :] = mul(acted[...], qkv[:, at(width + i * TILE, TILE, TILE)]).astype(BF16).T
        v_t[sl, :] = mul(acted[...], qkv[:, at(2 * width + i * TILE, TILE, TILE)]).astype(BF16).T
        return carry

    before = pl.ds(0, total - length)
    lax.fori_loop(0, runs[0], project_own, 0)
    if not alone:

        @pl.when(odd)
        def _():
            for copy in near:
                copy.wait_recv()

        @pl.when(even & far_got)
        def _():
            for copy in relay:
                copy.wait_recv()

        @pl.when(odd & far_got)
        def _():
            for copy in relay:
                copy.wait_send()

    groups[1].move(0)
    lax.fori_loop(0, 2 * per, norm_step, 0)

    mine = seg_ext[2].astype(F32)
    for j in range(3):
        column = jnp.broadcast_to(seg_ext[j].astype(F32), (8, length)).T[:, 0:1]
        column = jnp.where(shard + j >= 2, column, -1.0)
        place = lax.broadcasted_iota(jnp.int32, (length, length), 0) + j * length
        lane = lax.broadcasted_iota(jnp.int32, (length, length), 1)
        near_by = (place > lane) & (place <= lane + WINDOW)
        mask[j * length : (j + 1) * length, :] = jnp.where(near_by & (column == mine), 0.0, MASKED)

    groups[1].move(1)
    for group in groups[2:]:
        group.send(0)
    lax.fori_loop(0, runs[0], project_earlier, 0)
    groups[1].move(2)

    half = length // 2

    def attend(h):
        sl = at(h * HEAD, HEAD, 16)
        key, query = k_t[sl, :].T, q_t[sl, :]
        first, last = pl.ds(0, half), pl.ds(total - half, half)
        middle = pl.ds(half, total - length)
        score_m = mul(key[half : total - half], query) + mask[middle, :]
        score_f = mul(key[:half], query[:, :half]) + mask[first, :half]
        score_l = mul(key[total - half :], query[:, half:]) + mask[last, half:]
        ends = [jnp.max(score, axis=0, keepdims=True) for score in (score_f, score_l)]
        top = jnp.maximum(jnp.max(score_m, axis=0, keepdims=True), jnp.concatenate(ends, axis=1))
        prob_m = jnp.exp2(score_m - top)
        prob_f = jnp.exp2(score_f - top[:, :half])
        prob_l = jnp.exp2(score_l - top[:, half:])
        ends = [jnp.sum(prob, axis=0, keepdims=True) for prob in (prob_f, prob_l)]
        norm = jnp.sum(prob_m, axis=0, keepdims=True) + jnp.concatenate(ends, axis=1)
        ends = [mul(v_t[sl, first], prob_f.astype(BF16)), mul(v_t[sl, last], prob_l.astype(BF16))]
        mixed = mul(v_t[sl, middle], prob_m.astype(BF16)) + jnp.concatenate(ends, axis=1)
        o_t[sl, :] = (mixed * (1.0 / norm)).astype(BF16)
        lse[h] = top + jnp.log2(norm)

    pairs = [start * TILE // HEAD // 2 for start in starts]
    last = groups[0].stages - 1

    def steps(index, table):
        for number, actions in table.items():

            @pl.when(index == number)
            def _():
                for group, what in actions:
                    if what == "send":
                        groups[group].send(0)
                    elif what == "settle":
                        groups[group].settle(last)
                    else:
                        groups[group].move(what)

    def attend_run(first, stop, table):
        def attend_pair(pair, carry):
            attend(2 * pair)
            attend(2 * pair + 1)
            steps(pair, table)
            return carry

        lax.fori_loop(first, stop, attend_pair, 0)

    def project_run(first, stop, table):
        def project_step(i, carry):
            project(i, carry)
            steps(i, table)
            return carry

        lax.fori_loop(first, stop, project_step, 0)

    attend_run(0, pairs[1], {pairs[1] - 2: [(2, 0), (3, 0), (4, 0)], pairs[1] - 1: [(1, "settle")]})
    groups[1].finish()
    project_run(starts[1], starts[2], {starts[1]: [(2, 1), (3, 1), (4, 1)]})
    keep = [
        pltpu.make_async_copy(src, dst, lsem.at[8 + i])
        for i, (src, dst) in enumerate(((qkv, qkv_hbm), (acted_t, acted_t_hbm), (q_t, q_t_hbm), (k_t, k_t_hbm), (v_t, v_t_hbm), (mask, mask_hbm)))
    ]
    for copy in keep:
        copy.start()

    attend_run(
        pairs[1], pairs[2],
        {pairs[1]: [(2, 2), (3, 2)], pairs[2] - 2: [(2, "settle"), (4, 2)]},
    )

    def keep_more(*more):
        for src, dst in more:
            copy = pltpu.make_async_copy(src, dst, lsem.at[8 + len(keep)])
            copy.start()
            keep.append(copy)

    keep_more((o_t, o_t_hbm))

    def turn(i, carry):
        sl = at(i * TILE, TILE, TILE)
        heads[:, sl] = o_t[sl, :].T
        return carry

    lax.fori_loop(0, tiles, turn, 0)
    groups[2].finish()
    keep_more((out, out_hbm))

    def out_step(i, carry):
        sl = at(i * TILE, TILE, TILE)
        hidden[:, sl] = state_low[:, sl].astype(F32) + mul(heads[...], out[:, sl])
        return carry

    lax.fori_loop(0, tiles, out_step, 0)
    keep_more((hidden, hidden_hbm))

    def norm_two(i, carry):
        sl = at(i * TILE, TILE, TILE)
        value = hidden[sl, :]
        scale = lax.rsqrt(jnp.mean(value * value, axis=-1, keepdims=True) + EPS)
        normed = (value * scale * rows_out[1:2, :]).astype(BF16)
        inner[sl, :] = normed
        inner_t[:, sl] = normed.T
        return carry

    lax.fori_loop(0, length // TILE, norm_two, 0)
    keep_more((inner_t, inner_t_hbm))

    groups[3].settle(last)
    groups[3].finish()
    keep_more((up, up_hbm))

    def up_step(i, carry):
        sl = at(i * TILE, TILE, TILE)
        value = mul(inner[...], up[:, sl]) + rows_out[2:3, sl]
        upper[:, sl] = value
        act = (value / (1.0 + jnp.exp(-value))).astype(BF16)
        lower[:, sl] = act
        lower_t[sl, :] = act.T
        return carry

    lax.fori_loop(0, tiles, up_step, 0)
    keep_more((upper, upper_hbm), (lower_t, lower_t_hbm))

    groups[4].settle(last)
    groups[4].finish()
    keep_more((down, down_hbm))

    def down_step(i, carry):
        sl = at(i * TILE, TILE, TILE)
        output[:, sl] = (hidden[:, sl] + (mul(lower[...], down[:, sl]) + rows_out[3:4, sl])).astype(BF16)
        return carry

    lax.fori_loop(0, tiles, down_step, 0)
    keep_more((output, output_hbm))

    if not alone:

        @pl.when(far_ok)
        def _():
            for copy in far[nchunk - 2 :]:
                copy.wait_send()

        @pl.when(even)
        def _():
            for copy in near[nchunk - 2 :]:
                copy.wait_send()

    for copy in vecs:
        copy.wait_send()
    for group in groups:
        group.drain()
    for copy in keep:
        copy.wait()


def forward(count, tokens, earlier, segs, vec, query_scale, w_qkv, w_out, w_up, w_down):
    length, width = tokens.shape
    total = 3 * length
    heads = width // HEAD
    inputs = [x for x in (tokens, earlier, segs, vec, query_scale, w_qkv, w_out, w_up, w_down) if x is not None]
    if earlier is None:
        params = pltpu.CompilerParams(collective_id=0, has_side_effects=True, vmem_limit_bytes=VMEM_LIMIT)
    else:
        params = pltpu.CompilerParams(vmem_limit_bytes=VMEM_LIMIT)
    shape = jax.ShapeDtypeStruct
    outs = (
        shape((length, width), BF16),
        shape((width, total), BF16),
        shape((width, length), BF16),
        shape((width, total), BF16),
        shape((width, total), BF16),
        shape((width, length), BF16),
        shape((heads, 1, length), F32),
        shape((length, width), F32),
        shape((width, length), BF16),
        shape((length, width), F32),
        shape((width, length), BF16),
        shape((8, width), F32),
        shape((width, 3 * width), BF16),
        shape((width, width), BF16),
        shape((width, width), BF16),
        shape((width, width), BF16),
        shape((total, length), F32),
    )
    specs = [ANY] * 17
    specs[6] = specs[11] = VM
    buffer = pltpu.VMEM
    return pl.pallas_call(
        functools.partial(forward_kernel, count) if earlier is not None else lambda *refs: forward_kernel(count, refs[0], None, *refs[1:]),
        name="forward_layer",
        out_shape=outs,
        in_specs=[ANY] * (len(inputs) - 5) + [VM] + [ANY] * 4,
        out_specs=tuple(specs),
        scratch_shapes=[
            buffer((3,) + segs.shape[-2:], jnp.int32),
            buffer((count,) + vec.shape[-2:], F32),
            buffer((width, 3 * width), BF16),
            buffer((width, width), BF16),
            buffer((width, width), BF16),
            buffer((width, width), BF16),
            buffer((total, width), BF16),
            buffer((width, total), BF16),
            buffer((width, length), BF16),
            buffer((width, total), BF16),
            buffer((width, total), BF16),
            buffer((width, length), BF16),
            buffer((length, width), BF16),
            buffer((length, width), BF16),
            buffer((length, width), F32),
            buffer((length, width), F32),
            buffer((width, length), BF16),
            buffer((width, length), BF16),
            buffer((total, length), F32),
            buffer((length, width), BF16),
            pltpu.SemaphoreType.DMA((448,)),
            pltpu.SemaphoreType.DMA((448,)),
            pltpu.SemaphoreType.DMA((32,)),
        ],
        compiler_params=params,
    )(*inputs)


class Halving:
    def __init__(self, sems, credits, count, rows, orders, acc, other, land, result, reused):
        self.sems, self.credits, self.rows, self.half, self.reused = sems, credits, rows, rows // 2, reused
        self.acc, self.other, self.land, self.result = acc, other, land, result
        self.bits = count.bit_length() - 1
        self.plan, self.core_slot, self.cross_slot, self.share_slot = [], [], [], []
        self.at_stage = [0] * len(orders)
        for order in orders:
            left, whole, base, stages = list(range(self.bits)), True, 0, []
            for what in order:
                steps = []
                if what == "x":
                    whole = False
                else:
                    left.remove(what)
                for mask in span(left):
                    size = rows if whole else self.half
                    steps.append((mask, base, size, sems.slot()))
                    base += size
                stages.append((what, whole, steps))
            self.plan.append(stages)
            self.core_slot.append(sems.slot())
            self.cross_slot.append(sems.slot())
            self.share_slot.append(sems.slot())

    def partner(self, what):
        rep, shard = lax.axis_index("rep"), lax.axis_index("shard")
        if what == "core":
            return flip(rep, 1), shard
        if what == "x":
            return flip(rep, 2), shard
        return rep, flip(shard, 1 << what)

    def credit(self, part, what):
        place = 0 if what == "core" else 1 if what == "x" else 2 + what
        return self.credits.at[part * (self.bits + 2) + place]

    def allow(self, part, what):
        rep, shard = self.partner(what)
        pl.semaphore_signal(
            self.credit(part, what), inc=1, device_id={"rep": rep, "shard": shard}, device_id_type=MESH
        )

    def core_copy(self, part):
        return self.sems.remote(self.other[part], self.land[part], *self.partner("core"), self.core_slot[part])

    def core_send(self, part):
        if self.reused:
            pl.semaphore_wait(self.credit(part, "core"), 1)
        self.core_copy(part).start()

    def core_add(self, part):
        self.core_copy(part).wait_recv()
        acc, land = self.acc[part], self.land[part]

        def step(i, carry):
            sl = at(i * TILE, TILE, TILE)
            acc[sl, :] = (acc[sl, :].astype(F32) + land[sl, :].astype(F32)).astype(BF16)
            return carry

        lax.fori_loop(0, acc.shape[0] // TILE, step, 0)
        for what, _, _ in self.plan[part]:
            self.allow(part, what)
        self.send(part, 0)

    def copy(self, part, stage, step):
        what, whole, _ = self.plan[part][stage]
        mask, base, size, slot = step
        shard, cross = lax.axis_index("shard"), lax.div(lax.axis_index("rep"), 2)
        if what == "x":
            row = flip(shard, mask) * self.rows + (1 - cross) * self.half
        else:
            row = flip(shard, mask | (1 << what)) * self.rows
            row = row if whole else row + cross * self.half
        src = self.acc[part].at[at(row, size, 16)]
        return self.sems.remote(src, self.land[part].at[pl.ds(base, size)], *self.partner(what), slot)

    def send(self, part, stage):
        what, _, steps = self.plan[part][stage]
        pl.semaphore_wait(self.credit(part, what), 1)
        for step in steps:
            self.copy(part, stage, step).start()

    def receive(self, part, stage):
        what, whole, steps = self.plan[part][stage]
        shard, cross = lax.axis_index("shard"), lax.div(lax.axis_index("rep"), 2)
        for step in steps:
            mask, base, size, _ = step
            self.copy(part, stage, step).wait_recv()
            row = flip(shard, mask) * self.rows
            row = row if whole else row + cross * self.half
            sl = at(row, size, 16)
            new = self.acc[part][sl, :].astype(F32) + self.land[part][pl.ds(base, size), :].astype(F32)
            self.acc[part][sl, :] = new.astype(BF16)

    def advance(self, part):
        stage = self.at_stage[part]
        self.at_stage[part] += 1
        if stage <= self.bits:
            self.receive(part, stage)
        if stage < self.bits:
            self.send(part, stage + 1)
        elif stage == self.bits:
            core, cross = self.sides()
            shard = lax.axis_index("shard")
            row = shard * self.rows + cross * self.half
            self.result[part].at[core][at(cross * self.half, self.half, 16), :] = self.acc[part][at(row, self.half, 16), :]
            self.cross_copy(part).start()
        elif stage == self.bits + 1:
            self.cross_copy(part).wait_recv()
            self.share_copy(part).start()
        else:
            self.share_copy(part).wait_recv()

    def sides(self):
        rep = lax.axis_index("rep")
        return lax.rem(rep, 2), lax.div(rep, 2)

    def cross_copy(self, part):
        core, cross = self.sides()
        spot = self.result[part].at[core, at(cross * self.half, self.half, 16)]
        return self.sems.remote(spot, spot, *self.partner("x"), self.cross_slot[part])

    def share_copy(self, part):
        core, _ = self.sides()
        spot = self.result[part].at[core]
        return self.sems.remote(spot, spot, *self.partner("core"), self.share_slot[part])

    def drain_other(self, part):
        self.core_copy(part).wait_send()

    def drain_acc(self, part):
        for stage in range(self.bits + 1):
            for step in self.plan[part][stage][2]:
                self.copy(part, stage, step).wait_send()

    def drain_result(self, part):
        self.cross_copy(part).wait_send()
        self.share_copy(part).wait_send()


def backward_kernel(count, alone, *refs):
    (
        cot_hbm, tokens_hbm, hidden_hbm, inner_t_hbm, upper_hbm, lower_t_hbm, o_t_hbm, q_t_hbm, k_t_hbm, v_t_hbm,
        acted_t_hbm, qkv_hbm, out_hbm, up_hbm, down_hbm, mask_hbm, lse, rows_in,
    ) = refs[:18]
    if alone:
        (hidden_out, qkv_out, out_out, up_out, down_out, acted_out, small_out) = refs[18:25]
    else:
        (input_grad, qkv_out, out_out, up_out, down_out, small_out) = refs[18:24]
    scratch = refs[25:] if alone else refs[24:]
    (
        wide, flat, wtile, first_f32, grad_hidden, q_t, k_t, v_t, do_t, delta, mask, scale_sum, acc, other, land,
        result_ff, result_qkv, factor, near_in, far_in, state_low, small_now, small_in, lsem, send, recv, credits,
    ) = scratch
    rep, shard = lax.axis_index("rep"), lax.axis_index("shard")
    core = lax.rem(rep, 2)
    length, width = cot_hbm.shape
    total = 3 * length
    tiles = width // TILE
    rows = width // count
    cols = width // 2
    heads = width // HEAD
    own = pl.ds(total - length, length)
    bits = count.bit_length() - 1
    sems = Sems(send, recv)
    lower_t, inner_t, o_t = (wide.at[:, pl.ds(i * length, length)] for i in range(3))
    cot, grad_upper, grad_attn = (flat.at[i] for i in range(3))
    parts = [[ref.at[i] for i in range(3)] for ref in (acc, other, land, result_ff, result_qkv)]

    def local(src, dst, slot):
        return pltpu.make_async_copy(src, dst, lsem.at[slot])

    loads = {
        "cot": local(cot_hbm, cot, 0),
        "lower": local(lower_t_hbm, lower_t, 1),
        "upper": local(upper_hbm, first_f32, 2),
        "inner": local(inner_t_hbm, inner_t, 3),
        "o": local(o_t_hbm, o_t, 4),
        "q": local(q_t_hbm, q_t, 5),
        "k": local(k_t_hbm, k_t, 6),
        "v": local(v_t_hbm, v_t, 7),
        "mask": local(mask_hbm, mask, 8),
        "state": local(tokens_hbm, state_low, 9),
    }
    load_hidden = local(hidden_hbm, first_f32, 10)
    load_acted = local(acted_t_hbm, wide, 11)

    def tile_copy(src, order, i):
        slot = lax.rem(order * tiles + i, 6)
        return local(src.at[at(i * TILE, TILE, TILE)], wtile.at[slot], 12 + slot)

    def wide_copies(i):
        first = 3 * (i % 2)
        return [
            local(qkv_hbm.at[pl.ds(i * TILE, TILE), pl.ds(k * width, width)], wtile.at[first + k], 12 + first + k)
            for k in range(3)
        ]

    def tile_next(src, after, order, i):
        tile_copy(src, order, i).wait()
        if after is not None:
            tile_copy(after, order + 1, i).start()
        return lax.rem(order * tiles + i, 6)

    for name in ("lower", "cot"):
        loads[name].start()
    loads["upper"].start()
    for i in range(tiles):
        tile_copy(down_hbm, 0, i).start()
    for name in ("inner", "o"):
        loads[name].start()
    if alone:
        ff = qkv = None
    else:
        greet(count)
        ff = Halving(sems, credits.at[0], count, rows, beside_orders(bits), *parts[:4], False)
        cut = cols * 3 // 5 // 128 * 128
        runs = ((0, 0, cols), (1, 0, cut), (1, cut, cols - cut), (2, 0, cut), (2, cut, cols - cut))
        back = [[ref.at[2 - m, :, pl.ds(at_col, size)] for m, at_col, size in runs] for ref in (acc, other, land)]
        ends = [result_qkv.at[m, :, :, pl.ds(at_col, size)] for m, at_col, size in runs]
        qkv = Halving(sems, credits.at[1], count, rows, tail_orders(bits), *back, ends, True)
    copies_out = []

    def group_parts(first_use, part):
        return (part,) if first_use else ((0,), (1, 2), (3, 4))[part]

    def weight_side(group, part, left, right, side_core, first_use=False):
        theirs = side_core is not core
        dest = (other if theirs else acc).at[part if first_use else 2 - part]

        def step(i, carry):
            sl = at(i * cols, cols, 16)
            dest[sl, :] = right(left(sl), side_core * cols).astype(BF16)
            return carry

        lax.fori_loop(0, 2, step, 0)
        if theirs and group is not None:
            for run in group_parts(first_use, part):
                group.core_send(run)

    def weight_out(part, target, first, first_use=False):
        for ref, side_core in ((other, 1 - core), (acc, core)):
            copy = local(ref.at[part if first_use else 2 - part], target.at[:, at(first + side_core * cols, cols, 128)], 20 + len(copies_out))
            copy.start()
            copies_out.append(copy)

    def weight_grad(group, part, left, right, target):
        weight_side(group, part, left, right, 1 - core, True)
        weight_side(group, part, left, right, core, True)
        if alone:
            weight_out(part, target, 0, True)

    small_now[0] = jnp.zeros_like(small_now[0])
    loads["lower"].wait()
    loads["cot"].wait()
    weight_grad(
        ff, 2, lambda sl: lower_t[sl, :], lambda left, col: mul(left, cot[:, at(col, cols, 128)]), down_out
    )
    loads["upper"].wait()

    def down_step(i, carry):
        sl = at(i * TILE, TILE, TILE)
        slot = tile_next(down_hbm, up_hbm, 0, i)
        grad_lower = mul(cot[...], wtile[slot], 1, 1)
        value = first_f32[:, sl]
        gate = 1.0 / (1.0 + jnp.exp(-value))
        grad = (grad_lower * (gate + value * gate * (1.0 - gate))).astype(BF16)
        grad_upper[:, sl] = grad
        small_now[0, 2:3, sl] = jnp.sum(grad.astype(F32), axis=0, keepdims=True)
        small_now[0, 3:4, sl] = jnp.sum(cot[:, sl].astype(F32), axis=0, keepdims=True)
        return carry

    lax.fori_loop(0, tiles, down_step, 0)
    load_hidden.start()
    for name in ("q", "k", "v", "mask", "state"):
        loads[name].start()
    loads["inner"].wait()
    weight_grad(
        ff, 1, lambda sl: inner_t[sl, :], lambda left, col: mul(left, grad_upper[:, at(col, cols, 128)]), up_out
    )
    if not alone:
        ff.core_add(2)

    def up_step(i, carry):
        sl = at(i * TILE, TILE, TILE)
        slot = tile_next(up_hbm, out_hbm, 1, i)
        grad_hidden[:, sl] = mul(grad_upper[...], wtile[slot], 1, 1)
        return carry

    lax.fori_loop(0, tiles, up_step, 0)
    load_hidden.wait()
    if not alone:
        ff.core_add(1)

    def norm_step(i, carry):
        sl = at(i * TILE, TILE, TILE)
        value = first_f32[sl, :]
        scale = lax.rsqrt(jnp.mean(value * value, axis=-1, keepdims=True) + EPS)
        normed = value * scale
        grad = grad_hidden[sl, :]
        small_now[0, 1:2, :] += jnp.sum(grad * normed, axis=0, keepdims=True)
        weighted = grad * rows_in[1:2, :]
        along = jnp.mean(weighted * normed, axis=-1, keepdims=True)
        whole = cot[sl, :].astype(F32) + scale * (weighted - normed * along)
        grad_hidden[sl, :] = whole
        grad_attn[sl, :] = whole.astype(BF16)
        return carry

    lax.fori_loop(0, length // TILE, norm_step, 0)
    loads["o"].wait()
    weight_grad(
        ff, 0, lambda sl: o_t[sl, :], lambda left, col: mul(left, grad_attn[:, at(col, cols, 128)]), out_out
    )

    def out_step(i, carry):
        sl = at(i * TILE, TILE, TILE)
        slot = tile_next(out_hbm, None, 2, i)
        do_t[sl, :] = mul(grad_attn[...], wtile[slot], 1, 1).astype(BF16).T
        return carry

    lax.fori_loop(0, tiles, out_step, 0)
    if not alone:
        ff.core_add(0)

    def delta_step(h, carry):
        sl = at(h * HEAD, HEAD, 16)
        delta[h] = jnp.sum(o_t[sl, :].astype(F32) * do_t[sl, :].astype(F32), axis=0, keepdims=True)
        return carry

    lax.fori_loop(0, heads, delta_step, 0)
    load_acted.start()
    for i in range(2):
        for copy in wide_copies(i):
            copy.start()
    for name in ("q", "k", "v", "mask"):
        loads[name].wait()
    scale_sum[...] = jnp.zeros_like(scale_sum)
    factor[...] = jnp.broadcast_to(rows_in[4:5, 0:HEAD] * LN2, (128, HEAD)).T
    half = length // 2
    pieces = (
        (0, half, (0,)),
        (half, length, (0, 1)),
        (half + length, length, (0, 1)),
        (total - half, half, (1,)),
    )

    def attend(h, carry):
        sl = at(h * HEAD, HEAD, 16)
        query, grad = q_t[sl, :], do_t[sl, :]
        parts_dq = [jnp.zeros((HEAD, half), F32)] * 2
        for first, size, sides in pieces:
            ks, qs = pl.ds(first, size), slice(sides[0] * half, (sides[-1] + 1) * half)
            key, value = k_t[sl, ks], v_t[sl, ks]
            query_part, grad_part = query[:, qs], grad[:, qs]
            probs = jnp.exp2(mul(key.T, query_part) + mask[ks, qs] - lse[h][:, qs])
            scores = (probs * (mul(value.T, grad_part) - delta[h][:, qs])).astype(BF16)
            v_t[sl, ks] = mul(grad_part, probs.astype(BF16), 1, 1).astype(BF16)
            k_t[sl, ks] = (mul(query_part, scores, 1, 1) * LN2).astype(BF16)
            term = mul(key, scores)
            for place, side in enumerate(sides):
                parts_dq[side] = parts_dq[side] + term[:, place * half : (place + 1) * half]
        dq = jnp.concatenate(parts_dq, axis=1)
        scale_sum[...] += dq * query.astype(F32)
        q_t[sl, :] = (dq * factor[:, 0:1]).astype(BF16)
        if not alone:
            for head in sorted({step[0] for step in FF_STEPS}):

                @pl.when(h == head)
                def _():
                    for _, part, stage in [step for step in FF_STEPS if step[0] == head]:
                        ff.at_stage[part] = stage
                        ff.advance(part)
                        if stage == bits:
                            for run in group_parts(False, 2 - part):
                                qkv.allow(run, "core")

        return carry

    lax.fori_loop(0, heads, attend, 0)

    def give_result(group, part, target, first):
        for side in range(2):
            src = (result_ff if group is ff else result_qkv).at[part, side]
            copy = local(src, target.at[:, pl.ds(first + side * cols, cols)], 20 + len(copies_out))
            copy.start()
            copies_out.append(copy)

    load_acted.wait()
    odd = lax.rem(shard, 2) == 1
    even = jnp.logical_not(odd)
    far_ok, far_got = shard >= 2, shard < count - 2
    buddy = flip(shard, 1)
    far_to = lax.rem(shard + count - 2, count)
    give_slots = [sems.slot() for _ in range(tiles)]
    far_slots = [sems.slot() for _ in range(tiles)]

    def give(i):
        sl = pl.ds(i * TILE, TILE)
        return sems.remote(flat.at[1, :, sl], near_in.at[:, sl], rep, buddy, give_slots[i])

    def far(i):
        sl = pl.ds(i * TILE, TILE)
        return sems.remote(flat.at[0, :, sl], far_in.at[:, sl], rep, far_to, far_slots[i])

    def state_step(i):
        sl = pl.ds(i * TILE, TILE)
        for copy in wide_copies(i):
            copy.wait()
        slot = 3 * (i % 2)
        both = mul(wtile[slot + 1], k_t[...]) + mul(wtile[slot + 2], v_t[...])
        mine = both[:, total - length :] + mul(wtile[slot], q_t[...])
        both = jnp.concatenate([both[:, : total - length], mine], axis=1)
        low = both.astype(BF16)
        sums = jnp.sum(both * wide[sl, :].astype(F32), axis=1, keepdims=True)
        small_now[0, 0:1, sl] = jnp.broadcast_to(sums, (TILE, 128)).T[0:1, :] / rows_in[0:1, sl]
        for j in range(3):
            flat[j, :, sl] = low[:, j * length : (j + 1) * length].T
        if i + 2 < tiles:
            for copy in wide_copies(i + 2):
                copy.start()

    def give_start(i):
        @pl.when(odd | far_ok)
        def _():
            give(i).start()

    def far_start(i):
        @pl.when(even | far_ok)
        def _():
            give(i).wait_recv()

        @pl.when(odd & far_ok)
        def _():
            sl = pl.ds(i * TILE, TILE)
            flat[0, :, sl] = (flat[0, :, sl].astype(F32) + near_in[:, sl].astype(F32)).astype(BF16)

        @pl.when(far_ok)
        def _():
            far(i).start()

    if alone:
        for copy in copies_out:
            copy.wait()
    else:
        ff.at_stage = [max([step[2] + 1 for step in FF_STEPS if step[1] == part]) for part in range(3)]
        for part in (1, 2):
            ff.drain_other(part)
            ff.drain_acc(part)
    for side_core in (1 - core, core):
        weight_side(
            qkv, 0, lambda sl: wide[sl, own], lambda left, col: mul(left, q_t[at(col, cols, 16), :], 1, 1), side_core
        )
    for i in range(tiles):
        state_step(i)
        if alone:
            continue
        give_start(i)
        if i == 0:
            qkv.core_add(0)
            ff.advance(0)
        if i == 4:
            far_start(0)
    spread = jnp.sum(scale_sum[...], axis=1, keepdims=True)
    small_now[0, 4:5, 0:HEAD] = jnp.broadcast_to(spread, (HEAD, 128)).T[0:1, :]
    partners = ("core", "x") + tuple(range(bits))
    small_slots = [sems.slot() for _ in partners]

    def small_copy(number):
        return sems.remote(
            small_now.at[number], small_in.at[number], *ff.partner(partners[number]), small_slots[number]
        )

    def small_step(number):
        small_copy(number).wait()
        small_now[number + 1] = small_now[number] + small_in[number]
        if number + 1 < len(partners):
            small_copy(number + 1).start()

    if not alone:
        small_copy(0).start()
        ff.advance(0)
        for run in group_parts(False, 2):
            qkv.allow(run, "core")
        far_start(1)
    weight_side(qkv, 1, lambda sl: wide[sl, :], lambda left, col: mul(left, k_t[at(col, cols, 16), :], 1, 1), 1 - core)
    if not alone:
        far_start(2)
        small_step(0)
    weight_side(qkv, 1, lambda sl: wide[sl, :], lambda left, col: mul(left, k_t[at(col, cols, 16), :], 1, 1), core)
    if not alone:
        ff.drain_other(0)
        ff.drain_acc(0)
        qkv.core_add(1)
        qkv.core_add(2)
        qkv.advance(0)
        far_start(3)
        small_step(1)
    weight_side(qkv, 2, lambda sl: wide[sl, :], lambda left, col: mul(left, v_t[at(col, cols, 16), :], 1, 1), 1 - core)
    if not alone:
        far_start(4)
    weight_side(qkv, 2, lambda sl: wide[sl, :], lambda left, col: mul(left, v_t[at(col, cols, 16), :], 1, 1), core)
    if alone:
        for part in range(3):
            weight_out(part, qkv_out, part * width)
    if alone:
        small_out[...] = small_now[0]
        tail = [local(grad_hidden, hidden_out, 18), local(flat, acted_out, 19)]
        for copy in tail:
            copy.start()
        loads["state"].wait()
        for copy in tail + copies_out[6:]:
            copy.wait()
        return

    qkv.core_add(3)
    qkv.core_add(4)
    small_step(2)

    def round_robin(*order):
        for part in order:
            qkv.advance(part)

    round_robin(0, 2, 1)
    round_robin(4, 3)
    ff.advance(0)
    for part, target in enumerate((out_out, up_out, down_out)):
        ff.advance(part)
        give_result(ff, part, target, 0)
    small_step(3)
    round_robin(0, 2, 1)
    round_robin(4, 3)

    loads["state"].wait()
    for i in range(tiles):

        @pl.when(far_got)
        def _():
            far(i).wait_recv()


    def final_step(i, carry):
        sl = at(i * 128, 128, 128)
        state = state_low[sl, :].astype(F32)
        inverse = lax.rsqrt(jnp.mean(state * state, axis=-1, keepdims=True) + EPS)
        normed = state * inverse
        grad = flat[2, sl, :].astype(F32)
        grad += jnp.where(even, near_in[sl, :].astype(F32), 0.0)
        grad += jnp.where(far_got, far_in[sl, :].astype(F32), 0.0)
        weighted = grad * rows_in[0:1, :]
        along = jnp.mean(weighted * normed, axis=-1, keepdims=True)
        state_low[sl, :] = (grad_hidden[sl, :] + inverse * (weighted - normed * along)).astype(BF16)
        return carry

    lax.fori_loop(0, length // 128, final_step, 0)
    write = local(state_low, input_grad, 18)
    write.start()
    for number in range(4, len(partners)):
        small_step(number)
    last = len(partners)
    small_out[...] = jnp.zeros_like(small_out)
    for place in range(count):

        @pl.when(shard == place)
        def _():
            small_out[0:4, 0:rows] = small_now[last, 0:4, place * rows : (place + 1) * rows]

    small_out[4:5, 0:HEAD] = small_now[last, 4:5, 0:HEAD] * rows_in[5:6, 0:HEAD]
    while min(qkv.at_stage) <= bits + 2:
        round_robin(*[part for part in (0, 2, 1, 4, 3) if qkv.at_stage[part] <= bits + 2])
    for part in range(3):
        give_result(qkv, part, qkv_out, part * width)

    for i in range(tiles):

        @pl.when(odd | far_ok)
        def _():
            give(i).wait_send()

        @pl.when(far_ok)
        def _():
            far(i).wait_send()

    for part in range(5):
        qkv.drain_other(part)
        qkv.drain_acc(part)
        qkv.drain_result(part)
    for part in range(3):
        ff.drain_result(part)
    for copy in copies_out:
        copy.wait()
    write.wait()


FF_STEPS = (
    (2, 2, 0), (4, 1, 0), (7, 2, 1), (8, 1, 1), (9, 2, 2), (10, 0, 0),
    (11, 1, 2), (12, 2, 3), (13, 1, 3), (14, 0, 1), (15, 2, 4), (15, 1, 4),
)


def backward(count, alone, *inputs):
    length, width = inputs[0].shape
    total = 3 * length
    rows = width // count
    cols = width // 2
    heads = width // HEAD
    bits = count.bit_length() - 1
    shape = jax.ShapeDtypeStruct
    if alone:
        outs = (
            shape((length, width), F32),
            shape((width, 3 * width), BF16),
            shape((width, width), BF16),
            shape((width, width), BF16),
            shape((width, width), BF16),
            shape((3, length, width), BF16),
            shape((8, width), F32),
        )
        params = pltpu.CompilerParams(vmem_limit_bytes=VMEM_LIMIT)
    else:
        outs = (
            shape((length, width), BF16),
            shape((rows, 3 * width), BF16),
            shape((rows, width), BF16),
            shape((rows, width), BF16),
            shape((rows, width), BF16),
            shape((8, 256), F32),
        )
        params = pltpu.CompilerParams(collective_id=1, has_side_effects=True, vmem_limit_bytes=VMEM_LIMIT)
    buffer = pltpu.VMEM
    return pl.pallas_call(
        functools.partial(backward_kernel, count, alone),
        name="backward_layer",
        out_shape=outs,
        in_specs=[ANY] * 16 + [VM] * 2,
        out_specs=(ANY,) * (len(outs) - 1) + (VM,),
        scratch_shapes=[
            buffer((width, total), BF16),
            buffer((3, length, width), BF16),
            buffer((6, TILE, width), BF16),
            buffer((length, width), F32),
            buffer((length, width), F32),
            buffer((width, length), BF16),
            buffer((width, total), BF16),
            buffer((width, total), BF16),
            buffer((width, length), BF16),
            buffer((heads, 1, length), F32),
            buffer((total, length), F32),
            buffer((HEAD, length), F32),
            buffer((3, width, cols), BF16),
            buffer((3, width, cols), BF16),
            buffer((3, width, cols), BF16),
            buffer((3, 2, rows, cols), BF16),
            buffer((3, 2, rows, cols), BF16),
            buffer((HEAD, 128), F32),
            buffer((length, width), BF16),
            buffer((length, width), BF16),
            buffer((length, width), BF16),
            buffer((bits + 3, 8, width), F32),
            buffer((bits + 2, 8, width), F32),
            pltpu.SemaphoreType.DMA((40,)),
            pltpu.SemaphoreType.DMA((192,)),
            pltpu.SemaphoreType.DMA((192,)),
            pltpu.SemaphoreType.REGULAR((2, 5 * (bits + 2))),
        ],
        compiler_params=params,
    )(*inputs)


def finish_kernel(*refs):
    small = refs[6]
    for src, dst in zip(refs[:6], refs[7:13]):
        dst[...] = src[...].astype(dst.dtype)
    for row, dst in enumerate(refs[13:]):
        dst[...] = small[row, 0 : dst.shape[0]]


def finish(small, *arrays):
    shape = jax.ShapeDtypeStruct
    outs = [shape(array.shape, F32 if place < 4 else array.dtype) for place, array in enumerate(arrays)]
    specs = [pl.BlockSpec((array.shape[0] // 2, array.shape[1]), lambda i: (i, 0)) for array in arrays]
    lines = [arrays[0].shape[0]] * 4 + [HEAD]
    outs += [shape((line,), F32) for line in lines]
    line_specs = [pl.BlockSpec((line,), lambda i: (0,)) for line in lines]
    return pl.pallas_call(
        finish_kernel,
        name="finish",
        grid=(2,),
        out_shape=tuple(outs),
        in_specs=specs + [pl.BlockSpec(small.shape, lambda i: (0, 0))],
        out_specs=tuple(specs + line_specs),
        compiler_params=pltpu.CompilerParams(vmem_limit_bytes=VMEM_LIMIT),
    )(*arrays, small)


def shifted(value, steps):
    count = lax.axis_size("shard")
    first, last = (max(0, -steps), min(count, count - steps))
    return lax.ppermute(value, "shard", [(source, source + steps) for source in range(first, last)])


def gather_plain(tokens, segs, vec, *weights):
    whole = tuple(lax.all_gather(weight, "shard", axis=0, tiled=True) for weight in weights)
    earlier = jnp.concatenate([shifted(tokens, 2), shifted(tokens, 1)])
    seg_ext = jnp.stack([shifted(segs, 2), shifted(segs, 1), segs])
    return (earlier, seg_ext, lax.all_gather(vec, "shard", axis=0)) + whole


def reduce_plain(qkv_grad, out_grad, up_grad, down_grad, grad_acted, small):
    owned = []
    for grad in (qkv_grad, out_grad, up_grad, down_grad):
        part = lax.psum_scatter(grad, "shard", scatter_dimension=0, tiled=True)
        owned.append(lax.psum(part, "rep").astype(F32))
    parts = [grad_acted[2], shifted(grad_acted[0], -2), shifted(grad_acted[1], -1)]
    return (*owned, sum(part.astype(F32) for part in parts), lax.psum(small, ("rep", "shard")))


def body(
    tokens,
    segments,
    cotangent,
    gain_one,
    qkv_weight,
    query_scale,
    out_weight,
    gain_two,
    up_weight,
    up_bias,
    down_weight,
    down_bias,
):
    count = lax.axis_size("shard")
    shard = lax.axis_index("shard")
    length, width = tokens.shape[1:]
    rows = qkv_weight.shape[0]

    vec = jnp.concatenate([gain_one, gain_two, up_bias, down_bias]).astype(F32)
    vec = jnp.pad(vec, (0, -vec.shape[0] % 1024)).reshape(-1, 128)
    segs = segments
    whole_tiles = rows % 32 == 0 and count >= 4 and count & (count - 1) == 0 and lax.axis_size("rep") == 4
    weights = (qkv_weight, out_weight, up_weight, down_weight)
    earlier = None
    if not whole_tiles:
        earlier, segs, vec, *weights = gather_plain(tokens[0], segs, vec, *weights)
    output, acted_t, q_t, k_t, v_t, o_t, lse, hidden, inner_t, upper, lower_t, rows_in, qkv, out, up, down, mask = forward(
        count, tokens[0], earlier, segs, vec, query_scale[None], *weights
    )
    results = backward(
        count, not whole_tiles, cotangent[0], tokens[0], hidden, inner_t, upper, lower_t, o_t, q_t, k_t, v_t, acted_t,
        qkv, out, up, down, mask, lse, rows_in,
    )
    if whole_tiles:
        qkv_own, out_own, up_own, down_own, output, input_grad, *vectors = finish(
            results[5], *results[1:5], output, results[0]
        )
    else:
        grad_hidden, *partial = results
        qkv_own, out_own, up_own, down_own, grad_acted, small = reduce_plain(*partial)
        state = tokens[0].astype(F32)
        inverse = lax.rsqrt(jnp.mean(state * state, axis=-1, keepdims=True) + EPS)
        normed = state * inverse
        weighted = grad_acted * rows_in[0:1]
        along = jnp.mean(weighted * normed, axis=-1, keepdims=True)
        input_grad = (grad_hidden + inverse * (weighted - normed * along)).astype(BF16)
        mine = lax.dynamic_slice_in_dim(small[:4], shard * rows, rows, 1)
        vectors = [*mine, small[4, :HEAD] * rows_in[5, :HEAD]]

    return (
        output[None],
        input_grad[None],
        vectors[0],
        qkv_own,
        vectors[4],
        out_own,
        vectors[1],
        up_own,
        vectors[2],
        down_own,
        vectors[3],
    )


def solution(mesh):
    return jax.shard_map(
        body,
        mesh=mesh,
        in_specs=(
            P("rep", "shard", None),
            P("rep", "shard"),
            P("rep", "shard", None),
            P("shard"),
            P("shard", None),
            P(),
            P("shard", None),
            P("shard"),
            P("shard", None),
            P("shard"),
            P("shard", None),
            P("shard"),
        ),
        out_specs=(
            P("rep", "shard", None),
            P("rep", "shard", None),
            P("shard"),
            P("shard", None),
            P(),
            P("shard", None),
            P("shard"),
            P("shard", None),
            P("shard"),
            P("shard", None),
            P("shard"),
        ),
        check_vma=False,
    )
```

```python
import functools
import math

import jax
import jax.numpy as jnp
from jax import lax
from jax.experimental import pallas as pl
from jax.experimental.pallas import tpu as pltpu
from jax.sharding import PartitionSpec as P

HEAD = 80
WINDOW = 1024
EPS = 1e-06
LOG2E = 1.442695041
LN2 = math.log(2.0)
MASKED = -1e30
TILE = 256
MESH = pl.DeviceIdType.MESH
F32 = jnp.float32
BF16 = jnp.bfloat16
VMEM_LIMIT = 62 * 2**20
HALO_CHUNKS = 8
ANY = pl.BlockSpec(memory_space=pl.ANY)
VM = pl.BlockSpec(memory_space=pltpu.VMEM)


def mul(a, b, left=1, right=0):
    return lax.dot_general(a, b, (((left,), (right,)), ((), ())), preferred_element_type=F32)


def at(start, size, unit):
    return pl.ds(pl.multiple_of(start, unit), size)


def bit_of(index, bit):
    return lax.rem(lax.div(index, 1 << bit), 2)


def flip(index, mask):
    out = index
    bit = 0
    while mask >> bit:
        if (mask >> bit) & 1:
            out = out + (1 - 2 * bit_of(index, bit)) * (1 << bit)
        bit += 1
    return out


def span(bits):
    masks = [0]
    for bit in bits:
        masks = masks + [mask | (1 << bit) for mask in masks]
    return masks


def stage_orders(bits):
    rest = list(range(2, bits))
    return (["x", 0, 1] + rest, [0, 1, "x"] + rest, [1, "x", 0] + rest)


def cross_orders(bits):
    rest = list(range(2, bits))
    return (["x", 0, 1] + rest, ["x", 1, 0] + rest, ["x", 0, 1] + rest)


def greet(count):
    rep, shard = lax.axis_index("rep"), lax.axis_index("shard")
    barrier = pltpu.get_barrier_semaphore()
    for step in range(1, count):
        other = lax.rem(shard + step, count)
        pl.semaphore_signal(barrier, inc=1, device_id={"rep": rep, "shard": other}, device_id_type=MESH)
    for mask in (1, 2):
        pl.semaphore_signal(barrier, inc=1, device_id={"rep": flip(rep, mask), "shard": shard}, device_id_type=MESH)
    pl.semaphore_wait(barrier, count + 1)


class Sems:
    def __init__(self, send, recv):
        self.send, self.recv, self.sends, self.recvs = send, recv, 0, 0

    def send_slot(self):
        self.sends += 1
        return self.sends - 1

    def recv_slot(self):
        self.recvs += 1
        return self.recvs - 1

    def slot(self):
        return self.send_slot(), self.recv_slot()

    def remote(self, src, dst, rep, shard, slot):
        return pltpu.make_async_remote_copy(
            src_ref=src,
            dst_ref=dst,
            send_sem=self.send.at[slot[0]],
            recv_sem=self.recv.at[slot[1]],
            device_id={"rep": rep, "shard": shard},
            device_id_type=MESH,
        )


class Doubling:
    def __init__(self, sems, count, rows, orders, parts):
        self.sems, self.rows, self.half, self.parts = sems, rows, rows // 2, parts
        bits = count.bit_length() - 1
        self.stages = bits + 1
        self.plan = []
        for order in orders:
            have, whole, stages = [], False, []
            for what in order[::-1]:
                masks = span(have)[1:] if what == "x" else span(have)
                stages.append([(what, mask, whole, len(stages)) for mask in masks])
                if what == "x":
                    whole = True
                else:
                    have.append(what)
            self.plan.append(stages)
        self.copy_send = [sems.send_slot() for _ in orders]
        self.stage_recv = [[sems.recv_slot() for _ in range(self.stages)] for _ in orders]
        self.ahead_slot = [sems.slot() for _ in orders]

    def copy(self, part, step):
        what, mask, whole, stage = step
        rep, shard = lax.axis_index("rep"), lax.axis_index("shard")
        core, cross = lax.rem(rep, 2), lax.div(rep, 2)
        src, dst, first, cols = self.parts[part]
        across = at(first + core * cols, cols, 128)
        shift, size = (0, self.rows) if whole else (cross * self.half, self.half)
        row = flip(shard, mask) * self.rows + shift
        to = dst.at[at(row, size, 16), across]
        here = src.at[at(shift, size, 16), across] if mask == 0 else to
        slot = self.copy_send[part], self.stage_recv[part][stage]
        if what == "x":
            return self.sems.remote(here, to, flip(rep, 2), shard, slot)
        return self.sems.remote(here, to, rep, flip(shard, 1 << what), slot)

    def ahead(self, part, step):
        what, mask, whole, _ = step
        rep, shard = lax.axis_index("rep"), lax.axis_index("shard")
        core, cross = lax.rem(rep, 2), lax.div(rep, 2)
        _, dst, first, cols = self.parts[part]
        if what == "x":
            row, size = flip(shard, mask) * self.rows + (1 - cross) * self.half, self.half
        else:
            shift, size = (0, self.rows) if whole else (cross * self.half, self.half)
            row = flip(shard, mask | (1 << what)) * self.rows + shift
        spot = dst.at[at(row, size, 16), at(first + core * cols, cols, 128)]
        return self.sems.remote(spot, spot, flip(rep, 1), shard, self.ahead_slot[part])

    def together(self, part, stages, slot):
        rep, shard = lax.axis_index("rep"), lax.axis_index("shard")
        _, dst, first, cols = self.parts[part]
        size = sum(self.rows if step[2] else self.half for stage in stages for step in self.plan[part][stage])
        spot = dst.at[pl.ds(0, size), at(first + lax.rem(rep, 2) * cols, cols, 128)]
        return self.sems.remote(spot, spot, flip(rep, 1), shard, slot)

    def arrive(self, part, stage):
        self.together(part, [stage], (self.copy_send[part], self.stage_recv[part][stage])).wait_recv()

    def send(self, stage):
        for part in range(3):
            for step in self.plan[part][stage]:
                self.copy(part, step).start()

    def settle(self, stage):
        for part in range(3):
            self.arrive(part, stage)
            for step in self.plan[part][stage]:
                self.ahead(part, step).start()

    def move(self, stage):
        for part in range(3):
            self.arrive(part, stage)
            for step in self.plan[part][stage + 1]:
                self.copy(part, step).start()
            for step in self.plan[part][stage]:
                self.ahead(part, step).start()

    def finish(self):
        for part in range(3):
            self.together(part, range(self.stages), self.ahead_slot[part]).wait_recv()

    def drain(self):
        for part in range(3):
            slot = self.copy_send[part], self.stage_recv[part][0]
            self.together(part, range(self.stages), slot).wait_send()
            self.together(part, range(self.stages), self.ahead_slot[part]).wait_send()


def tail_orders(bits):
    rest = list(range(2, bits))
    cross = ["x", 0, 1] + rest
    return (cross, cross, ["x", 1, 0] + rest, [0, "x", 1] + rest, cross)


def beside_orders(bits):
    rest = list(range(2, bits))
    return (["x", 0, 1] + rest, [0, 1, "x"] + rest, [1, 0, "x"] + rest)


class Gathered:
    stages = 1

    def send(self, stage):
        pass

    settle = move = send

    def finish(self):
        pass

    drain = finish


def forward_kernel(count, *refs):
    (tokens, earlier, segs, vec, query_scale, w_qkv, w_out, w_up, w_down) = refs[:9]
    results = refs[9:26]
    alone = earlier is not None
    (
        output_hbm, acted_t_hbm, q_t_hbm, k_t_hbm, v_t_hbm, o_t_hbm, lse, hidden_hbm,
        inner_t_hbm, upper_hbm, lower_t_hbm, rows_out, qkv_hbm, out_hbm, up_hbm, down_hbm, mask_hbm,
    ) = results
    (
        seg_ext, vec_full, qkv, out, up, down, acted, acted_t, q_t, k_t, v_t, o_t, heads, inner,
        hidden, upper, inner_t, lower_t, mask, state_low, send, recv, lsem,
    ) = refs[26:]
    rep, shard = lax.axis_index("rep"), lax.axis_index("shard")
    length, width = tokens.shape
    total = 3 * length
    rows = w_qkv.shape[0]
    tiles = width // TILE
    own = pl.ds(total - length, length)
    sems = Sems(send, recv)
    lower, output = heads, inner
    bits = count.bit_length() - 1

    runs = [tiles * 2 // 5, tiles - tiles * 2 // 5]
    starts = [0, runs[0], tiles]
    wide_part = width // 5 // 128 * 128
    last_part = width // 2 - 2 * wide_part
    if alone:
        groups = [Gathered()] * 5
    else:
        groups = []
        for run, start in zip(runs, starts):
            parts = [(w_qkv, qkv, p * width + start * TILE, run * TILE // 2) for p in range(3)]
            groups.append(Doubling(sems, count, rows, stage_orders(bits) if start else cross_orders(bits), parts))
        for w, full in ((w_out, out), (w_up, up), (w_down, down)):
            parts = [(w, full, 0, wide_part), (w, full, 2 * wide_part, wide_part), (w, full, 4 * wide_part, last_part)]
            groups.append(Doubling(sems, count, rows, stage_orders(bits), parts))

    pairs = [(tokens, acted.at[own]), (tokens, state_low)]
    if alone:
        pairs += [(earlier, acted.at[pl.ds(0, 2 * length)]), (segs, seg_ext), (vec, vec_full)]
        pairs += [(w_qkv, qkv), (w_out, out), (w_up, up), (w_down, down)]
    else:
        mine = at(shard * rows, rows, 16)
        pairs += [(segs, seg_ext.at[2]), (vec, vec_full.at[shard])]
        pairs += [(w_qkv, qkv.at[mine]), (w_out, out.at[mine]), (w_up, up.at[mine]), (w_down, down.at[mine])]
    loads = [pltpu.make_async_copy(src, dst, lsem.at[i]) for i, (src, dst) in enumerate(pairs)]
    for copy in loads:
        copy.start()

    odd = lax.rem(shard, 2) == 1
    even = jnp.logical_not(odd)
    far_ok, far_got = shard < count - 2, shard >= 2
    buddy = flip(shard, 1)
    far_to = lax.rem(shard + 2, count)
    nchunk = HALO_CHUNKS
    part = length // nchunk
    far, near, relay, vecs = [], [], [], []
    for i in range(0 if alone else nchunk):
        here = pl.ds(i * part, part)
        far_spot, near_spot = acted.at[pl.ds(i * part, part)], acted.at[pl.ds(length + i * part, part)]
        slot = sems.slot()
        far.append(sems.remote(tokens.at[here], far_spot, rep, far_to, sems.slot()))
        near.append(sems.remote(tokens.at[here], near_spot, rep, buddy, slot))
        relay.append(sems.remote(far_spot, near_spot, rep, buddy, slot))
    if not alone:
        slot = sems.slot()
        far.append(sems.remote(segs, seg_ext.at[0], rep, far_to, sems.slot()))
        near.append(sems.remote(segs, seg_ext.at[1], rep, buddy, slot))
        relay.append(sems.remote(seg_ext.at[0], seg_ext.at[1], rep, buddy, slot))
        vecs = [
            sems.remote(vec, vec_full.at[shard], rep, lax.rem(shard + step, count), sems.slot()) for step in range(1, count)
        ]

    def far_start(*which):
        @pl.when(far_ok)
        def _():
            for i in which:
                far[i].start()

    def near_start(*which):
        @pl.when(even)
        def _():
            for i in which:
                near[i].start()

    def far_next(i):
        @pl.when(far_ok)
        def _():
            far[i].wait_send()
            far[i + 2].start()

    def near_next(i):
        @pl.when(even)
        def _():
            near[i].wait_send()
            near[i + 2].start()

    def relay_start(*which):
        @pl.when(far_got)
        def _():
            for i in which:
                far[i].wait_recv()

        @pl.when(odd & far_got)
        def _():
            for i in which:
                relay[i].start()

    if not alone:
        greet(count)
        groups[0].send(0)
        far_start(nchunk, 0, 1)
        near_start(nchunk, 0, 1)
        for copy in vecs:
            copy.start()
        groups[0].move(0)
        relay_start(nchunk)
        for i in range(nchunk):
            relay_start(i)
            if i + 2 < nchunk:
                far_next(i)
                near_next(i)
            if i == 0:
                groups[0].move(1)
            if i == 2:
                groups[0].move(2)
            if i == 6:
                groups[1].send(0)

    for copy in loads:
        copy.wait()
    for copy in vecs:
        copy.wait_recv()
    each = width // count
    lines = [jnp.concatenate([vec_full[i][j : j + 1, :] for j in range(-(-4 * each // 128))], axis=1) for i in range(count)]
    rows_out[...] = jnp.zeros_like(rows_out)
    for k in range(4):
        rows_out[k : k + 1, :] = jnp.concatenate([line[:, k * each : (k + 1) * each] for line in lines], axis=1)
    value = query_scale[...]
    soft = jnp.maximum(value, 0.0) + jnp.log(1.0 + jnp.exp(-jnp.abs(value)))
    rows_out[4:5, :] = jnp.concatenate([soft * (LOG2E / math.sqrt(HEAD) / LN2)] * (width // HEAD), axis=1)
    rows_out[5:6, 0:HEAD] = LN2 / (soft * (1.0 + jnp.exp(-value)))

    def norm_rows(i):
        sl = at(i * TILE, TILE, TILE)
        state = acted[sl, :].astype(F32)
        scale = lax.rsqrt(jnp.mean(state * state, axis=-1, keepdims=True) + EPS)
        value = (state * scale * rows_out[0:1, :]).astype(BF16)
        value = jnp.where(shard + i * TILE // length >= 2, value, jnp.zeros_like(value))
        acted[sl, :] = value
        acted_t[:, sl] = value.T

    def norm_step(i, carry):
        norm_rows(i)
        return carry

    per = length // TILE
    lax.fori_loop(2 * per, 3 * per, norm_step, 0)

    groups[0].settle(groups[0].stages - 1)
    groups[0].finish()

    def project_own(i, carry):
        sl = at(i * TILE, TILE, TILE)
        q_t[sl, :] = (mul(acted[own, :], qkv[:, sl]) * rows_out[4:5, sl]).astype(BF16).T
        k_t[sl, own] = mul(acted[own, :], qkv[:, at(width + i * TILE, TILE, TILE)]).astype(BF16).T
        v_t[sl, own] = mul(acted[own, :], qkv[:, at(2 * width + i * TILE, TILE, TILE)]).astype(BF16).T
        return carry

    def project_earlier(i, carry):
        sl = at(i * TILE, TILE, TILE)
        k_t[sl, before] = mul(acted[before, :], qkv[:, at(width + i * TILE, TILE, TILE)]).astype(BF16).T
        v_t[sl, before] = mul(acted[before, :], qkv[:, at(2 * width + i * TILE, TILE, TILE)]).astype(BF16).T
        return carry

    def project(i, carry):
        sl = at(i * TILE, TILE, TILE)
        q_t[sl, :] = (mul(acted[own, :], qkv[:, sl]) * rows_out[4:5, sl]).astype(BF16).T
        k_t[sl, :] = mul(acted[...], qkv[:, at(width + i * TILE, TILE, TILE)]).astype(BF16).T
        v_t[sl, :] = mul(acted[...], qkv[:, at(2 * width + i * TILE, TILE, TILE)]).astype(BF16).T
        return carry

    before = pl.ds(0, total - length)
    lax.fori_loop(0, runs[0], project_own, 0)
    keep = []

    def keep_more(*more):
        for src, dst in more:
            copy = pltpu.make_async_copy(src, dst, lsem.at[8 + len(keep)])
            copy.start()
            keep.append(copy)

    def keep_run(run):
        sizes = [pl.ds(p * width + starts[run] * TILE, runs[run] * TILE) for p in range(3)]
        keep_more(*[(qkv.at[:, size], qkv_hbm.at[:, size]) for size in sizes])

    keep_run(0)
    if not alone:

        @pl.when(odd)
        def _():
            for copy in near:
                copy.wait_recv()

        @pl.when(even & far_got)
        def _():
            for copy in relay:
                copy.wait_recv()

        @pl.when(odd & far_got)
        def _():
            for copy in relay:
                copy.wait_send()

    groups[1].move(0)
    lax.fori_loop(0, 2 * per, norm_step, 0)

    mine = seg_ext[2].astype(F32)
    for j in range(3):
        column = jnp.broadcast_to(seg_ext[j].astype(F32), (8, length)).T[:, 0:1]
        column = jnp.where(shard + j >= 2, column, -1.0)
        place = lax.broadcasted_iota(jnp.int32, (length, length), 0) + j * length
        lane = lax.broadcasted_iota(jnp.int32, (length, length), 1)
        near_by = (place > lane) & (place <= lane + WINDOW)
        mask[j * length : (j + 1) * length, :] = jnp.where(near_by & (column == mine), 0.0, MASKED)

    keep_more((acted_t, acted_t_hbm), (mask, mask_hbm))
    groups[1].move(1)
    for group in groups[2:]:
        group.send(0)
    lax.fori_loop(0, runs[0], project_earlier, 0)
    groups[1].move(2)

    half = length // 2

    def attend(h):
        sl = at(h * HEAD, HEAD, 16)
        key, query = k_t[sl, :].T, q_t[sl, :]
        first, last = pl.ds(0, half), pl.ds(total - half, half)
        middle = pl.ds(half, total - length)
        score_m = mul(key[half : total - half], query) + mask[middle, :]
        score_f = mul(key[:half], query[:, :half]) + mask[first, :half]
        score_l = mul(key[total - half :], query[:, half:]) + mask[last, half:]
        ends = [jnp.max(score, axis=0, keepdims=True) for score in (score_f, score_l)]
        top = jnp.maximum(jnp.max(score_m, axis=0, keepdims=True), jnp.concatenate(ends, axis=1))
        prob_m = jnp.exp2(score_m - top)
        prob_f = jnp.exp2(score_f - top[:, :half])
        prob_l = jnp.exp2(score_l - top[:, half:])
        ends = [jnp.sum(prob, axis=0, keepdims=True) for prob in (prob_f, prob_l)]
        norm = jnp.sum(prob_m, axis=0, keepdims=True) + jnp.concatenate(ends, axis=1)
        ends = [mul(v_t[sl, first], prob_f.astype(BF16)), mul(v_t[sl, last], prob_l.astype(BF16))]
        mixed = mul(v_t[sl, middle], prob_m.astype(BF16)) + jnp.concatenate(ends, axis=1)
        o_t[sl, :] = (mixed * (1.0 / norm)).astype(BF16)
        lse[h] = top + jnp.log2(norm)

    pairs = [start * TILE // HEAD // 2 for start in starts]
    last = groups[0].stages - 1

    def steps(index, table):
        for number, actions in table.items():

            @pl.when(index == number)
            def _():
                for group, what in actions:
                    if what == "send":
                        groups[group].send(0)
                    elif what == "settle":
                        groups[group].settle(last)
                    else:
                        groups[group].move(what)

    def attend_run(first, stop, table):
        def attend_pair(pair, carry):
            attend(2 * pair)
            attend(2 * pair + 1)
            steps(pair, table)
            return carry

        lax.fori_loop(first, stop, attend_pair, 0)

    def project_run(first, stop, table):
        def project_step(i, carry):
            project(i, carry)
            steps(i, table)
            return carry

        lax.fori_loop(first, stop, project_step, 0)

    attend_run(0, pairs[1], {pairs[1] - 2: [(2, 0), (3, 0), (4, 0)], pairs[1] - 1: [(1, "settle")]})
    groups[1].finish()
    keep_run(1)
    project_run(starts[1], starts[2], {starts[1]: [(2, 1), (3, 1), (4, 1)]})
    keep_more((q_t, q_t_hbm), (k_t, k_t_hbm), (v_t, v_t_hbm))
    attend_run(
        pairs[1], pairs[2],
        {pairs[1]: [(2, 2), (3, 2)], pairs[2] - 2: [(2, "settle"), (4, 2)]},
    )

    keep_more((o_t, o_t_hbm))

    def turn(i, carry):
        sl = at(i * TILE, TILE, TILE)
        heads[:, sl] = o_t[sl, :].T
        return carry

    lax.fori_loop(0, tiles, turn, 0)
    groups[2].finish()
    keep_more((out, out_hbm))

    def out_step(i, carry):
        sl = at(i * TILE, TILE, TILE)
        hidden[:, sl] = state_low[:, sl].astype(F32) + mul(heads[...], out[:, sl])
        return carry

    lax.fori_loop(0, tiles, out_step, 0)
    keep_more((hidden, hidden_hbm))

    def norm_two(i, carry):
        sl = at(i * TILE, TILE, TILE)
        value = hidden[sl, :]
        scale = lax.rsqrt(jnp.mean(value * value, axis=-1, keepdims=True) + EPS)
        normed = (value * scale * rows_out[1:2, :]).astype(BF16)
        inner[sl, :] = normed
        inner_t[:, sl] = normed.T
        return carry

    lax.fori_loop(0, length // TILE, norm_two, 0)
    keep_more((inner_t, inner_t_hbm))

    groups[3].settle(last)
    groups[3].finish()
    keep_more((up, up_hbm))

    def up_step(i, carry):
        sl = at(i * TILE, TILE, TILE)
        value = mul(inner[...], up[:, sl]) + rows_out[2:3, sl]
        upper[:, sl] = value
        act = (value / (1.0 + jnp.exp(-value))).astype(BF16)
        lower[:, sl] = act
        lower_t[sl, :] = act.T
        return carry

    lax.fori_loop(0, tiles, up_step, 0)
    keep_more((upper, upper_hbm), (lower_t, lower_t_hbm))

    groups[4].settle(last)
    groups[4].finish()
    keep_more((down, down_hbm))

    def down_step(i, carry):
        sl = at(i * TILE, TILE, TILE)
        output[:, sl] = (hidden[:, sl] + (mul(lower[...], down[:, sl]) + rows_out[3:4, sl])).astype(BF16)
        return carry

    lax.fori_loop(0, tiles, down_step, 0)
    keep_more((output, output_hbm))

    if not alone:

        @pl.when(far_ok)
        def _():
            for copy in far[nchunk - 2 :]:
                copy.wait_send()

        @pl.when(even)
        def _():
            for copy in near[nchunk - 2 :]:
                copy.wait_send()

    for copy in vecs:
        copy.wait_send()
    for group in groups:
        group.drain()
    for copy in keep:
        copy.wait()


def forward(count, tokens, earlier, segs, vec, query_scale, w_qkv, w_out, w_up, w_down):
    length, width = tokens.shape
    total = 3 * length
    heads = width // HEAD
    bits = count.bit_length() - 1
    sends = recvs = 1
    if earlier is None:
        single = 2 * (HALO_CHUNKS + 1) + count - 1
        sends, recvs = 5 * 6 + single, 5 * 3 * (bits + 2) + single
    inputs = [x for x in (tokens, earlier, segs, vec, query_scale, w_qkv, w_out, w_up, w_down) if x is not None]
    if earlier is None:
        params = pltpu.CompilerParams(collective_id=0, has_side_effects=True, vmem_limit_bytes=VMEM_LIMIT)
    else:
        params = pltpu.CompilerParams(vmem_limit_bytes=VMEM_LIMIT)
    shape = jax.ShapeDtypeStruct
    outs = (
        shape((length, width), BF16),
        shape((width, total), BF16),
        shape((width, length), BF16),
        shape((width, total), BF16),
        shape((width, total), BF16),
        shape((width, length), BF16),
        shape((heads, 1, length), F32),
        shape((length, width), F32),
        shape((width, length), BF16),
        shape((length, width), F32),
        shape((width, length), BF16),
        shape((8, width), F32),
        shape((width, 3 * width), BF16),
        shape((width, width), BF16),
        shape((width, width), BF16),
        shape((width, width), BF16),
        shape((total, length), F32),
    )
    specs = [ANY] * 17
    specs[6] = specs[11] = VM
    buffer = pltpu.VMEM
    return pl.pallas_call(
        functools.partial(forward_kernel, count) if earlier is not None else lambda *refs: forward_kernel(count, refs[0], None, *refs[1:]),
        name="forward_layer",
        out_shape=outs,
        in_specs=[ANY] * (len(inputs) - 5) + [VM] + [ANY] * 4,
        out_specs=tuple(specs),
        scratch_shapes=[
            buffer((3,) + segs.shape[-2:], jnp.int32),
            buffer((count,) + vec.shape[-2:], F32),
            buffer((width, 3 * width), BF16),
            buffer((width, width), BF16),
            buffer((width, width), BF16),
            buffer((width, width), BF16),
            buffer((total, width), BF16),
            buffer((width, total), BF16),
            buffer((width, length), BF16),
            buffer((width, total), BF16),
            buffer((width, total), BF16),
            buffer((width, length), BF16),
            buffer((length, width), BF16),
            buffer((length, width), BF16),
            buffer((length, width), F32),
            buffer((length, width), F32),
            buffer((width, length), BF16),
            buffer((width, length), BF16),
            buffer((total, length), F32),
            buffer((length, width), BF16),
            pltpu.SemaphoreType.DMA((sends,)),
            pltpu.SemaphoreType.DMA((recvs,)),
            pltpu.SemaphoreType.DMA((28,)),
        ],
        compiler_params=params,
    )(*inputs)


class Halving:
    def __init__(self, sems, credits, count, rows, orders, acc, other, land, result, reused):
        self.sems, self.credits, self.rows, self.half, self.reused = sems, credits, rows, rows // 2, reused
        self.acc, self.other, self.land, self.result = acc, other, land, result
        self.bits = count.bit_length() - 1
        self.plan, self.core_slot, self.cross_slot, self.share_slot = [], [], [], []
        self.stage_send, self.stage_recv = [], []
        self.at_stage = [0] * len(orders)
        for order in orders:
            left, whole, base, stages = list(range(self.bits)), True, 0, []
            for what in order:
                steps = []
                if what == "x":
                    whole = False
                else:
                    left.remove(what)
                for mask in span(left):
                    size = rows if whole else self.half
                    steps.append((mask, base, size, len(stages)))
                    base += size
                stages.append((what, whole, steps))
            self.plan.append(stages)
            self.core_slot.append(sems.slot())
            self.cross_slot.append(sems.slot())
            self.share_slot.append(sems.slot())
            self.stage_send.append(sems.send_slot())
            self.stage_recv.append([sems.recv_slot() for _ in order])

    def partner(self, what):
        rep, shard = lax.axis_index("rep"), lax.axis_index("shard")
        if what == "core":
            return flip(rep, 1), shard
        if what == "x":
            return flip(rep, 2), shard
        return rep, flip(shard, 1 << what)

    def credit(self, part, what):
        place = 0 if what == "core" else 1 if what == "x" else 2 + what
        return self.credits.at[part * (self.bits + 2) + place]

    def allow(self, part, what):
        rep, shard = self.partner(what)
        pl.semaphore_signal(
            self.credit(part, what), inc=1, device_id={"rep": rep, "shard": shard}, device_id_type=MESH
        )

    def core_copy(self, part):
        return self.sems.remote(self.other[part], self.land[part], *self.partner("core"), self.core_slot[part])

    def core_send(self, part):
        if self.reused:
            pl.semaphore_wait(self.credit(part, "core"), 1)
        self.core_copy(part).start()

    def core_add(self, part):
        self.core_copy(part).wait_recv()
        acc, land = self.acc[part], self.land[part]

        def step(i, carry):
            sl = at(i * TILE, TILE, TILE)
            acc[sl, :] = (acc[sl, :].astype(F32) + land[sl, :].astype(F32)).astype(BF16)
            return carry

        lax.fori_loop(0, acc.shape[0] // TILE, step, 0)
        for what, _, _ in self.plan[part]:
            self.allow(part, what)
        self.send(part, 0)

    def copy(self, part, stage, step):
        what, whole, _ = self.plan[part][stage]
        mask, base, size, _ = step
        slot = self.stage_send[part], self.stage_recv[part][stage]
        shard, cross = lax.axis_index("shard"), lax.div(lax.axis_index("rep"), 2)
        if what == "x":
            row = flip(shard, mask) * self.rows + (1 - cross) * self.half
        else:
            row = flip(shard, mask | (1 << what)) * self.rows
            row = row if whole else row + cross * self.half
        src = self.acc[part].at[at(row, size, 16)]
        return self.sems.remote(src, self.land[part].at[pl.ds(base, size)], *self.partner(what), slot)

    def send(self, part, stage):
        what, _, steps = self.plan[part][stage]
        pl.semaphore_wait(self.credit(part, what), 1)
        for step in steps:
            self.copy(part, stage, step).start()

    def receive(self, part, stage):
        what, whole, steps = self.plan[part][stage]
        shard, cross = lax.axis_index("shard"), lax.div(lax.axis_index("rep"), 2)
        slot = self.stage_send[part], self.stage_recv[part][stage]
        spot = self.land[part].at[pl.ds(steps[0][1], sum(step[2] for step in steps))]
        self.sems.remote(spot, spot, *self.partner(what), slot).wait_recv()
        for mask, base, size, _ in steps:
            row = flip(shard, mask) * self.rows
            row = row if whole else row + cross * self.half
            sl = at(row, size, 16)
            new = self.acc[part][sl, :].astype(F32) + self.land[part][pl.ds(base, size), :].astype(F32)
            self.acc[part][sl, :] = new.astype(BF16)

    def advance(self, part):
        stage = self.at_stage[part]
        self.at_stage[part] += 1
        if stage <= self.bits:
            self.receive(part, stage)
        if stage < self.bits:
            self.send(part, stage + 1)
        elif stage == self.bits:
            core, cross = self.sides()
            shard = lax.axis_index("shard")
            row = shard * self.rows + cross * self.half
            self.result[part].at[core][at(cross * self.half, self.half, 16), :] = self.acc[part][at(row, self.half, 16), :]
            self.cross_copy(part).start()
        elif stage == self.bits + 1:
            self.cross_copy(part).wait_recv()
            self.share_copy(part).start()
        else:
            self.share_copy(part).wait_recv()

    def sides(self):
        rep = lax.axis_index("rep")
        return lax.rem(rep, 2), lax.div(rep, 2)

    def cross_copy(self, part):
        core, cross = self.sides()
        spot = self.result[part].at[core, at(cross * self.half, self.half, 16)]
        return self.sems.remote(spot, spot, *self.partner("x"), self.cross_slot[part])

    def share_copy(self, part):
        core, _ = self.sides()
        spot = self.result[part].at[core]
        return self.sems.remote(spot, spot, *self.partner("core"), self.share_slot[part])

    def drain_other(self, part):
        self.core_copy(part).wait_send()

    def drain_acc(self, part):
        size = sum(step[2] for _, _, steps in self.plan[part] for step in steps)
        spot = self.acc[part].at[pl.ds(0, size)]
        slot = self.stage_send[part], self.stage_recv[part][0]
        self.sems.remote(spot, spot, *self.partner("core"), slot).wait_send()

    def drain_result(self, part):
        self.cross_copy(part).wait_send()
        self.share_copy(part).wait_send()


def backward_kernel(count, alone, *refs):
    (
        cot_hbm, tokens_hbm, hidden_hbm, inner_t_hbm, upper_hbm, lower_t_hbm, o_t_hbm, q_t_hbm, k_t_hbm, v_t_hbm,
        acted_t_hbm, qkv_hbm, out_hbm, up_hbm, down_hbm, mask_hbm, lse, rows_in,
    ) = refs[:18]
    if alone:
        (hidden_out, qkv_out, out_out, up_out, down_out, acted_out, small_out) = refs[18:25]
    else:
        (input_grad, qkv_out, out_out, up_out, down_out, small_out) = refs[18:24]
    scratch = refs[25:] if alone else refs[24:]
    (
        wide, flat, wtile, first_f32, grad_hidden, q_t, k_t, v_t, do_t, delta, mask, scale_sum, acc, other, land,
        result_ff, result_qkv, factor, near_in, far_in, state_low, small_now, small_in, lsem, send, recv, credits,
    ) = scratch
    rep, shard = lax.axis_index("rep"), lax.axis_index("shard")
    core = lax.rem(rep, 2)
    length, width = cot_hbm.shape
    total = 3 * length
    tiles = width // TILE
    rows = width // count
    cols = width // 2
    heads = width // HEAD
    own = pl.ds(total - length, length)
    bits = count.bit_length() - 1
    sems = Sems(send, recv)
    lower_t, inner_t, o_t = (wide.at[:, pl.ds(i * length, length)] for i in range(3))
    cot, grad_upper, grad_attn = (flat.at[i] for i in range(3))
    parts = [[ref.at[i] for i in range(3)] for ref in (acc, other, land, result_ff, result_qkv)]

    def local(src, dst, slot):
        return pltpu.make_async_copy(src, dst, lsem.at[slot])

    loads = {
        "cot": local(cot_hbm, cot, 0),
        "lower": local(lower_t_hbm, lower_t, 1),
        "upper": local(upper_hbm, first_f32, 2),
        "inner": local(inner_t_hbm, inner_t, 3),
        "o": local(o_t_hbm, o_t, 4),
        "q": local(q_t_hbm, q_t, 5),
        "k": local(k_t_hbm, k_t, 6),
        "v": local(v_t_hbm, v_t, 7),
        "mask": local(mask_hbm, mask, 8),
        "state": local(tokens_hbm, state_low, 9),
    }
    load_hidden = local(hidden_hbm, first_f32, 10)
    load_acted = local(acted_t_hbm, wide, 11)

    def tile_copy(src, order, i):
        slot = lax.rem(order * tiles + i, 6)
        return local(src.at[at(i * TILE, TILE, TILE)], wtile.at[slot], 12 + slot)

    def wide_copies(i):
        first = 3 * (i % 2)
        return [
            local(qkv_hbm.at[pl.ds(i * TILE, TILE), pl.ds(k * width, width)], wtile.at[first + k], 12 + first + k)
            for k in range(3)
        ]

    def tile_next(src, after, order, i):
        tile_copy(src, order, i).wait()
        if after is not None:
            tile_copy(after, order + 1, i).start()
        return lax.rem(order * tiles + i, 6)

    for name in ("lower", "cot"):
        loads[name].start()
    loads["upper"].start()
    for i in range(tiles):
        tile_copy(down_hbm, 0, i).start()
    for name in ("inner", "o"):
        loads[name].start()
    if alone:
        ff = qkv = None
    else:
        greet(count)
        ff = Halving(sems, credits.at[0], count, rows, beside_orders(bits), *parts[:4], False)
        cut = cols * 3 // 5 // 128 * 128
        runs = ((0, 0, cols), (1, 0, cut), (1, cut, cols - cut), (2, 0, cut), (2, cut, cols - cut))
        back = [[ref.at[2 - m, :, pl.ds(at_col, size)] for m, at_col, size in runs] for ref in (acc, other, land)]
        ends = [result_qkv.at[m, :, :, pl.ds(at_col, size)] for m, at_col, size in runs]
        qkv = Halving(sems, credits.at[1], count, rows, tail_orders(bits), *back, ends, True)
    copies_out = []

    def group_parts(first_use, part):
        return (part,) if first_use else ((0,), (1, 2), (3, 4))[part]

    def weight_side(group, part, left, right, side_core, first_use=False):
        theirs = side_core is not core
        dest = (other if theirs else acc).at[part if first_use else 2 - part]

        def step(i, carry):
            sl = at(i * cols, cols, 16)
            dest[sl, :] = right(left(sl), side_core * cols).astype(BF16)
            return carry

        lax.fori_loop(0, 2, step, 0)
        if theirs and group is not None:
            for run in group_parts(first_use, part):
                group.core_send(run)

    def weight_out(part, target, first, first_use=False):
        for ref, side_core in ((other, 1 - core), (acc, core)):
            copy = local(ref.at[part if first_use else 2 - part], target.at[:, at(first + side_core * cols, cols, 128)], 20 + len(copies_out))
            copy.start()
            copies_out.append(copy)

    def weight_grad(group, part, left, right, target):
        weight_side(group, part, left, right, 1 - core, True)
        weight_side(group, part, left, right, core, True)
        if alone:
            weight_out(part, target, 0, True)

    small_now[0] = jnp.zeros_like(small_now[0])
    loads["lower"].wait()
    loads["cot"].wait()
    weight_grad(
        ff, 2, lambda sl: lower_t[sl, :], lambda left, col: mul(left, cot[:, at(col, cols, 128)]), down_out
    )
    loads["upper"].wait()

    def down_step(i, carry):
        sl = at(i * TILE, TILE, TILE)
        slot = tile_next(down_hbm, up_hbm, 0, i)
        grad_lower = mul(cot[...], wtile[slot], 1, 1)
        value = first_f32[:, sl]
        gate = 1.0 / (1.0 + jnp.exp(-value))
        grad = (grad_lower * (gate + value * gate * (1.0 - gate))).astype(BF16)
        grad_upper[:, sl] = grad
        small_now[0, 2:3, sl] = jnp.sum(grad.astype(F32), axis=0, keepdims=True)
        small_now[0, 3:4, sl] = jnp.sum(cot[:, sl].astype(F32), axis=0, keepdims=True)
        return carry

    lax.fori_loop(0, tiles, down_step, 0)
    load_hidden.start()
    for name in ("q", "k", "v", "mask", "state"):
        loads[name].start()
    loads["inner"].wait()
    weight_grad(
        ff, 1, lambda sl: inner_t[sl, :], lambda left, col: mul(left, grad_upper[:, at(col, cols, 128)]), up_out
    )
    if not alone:
        ff.core_add(2)

    def up_step(i, carry):
        sl = at(i * TILE, TILE, TILE)
        slot = tile_next(up_hbm, out_hbm, 1, i)
        grad_hidden[:, sl] = mul(grad_upper[...], wtile[slot], 1, 1)
        return carry

    lax.fori_loop(0, tiles, up_step, 0)
    load_hidden.wait()
    if not alone:
        ff.core_add(1)

    def norm_step(i, carry):
        sl = at(i * TILE, TILE, TILE)
        value = first_f32[sl, :]
        scale = lax.rsqrt(jnp.mean(value * value, axis=-1, keepdims=True) + EPS)
        normed = value * scale
        grad = grad_hidden[sl, :]
        small_now[0, 1:2, :] += jnp.sum(grad * normed, axis=0, keepdims=True)
        weighted = grad * rows_in[1:2, :]
        along = jnp.mean(weighted * normed, axis=-1, keepdims=True)
        whole = cot[sl, :].astype(F32) + scale * (weighted - normed * along)
        grad_hidden[sl, :] = whole
        grad_attn[sl, :] = whole.astype(BF16)
        return carry

    lax.fori_loop(0, length // TILE, norm_step, 0)
    loads["o"].wait()
    weight_grad(
        ff, 0, lambda sl: o_t[sl, :], lambda left, col: mul(left, grad_attn[:, at(col, cols, 128)]), out_out
    )

    def out_step(i, carry):
        sl = at(i * TILE, TILE, TILE)
        slot = tile_next(out_hbm, None, 2, i)
        do_t[sl, :] = mul(grad_attn[...], wtile[slot], 1, 1).astype(BF16).T
        return carry

    lax.fori_loop(0, tiles, out_step, 0)
    if not alone:
        ff.core_add(0)

    def delta_step(h, carry):
        sl = at(h * HEAD, HEAD, 16)
        delta[h] = jnp.sum(o_t[sl, :].astype(F32) * do_t[sl, :].astype(F32), axis=0, keepdims=True)
        return carry

    lax.fori_loop(0, heads, delta_step, 0)
    load_acted.start()
    for i in range(2):
        for copy in wide_copies(i):
            copy.start()
    for name in ("q", "k", "v", "mask"):
        loads[name].wait()
    scale_sum[...] = jnp.zeros_like(scale_sum)
    factor[...] = jnp.broadcast_to(rows_in[4:5, 0:HEAD] * LN2, (128, HEAD)).T
    half = length // 2
    pieces = (
        (0, half, (0,)),
        (half, length, (0, 1)),
        (half + length, length, (0, 1)),
        (total - half, half, (1,)),
    )

    def attend(h, carry):
        sl = at(h * HEAD, HEAD, 16)
        query, grad = q_t[sl, :], do_t[sl, :]
        parts_dq = [jnp.zeros((HEAD, half), F32)] * 2
        for first, size, sides in pieces:
            ks, qs = pl.ds(first, size), slice(sides[0] * half, (sides[-1] + 1) * half)
            key, value = k_t[sl, ks], v_t[sl, ks]
            query_part, grad_part = query[:, qs], grad[:, qs]
            probs = jnp.exp2(mul(key.T, query_part) + mask[ks, qs] - lse[h][:, qs])
            scores = (probs * (mul(value.T, grad_part) - delta[h][:, qs])).astype(BF16)
            v_t[sl, ks] = mul(grad_part, probs.astype(BF16), 1, 1).astype(BF16)
            k_t[sl, ks] = (mul(query_part, scores, 1, 1) * LN2).astype(BF16)
            term = mul(key, scores)
            for place, side in enumerate(sides):
                parts_dq[side] = parts_dq[side] + term[:, place * half : (place + 1) * half]
        dq = jnp.concatenate(parts_dq, axis=1)
        scale_sum[...] += dq * query.astype(F32)
        q_t[sl, :] = (dq * factor[:, 0:1]).astype(BF16)
        if not alone:
            for head in sorted({step[0] for step in FF_STEPS}):

                @pl.when(h == head)
                def _():
                    for _, part, stage in [step for step in FF_STEPS if step[0] == head]:
                        ff.at_stage[part] = stage
                        ff.advance(part)
                        if stage == bits:
                            for run in group_parts(False, 2 - part):
                                qkv.allow(run, "core")

        return carry

    lax.fori_loop(0, heads, attend, 0)

    def give_result(group, part, target, first):
        for side in range(2):
            src = (result_ff if group is ff else result_qkv).at[part, side]
            copy = local(src, target.at[:, pl.ds(first + side * cols, cols)], 20 + len(copies_out))
            copy.start()
            copies_out.append(copy)

    load_acted.wait()
    odd = lax.rem(shard, 2) == 1
    even = jnp.logical_not(odd)
    far_ok, far_got = shard >= 2, shard < count - 2
    buddy = flip(shard, 1)
    far_to = lax.rem(shard + count - 2, count)
    give_slots = [sems.slot() for _ in range(tiles)]
    far_slots = [sems.slot() for _ in range(tiles)]

    def give(i):
        sl = pl.ds(i * TILE, TILE)
        return sems.remote(flat.at[1, :, sl], near_in.at[:, sl], rep, buddy, give_slots[i])

    def far(i):
        sl = pl.ds(i * TILE, TILE)
        return sems.remote(flat.at[0, :, sl], far_in.at[:, sl], rep, far_to, far_slots[i])

    def state_step(i):
        sl = pl.ds(i * TILE, TILE)
        for copy in wide_copies(i):
            copy.wait()
        slot = 3 * (i % 2)
        both = mul(wtile[slot + 1], k_t[...]) + mul(wtile[slot + 2], v_t[...])
        mine = both[:, total - length :] + mul(wtile[slot], q_t[...])
        both = jnp.concatenate([both[:, : total - length], mine], axis=1)
        low = both.astype(BF16)
        sums = jnp.sum(both * wide[sl, :].astype(F32), axis=1, keepdims=True)
        small_now[0, 0:1, sl] = jnp.broadcast_to(sums, (TILE, 128)).T[0:1, :] / rows_in[0:1, sl]
        for j in range(3):
            flat[j, :, sl] = low[:, j * length : (j + 1) * length].T
        if i + 2 < tiles:
            for copy in wide_copies(i + 2):
                copy.start()

    def give_start(i):
        @pl.when(odd | far_ok)
        def _():
            give(i).start()

    def far_start(i):
        @pl.when(even | far_ok)
        def _():
            give(i).wait_recv()

        @pl.when(odd & far_ok)
        def _():
            sl = pl.ds(i * TILE, TILE)
            flat[0, :, sl] = (flat[0, :, sl].astype(F32) + near_in[:, sl].astype(F32)).astype(BF16)

        @pl.when(far_ok)
        def _():
            far(i).start()

    if alone:
        for copy in copies_out:
            copy.wait()
    else:
        ff.at_stage = [max([step[2] + 1 for step in FF_STEPS if step[1] == part]) for part in range(3)]
        for part in (1, 2):
            ff.drain_other(part)
            ff.drain_acc(part)
    for side_core in (1 - core, core):
        weight_side(
            qkv, 0, lambda sl: wide[sl, own], lambda left, col: mul(left, q_t[at(col, cols, 16), :], 1, 1), side_core
        )
    for i in range(tiles):
        state_step(i)
        if alone:
            continue
        give_start(i)
        if i == 0:
            qkv.core_add(0)
            ff.advance(0)
        if i == 4:
            far_start(0)
    spread = jnp.sum(scale_sum[...], axis=1, keepdims=True)
    small_now[0, 4:5, 0:HEAD] = jnp.broadcast_to(spread, (HEAD, 128)).T[0:1, :]
    partners = ("core", "x") + tuple(range(bits))
    small_slots = [sems.slot() for _ in partners]

    def small_copy(number):
        return sems.remote(
            small_now.at[number], small_in.at[number], *ff.partner(partners[number]), small_slots[number]
        )

    def small_step(number):
        small_copy(number).wait()
        small_now[number + 1] = small_now[number] + small_in[number]
        if number + 1 < len(partners):
            small_copy(number + 1).start()

    if not alone:
        small_copy(0).start()
        ff.advance(0)
        for run in group_parts(False, 2):
            qkv.allow(run, "core")
        far_start(1)
    weight_side(qkv, 1, lambda sl: wide[sl, :], lambda left, col: mul(left, k_t[at(col, cols, 16), :], 1, 1), 1 - core)
    if not alone:
        far_start(2)
        small_step(0)
    weight_side(qkv, 1, lambda sl: wide[sl, :], lambda left, col: mul(left, k_t[at(col, cols, 16), :], 1, 1), core)
    if not alone:
        ff.drain_other(0)
        ff.drain_acc(0)
        qkv.core_add(1)
        qkv.core_add(2)
        qkv.advance(0)
        far_start(3)
        small_step(1)
    weight_side(qkv, 2, lambda sl: wide[sl, :], lambda left, col: mul(left, v_t[at(col, cols, 16), :], 1, 1), 1 - core)
    if not alone:
        far_start(4)
    weight_side(qkv, 2, lambda sl: wide[sl, :], lambda left, col: mul(left, v_t[at(col, cols, 16), :], 1, 1), core)
    if alone:
        for part in range(3):
            weight_out(part, qkv_out, part * width)
    if alone:
        small_out[...] = small_now[0]
        tail = [local(grad_hidden, hidden_out, 18), local(flat, acted_out, 19)]
        for copy in tail:
            copy.start()
        loads["state"].wait()
        for copy in tail + copies_out[6:]:
            copy.wait()
        return

    qkv.core_add(3)
    qkv.core_add(4)
    small_step(2)

    def round_robin(*order):
        for part in order:
            qkv.advance(part)

    round_robin(0, 2, 1)
    round_robin(4, 3)
    ff.advance(0)
    for part, target in enumerate((out_out, up_out, down_out)):
        ff.advance(part)
        give_result(ff, part, target, 0)
    small_step(3)
    round_robin(0, 2, 1)
    round_robin(4, 3)

    loads["state"].wait()
    for i in range(tiles):

        @pl.when(far_got)
        def _():
            far(i).wait_recv()


    def final_step(i, carry):
        sl = at(i * 128, 128, 128)
        state = state_low[sl, :].astype(F32)
        inverse = lax.rsqrt(jnp.mean(state * state, axis=-1, keepdims=True) + EPS)
        normed = state * inverse
        grad = flat[2, sl, :].astype(F32)
        grad += jnp.where(even, near_in[sl, :].astype(F32), 0.0)
        grad += jnp.where(far_got, far_in[sl, :].astype(F32), 0.0)
        weighted = grad * rows_in[0:1, :]
        along = jnp.mean(weighted * normed, axis=-1, keepdims=True)
        state_low[sl, :] = (grad_hidden[sl, :] + inverse * (weighted - normed * along)).astype(BF16)
        return carry

    lax.fori_loop(0, length // 128, final_step, 0)
    write = local(state_low, input_grad, 18)
    write.start()
    for number in range(4, len(partners)):
        small_step(number)
    last = len(partners)
    small_out[...] = jnp.zeros_like(small_out)
    for place in range(count):

        @pl.when(shard == place)
        def _():
            small_out[0:4, 0:rows] = small_now[last, 0:4, place * rows : (place + 1) * rows]

    small_out[4:5, 0:HEAD] = small_now[last, 4:5, 0:HEAD] * rows_in[5:6, 0:HEAD]
    while min(qkv.at_stage) <= bits + 2:
        round_robin(*[part for part in (0, 2, 1, 4, 3) if qkv.at_stage[part] <= bits + 2])
    for part in range(3):
        give_result(qkv, part, qkv_out, part * width)

    for i in range(tiles):

        @pl.when(odd | far_ok)
        def _():
            give(i).wait_send()

        @pl.when(far_ok)
        def _():
            far(i).wait_send()

    for part in range(5):
        qkv.drain_other(part)
        qkv.drain_acc(part)
        qkv.drain_result(part)
    for part in range(3):
        ff.drain_result(part)
    for copy in copies_out:
        copy.wait()
    write.wait()


FF_STEPS = (
    (2, 2, 0), (4, 1, 0), (7, 2, 1), (8, 1, 1), (9, 2, 2), (10, 0, 0),
    (11, 1, 2), (12, 2, 3), (13, 1, 3), (14, 0, 1), (15, 2, 4), (15, 1, 4),
)


def backward(count, alone, *inputs):
    length, width = inputs[0].shape
    total = 3 * length
    rows = width // count
    cols = width // 2
    heads = width // HEAD
    bits = count.bit_length() - 1
    sends = recvs = 1
    if not alone:
        single = 2 * (width // TILE) + bits + 2
        sends, recvs = 8 * 4 + single, 8 * (bits + 4) + single
    shape = jax.ShapeDtypeStruct
    if alone:
        outs = (
            shape((length, width), F32),
            shape((width, 3 * width), BF16),
            shape((width, width), BF16),
            shape((width, width), BF16),
            shape((width, width), BF16),
            shape((3, length, width), BF16),
            shape((8, width), F32),
        )
        params = pltpu.CompilerParams(vmem_limit_bytes=VMEM_LIMIT)
    else:
        outs = (
            shape((length, width), BF16),
            shape((rows, 3 * width), BF16),
            shape((rows, width), BF16),
            shape((rows, width), BF16),
            shape((rows, width), BF16),
            shape((8, 256), F32),
        )
        params = pltpu.CompilerParams(collective_id=1, has_side_effects=True, vmem_limit_bytes=VMEM_LIMIT)
    buffer = pltpu.VMEM
    return pl.pallas_call(
        functools.partial(backward_kernel, count, alone),
        name="backward_layer",
        out_shape=outs,
        in_specs=[ANY] * 16 + [VM] * 2,
        out_specs=(ANY,) * (len(outs) - 1) + (VM,),
        scratch_shapes=[
            buffer((width, total), BF16),
            buffer((3, length, width), BF16),
            buffer((6, TILE, width), BF16),
            buffer((length, width), F32),
            buffer((length, width), F32),
            buffer((width, length), BF16),
            buffer((width, total), BF16),
            buffer((width, total), BF16),
            buffer((width, length), BF16),
            buffer((heads, 1, length), F32),
            buffer((total, length), F32),
            buffer((HEAD, length), F32),
            buffer((3, width, cols), BF16),
            buffer((3, width, cols), BF16),
            buffer((3, width, cols), BF16),
            buffer((3, 2, rows, cols), BF16),
            buffer((3, 2, rows, cols), BF16),
            buffer((HEAD, 128), F32),
            buffer((length, width), BF16),
            buffer((length, width), BF16),
            buffer((length, width), BF16),
            buffer((bits + 3, 8, width), F32),
            buffer((bits + 2, 8, width), F32),
            pltpu.SemaphoreType.DMA((32,)),
            pltpu.SemaphoreType.DMA((sends,)),
            pltpu.SemaphoreType.DMA((recvs,)),
            pltpu.SemaphoreType.REGULAR((2, 5 * (bits + 2))),
        ],
        compiler_params=params,
    )(*inputs)


def finish_kernel(*refs):
    small = refs[6]
    for src, dst in zip(refs[:6], refs[7:13]):
        dst[...] = src[...].astype(dst.dtype)
    for row, dst in enumerate(refs[13:]):
        dst[...] = small[row, 0 : dst.shape[0]]


def finish(small, *arrays):
    shape = jax.ShapeDtypeStruct
    outs = [shape(array.shape, F32 if place < 4 else array.dtype) for place, array in enumerate(arrays)]
    specs = [pl.BlockSpec((array.shape[0] // 2, array.shape[1]), lambda i: (i, 0)) for array in arrays]
    lines = [arrays[0].shape[0]] * 4 + [HEAD]
    outs += [shape((line,), F32) for line in lines]
    line_specs = [pl.BlockSpec((line,), lambda i: (0,)) for line in lines]
    return pl.pallas_call(
        finish_kernel,
        name="finish",
        grid=(2,),
        out_shape=tuple(outs),
        in_specs=specs + [pl.BlockSpec(small.shape, lambda i: (0, 0))],
        out_specs=tuple(specs + line_specs),
        compiler_params=pltpu.CompilerParams(vmem_limit_bytes=VMEM_LIMIT),
    )(*arrays, small)


def shifted(value, steps):
    count = lax.axis_size("shard")
    first, last = (max(0, -steps), min(count, count - steps))
    return lax.ppermute(value, "shard", [(source, source + steps) for source in range(first, last)])


def gather_plain(tokens, segs, vec, *weights):
    whole = tuple(lax.all_gather(weight, "shard", axis=0, tiled=True) for weight in weights)
    earlier = jnp.concatenate([shifted(tokens, 2), shifted(tokens, 1)])
    seg_ext = jnp.stack([shifted(segs, 2), shifted(segs, 1), segs])
    return (earlier, seg_ext, lax.all_gather(vec, "shard", axis=0)) + whole


def reduce_plain(qkv_grad, out_grad, up_grad, down_grad, grad_acted, small):
    owned = []
    for grad in (qkv_grad, out_grad, up_grad, down_grad):
        part = lax.psum_scatter(grad, "shard", scatter_dimension=0, tiled=True)
        owned.append(lax.psum(part, "rep").astype(F32))
    parts = [grad_acted[2], shifted(grad_acted[0], -2), shifted(grad_acted[1], -1)]
    return (*owned, sum(part.astype(F32) for part in parts), lax.psum(small, ("rep", "shard")))


def body(
    tokens,
    segments,
    cotangent,
    gain_one,
    qkv_weight,
    query_scale,
    out_weight,
    gain_two,
    up_weight,
    up_bias,
    down_weight,
    down_bias,
):
    count = lax.axis_size("shard")
    shard = lax.axis_index("shard")
    length, width = tokens.shape[1:]
    rows = qkv_weight.shape[0]

    vec = jnp.concatenate([gain_one, gain_two, up_bias, down_bias]).astype(F32)
    vec = jnp.pad(vec, (0, -vec.shape[0] % 1024)).reshape(-1, 128)
    segs = segments
    whole_tiles = rows % 32 == 0 and count >= 4 and count & (count - 1) == 0 and lax.axis_size("rep") == 4
    weights = (qkv_weight, out_weight, up_weight, down_weight)
    earlier = None
    if not whole_tiles:
        earlier, segs, vec, *weights = gather_plain(tokens[0], segs, vec, *weights)
    output, acted_t, q_t, k_t, v_t, o_t, lse, hidden, inner_t, upper, lower_t, rows_in, qkv, out, up, down, mask = forward(
        count, tokens[0], earlier, segs, vec, query_scale[None], *weights
    )
    results = backward(
        count, not whole_tiles, cotangent[0], tokens[0], hidden, inner_t, upper, lower_t, o_t, q_t, k_t, v_t, acted_t,
        qkv, out, up, down, mask, lse, rows_in,
    )
    if whole_tiles:
        qkv_own, out_own, up_own, down_own, output, input_grad, *vectors = finish(
            results[5], *results[1:5], output, results[0]
        )
    else:
        grad_hidden, *partial = results
        qkv_own, out_own, up_own, down_own, grad_acted, small = reduce_plain(*partial)
        state = tokens[0].astype(F32)
        inverse = lax.rsqrt(jnp.mean(state * state, axis=-1, keepdims=True) + EPS)
        normed = state * inverse
        weighted = grad_acted * rows_in[0:1]
        along = jnp.mean(weighted * normed, axis=-1, keepdims=True)
        input_grad = (grad_hidden + inverse * (weighted - normed * along)).astype(BF16)
        mine = lax.dynamic_slice_in_dim(small[:4], shard * rows, rows, 1)
        vectors = [*mine, small[4, :HEAD] * rows_in[5, :HEAD]]

    return (
        output[None],
        input_grad[None],
        vectors[0],
        qkv_own,
        vectors[4],
        out_own,
        vectors[1],
        up_own,
        vectors[2],
        down_own,
        vectors[3],
    )


def solution(mesh):
    return jax.shard_map(
        body,
        mesh=mesh,
        in_specs=(
            P("rep", "shard", None),
            P("rep", "shard"),
            P("rep", "shard", None),
            P("shard"),
            P("shard", None),
            P(),
            P("shard", None),
            P("shard"),
            P("shard", None),
            P("shard"),
            P("shard", None),
            P("shard"),
        ),
        out_specs=(
            P("rep", "shard", None),
            P("rep", "shard", None),
            P("shard"),
            P("shard", None),
            P(),
            P("shard", None),
            P("shard"),
            P("shard", None),
            P("shard"),
            P("shard", None),
            P("shard"),
        ),
        check_vma=False,
    )
```

```python
import functools
import math

import jax
import jax.numpy as jnp
from jax import lax
from jax.experimental import pallas as pl
from jax.experimental.pallas import tpu as pltpu
from jax.sharding import PartitionSpec as P

HEAD = 80
WINDOW = 1024
EPS = 1e-06
LOG2E = 1.442695041
LN2 = math.log(2.0)
MASKED = -1e30
TILE = 256
MESH = pl.DeviceIdType.MESH
F32 = jnp.float32
BF16 = jnp.bfloat16
VMEM_LIMIT = 62 * 2**20
HALO_CHUNKS = 8
ANY = pl.BlockSpec(memory_space=pl.ANY)
VM = pl.BlockSpec(memory_space=pltpu.VMEM)


def mul(a, b, left=1, right=0):
    return lax.dot_general(a, b, (((left,), (right,)), ((), ())), preferred_element_type=F32)


def at(start, size, unit):
    return pl.ds(pl.multiple_of(start, unit), size)


def bit_of(index, bit):
    return lax.rem(lax.div(index, 1 << bit), 2)


def flip(index, mask):
    out = index
    bit = 0
    while mask >> bit:
        if (mask >> bit) & 1:
            out = out + (1 - 2 * bit_of(index, bit)) * (1 << bit)
        bit += 1
    return out


def span(bits):
    masks = [0]
    for bit in bits:
        masks = masks + [mask | (1 << bit) for mask in masks]
    return masks


def stage_orders(bits):
    rest = list(range(2, bits))
    return (["x", 0, 1] + rest, [0, 1, "x"] + rest, [1, "x", 0] + rest)


def cross_orders(bits):
    rest = list(range(2, bits))
    return (["x", 0, 1] + rest, ["x", 1, 0] + rest, ["x", 0, 1] + rest)


def greet(count):
    rep, shard = lax.axis_index("rep"), lax.axis_index("shard")
    barrier = pltpu.get_barrier_semaphore()
    for step in range(1, count):
        other = lax.rem(shard + step, count)
        pl.semaphore_signal(barrier, inc=1, device_id={"rep": rep, "shard": other}, device_id_type=MESH)
    for mask in (1, 2):
        pl.semaphore_signal(barrier, inc=1, device_id={"rep": flip(rep, mask), "shard": shard}, device_id_type=MESH)
    pl.semaphore_wait(barrier, count + 1)


class Sems:
    def __init__(self, send, recv):
        self.send, self.recv, self.sends, self.recvs = send, recv, 0, 0

    def send_slot(self):
        self.sends += 1
        return self.sends - 1

    def recv_slot(self):
        self.recvs += 1
        return self.recvs - 1

    def slot(self):
        return self.send_slot(), self.recv_slot()

    def remote(self, src, dst, rep, shard, slot):
        return pltpu.make_async_remote_copy(
            src_ref=src,
            dst_ref=dst,
            send_sem=self.send.at[slot[0]],
            recv_sem=self.recv.at[slot[1]],
            device_id={"rep": rep, "shard": shard},
            device_id_type=MESH,
        )


class Doubling:
    def __init__(self, sems, count, rows, orders, parts):
        self.sems, self.rows, self.half, self.parts = sems, rows, rows // 2, parts
        bits = count.bit_length() - 1
        self.stages = bits + 1
        self.plan = []
        for order in orders:
            have, whole, stages = [], False, []
            for what in order[::-1]:
                masks = span(have)[1:] if what == "x" else span(have)
                stages.append([(what, mask, whole, len(stages)) for mask in masks])
                if what == "x":
                    whole = True
                else:
                    have.append(what)
            self.plan.append(stages)
        self.copy_send = [sems.send_slot() for _ in orders]
        self.stage_recv = [[sems.recv_slot() for _ in range(self.stages)] for _ in orders]
        self.ahead_slot = [sems.slot() for _ in orders]

    def copy(self, part, step):
        what, mask, whole, stage = step
        rep, shard = lax.axis_index("rep"), lax.axis_index("shard")
        core, cross = lax.rem(rep, 2), lax.div(rep, 2)
        src, dst, first, cols = self.parts[part]
        across = at(first + core * cols, cols, 128)
        shift, size = (0, self.rows) if whole else (cross * self.half, self.half)
        row = flip(shard, mask) * self.rows + shift
        to = dst.at[at(row, size, 16), across]
        here = src.at[at(shift, size, 16), across] if mask == 0 else to
        slot = self.copy_send[part], self.stage_recv[part][stage]
        if what == "x":
            return self.sems.remote(here, to, flip(rep, 2), shard, slot)
        return self.sems.remote(here, to, rep, flip(shard, 1 << what), slot)

    def ahead(self, part, step):
        what, mask, whole, _ = step
        rep, shard = lax.axis_index("rep"), lax.axis_index("shard")
        core, cross = lax.rem(rep, 2), lax.div(rep, 2)
        _, dst, first, cols = self.parts[part]
        if what == "x":
            row, size = flip(shard, mask) * self.rows + (1 - cross) * self.half, self.half
        else:
            shift, size = (0, self.rows) if whole else (cross * self.half, self.half)
            row = flip(shard, mask | (1 << what)) * self.rows + shift
        spot = dst.at[at(row, size, 16), at(first + core * cols, cols, 128)]
        return self.sems.remote(spot, spot, flip(rep, 1), shard, self.ahead_slot[part])

    def together(self, part, stages, slot):
        rep, shard = lax.axis_index("rep"), lax.axis_index("shard")
        _, dst, first, cols = self.parts[part]
        size = sum(self.rows if step[2] else self.half for stage in stages for step in self.plan[part][stage])
        spot = dst.at[pl.ds(0, size), at(first + lax.rem(rep, 2) * cols, cols, 128)]
        return self.sems.remote(spot, spot, flip(rep, 1), shard, slot)

    def arrive(self, part, stage):
        self.together(part, [stage], (self.copy_send[part], self.stage_recv[part][stage])).wait_recv()

    def send(self, stage):
        for part in range(3):
            for step in self.plan[part][stage]:
                self.copy(part, step).start()

    def settle(self, stage):
        for part in range(3):
            self.arrive(part, stage)
            for step in self.plan[part][stage]:
                self.ahead(part, step).start()

    def move(self, stage):
        for part in range(3):
            self.arrive(part, stage)
            for step in self.plan[part][stage + 1]:
                self.copy(part, step).start()
            for step in self.plan[part][stage]:
                self.ahead(part, step).start()

    def finish(self):
        for part in range(3):
            self.together(part, range(self.stages), self.ahead_slot[part]).wait_recv()

    def drain(self):
        for part in range(3):
            slot = self.copy_send[part], self.stage_recv[part][0]
            self.together(part, range(self.stages), slot).wait_send()
            self.together(part, range(self.stages), self.ahead_slot[part]).wait_send()


def tail_orders(bits):
    rest = list(range(2, bits))
    cross = ["x", 0, 1] + rest
    other = ["x", 1, 0] + rest
    return (cross, cross, other, [0, "x", 1] + rest, other)


def beside_orders(bits):
    rest = list(range(2, bits))
    return (["x", 0, 1] + rest, [0, 1, "x"] + rest, [1, 0, "x"] + rest)


class Gathered:
    stages = 1

    def send(self, stage):
        pass

    settle = move = send

    def finish(self):
        pass

    drain = finish


def forward_kernel(count, *refs):
    (tokens, earlier, segs, vec, query_scale, w_qkv, w_out, w_up, w_down) = refs[:9]
    results = refs[9:26]
    alone = earlier is not None
    (
        output_hbm, acted_t_hbm, q_t_hbm, k_t_hbm, v_t_hbm, o_t_hbm, lse, hidden_hbm,
        inner_t_hbm, upper_hbm, lower_t_hbm, rows_out, qkv_hbm, out_hbm, up_hbm, down_hbm, mask_hbm,
    ) = results
    (
        seg_ext, vec_full, qkv, out, up, down, acted, acted_t, q_t, k_t, v_t, o_t, heads, inner,
        hidden, upper, inner_t, lower_t, mask, state_low, send, recv, lsem,
    ) = refs[26:]
    rep, shard = lax.axis_index("rep"), lax.axis_index("shard")
    length, width = tokens.shape
    total = 3 * length
    rows = w_qkv.shape[0]
    tiles = width // TILE
    own = pl.ds(total - length, length)
    sems = Sems(send, recv)
    lower, output = heads, inner
    bits = count.bit_length() - 1

    runs = [tiles * 2 // 5, tiles - tiles * 2 // 5]
    starts = [0, runs[0], tiles]
    wide_part = width // 5 // 128 * 128
    last_part = width // 2 - 2 * wide_part
    if alone:
        groups = [Gathered()] * 5
    else:
        groups = []
        for run, start in zip(runs, starts):
            parts = [(w_qkv, qkv, p * width + start * TILE, run * TILE // 2) for p in range(3)]
            groups.append(Doubling(sems, count, rows, stage_orders(bits) if start else cross_orders(bits), parts))
        for w, full in ((w_out, out), (w_up, up), (w_down, down)):
            parts = [(w, full, 0, wide_part), (w, full, 2 * wide_part, wide_part), (w, full, 4 * wide_part, last_part)]
            groups.append(Doubling(sems, count, rows, stage_orders(bits), parts))

    pairs = [(tokens, acted.at[own]), (tokens, state_low)]
    if alone:
        pairs += [(earlier, acted.at[pl.ds(0, 2 * length)]), (segs, seg_ext), (vec, vec_full)]
        pairs += [(w_qkv, qkv), (w_out, out), (w_up, up), (w_down, down)]
    else:
        mine = at(shard * rows, rows, 16)
        pairs += [(segs, seg_ext.at[2]), (vec, vec_full.at[shard])]
        pairs += [(w_qkv, qkv.at[mine]), (w_out, out.at[mine]), (w_up, up.at[mine]), (w_down, down.at[mine])]
    loads = [pltpu.make_async_copy(src, dst, lsem.at[i]) for i, (src, dst) in enumerate(pairs)]
    for copy in loads:
        copy.start()

    odd = lax.rem(shard, 2) == 1
    even = jnp.logical_not(odd)
    far_ok, far_got = shard < count - 2, shard >= 2
    buddy = flip(shard, 1)
    far_to = lax.rem(shard + 2, count)
    nchunk = HALO_CHUNKS
    part = length // nchunk
    far, near, relay, vecs = [], [], [], []
    for i in range(0 if alone else nchunk):
        here = pl.ds(i * part, part)
        far_spot, near_spot = acted.at[pl.ds(i * part, part)], acted.at[pl.ds(length + i * part, part)]
        slot = sems.slot()
        far.append(sems.remote(tokens.at[here], far_spot, rep, far_to, sems.slot()))
        near.append(sems.remote(tokens.at[here], near_spot, rep, buddy, slot))
        relay.append(sems.remote(far_spot, near_spot, rep, buddy, slot))
    if not alone:
        slot = sems.slot()
        far.append(sems.remote(segs, seg_ext.at[0], rep, far_to, sems.slot()))
        near.append(sems.remote(segs, seg_ext.at[1], rep, buddy, slot))
        relay.append(sems.remote(seg_ext.at[0], seg_ext.at[1], rep, buddy, slot))
        vecs = [
            sems.remote(vec, vec_full.at[shard], rep, lax.rem(shard + step, count), sems.slot()) for step in range(1, count)
        ]

    def far_start(*which):
        @pl.when(far_ok)
        def _():
            for i in which:
                far[i].start()

    def near_start(*which):
        @pl.when(even)
        def _():
            for i in which:
                near[i].start()

    def far_next(i):
        @pl.when(far_ok)
        def _():
            far[i].wait_send()
            far[i + 2].start()

    def near_next(i):
        @pl.when(even)
        def _():
            near[i].wait_send()
            near[i + 2].start()

    def relay_start(*which):
        @pl.when(far_got)
        def _():
            for i in which:
                far[i].wait_recv()

        @pl.when(odd & far_got)
        def _():
            for i in which:
                relay[i].start()

    if not alone:
        greet(count)
        groups[0].send(0)
        far_start(nchunk, 0, 1)
        near_start(nchunk, 0, 1)
        for copy in vecs:
            copy.start()
        groups[0].move(0)
        relay_start(nchunk)
        for i in range(nchunk):
            relay_start(i)
            if i + 2 < nchunk:
                far_next(i)
                near_next(i)
            if i == 0:
                groups[0].move(1)
            if i == 2:
                groups[0].move(2)
            if i == 6:
                groups[1].send(0)

    for copy in loads:
        copy.wait()
    for copy in vecs:
        copy.wait_recv()
    each = width // count
    lines = [jnp.concatenate([vec_full[i][j : j + 1, :] for j in range(-(-4 * each // 128))], axis=1) for i in range(count)]
    rows_out[...] = jnp.zeros_like(rows_out)
    for k in range(4):
        rows_out[k : k + 1, :] = jnp.concatenate([line[:, k * each : (k + 1) * each] for line in lines], axis=1)
    value = query_scale[...]
    soft = jnp.maximum(value, 0.0) + jnp.log(1.0 + jnp.exp(-jnp.abs(value)))
    rows_out[4:5, :] = jnp.concatenate([soft * (LOG2E / math.sqrt(HEAD) / LN2)] * (width // HEAD), axis=1)
    rows_out[5:6, 0:HEAD] = LN2 / (soft * (1.0 + jnp.exp(-value)))

    def norm_rows(i):
        sl = at(i * TILE, TILE, TILE)
        state = acted[sl, :].astype(F32)
        scale = lax.rsqrt(jnp.mean(state * state, axis=-1, keepdims=True) + EPS)
        value = (state * scale * rows_out[0:1, :]).astype(BF16)
        value = jnp.where(shard + i * TILE // length >= 2, value, jnp.zeros_like(value))
        acted[sl, :] = value
        acted_t[:, sl] = value.T

    def norm_step(i, carry):
        norm_rows(i)
        return carry

    per = length // TILE
    lax.fori_loop(2 * per, 3 * per, norm_step, 0)

    groups[0].settle(groups[0].stages - 1)
    groups[0].finish()

    def project_own(i, carry):
        sl = at(i * TILE, TILE, TILE)
        q_t[sl, :] = (mul(acted[own, :], qkv[:, sl]) * rows_out[4:5, sl]).astype(BF16).T
        k_t[sl, own] = mul(acted[own, :], qkv[:, at(width + i * TILE, TILE, TILE)]).astype(BF16).T
        v_t[sl, own] = mul(acted[own, :], qkv[:, at(2 * width + i * TILE, TILE, TILE)]).astype(BF16).T
        return carry

    def project_earlier(i, carry):
        sl = at(i * TILE, TILE, TILE)
        k_t[sl, before] = mul(acted[before, :], qkv[:, at(width + i * TILE, TILE, TILE)]).astype(BF16).T
        v_t[sl, before] = mul(acted[before, :], qkv[:, at(2 * width + i * TILE, TILE, TILE)]).astype(BF16).T
        return carry

    def project(i, carry):
        sl = at(i * TILE, TILE, TILE)
        q_t[sl, :] = (mul(acted[own, :], qkv[:, sl]) * rows_out[4:5, sl]).astype(BF16).T
        k_t[sl, :] = mul(acted[...], qkv[:, at(width + i * TILE, TILE, TILE)]).astype(BF16).T
        v_t[sl, :] = mul(acted[...], qkv[:, at(2 * width + i * TILE, TILE, TILE)]).astype(BF16).T
        return carry

    before = pl.ds(0, total - length)
    lax.fori_loop(0, runs[0], project_own, 0)
    keep = []

    def keep_more(*more):
        for src, dst in more:
            copy = pltpu.make_async_copy(src, dst, lsem.at[8 + len(keep)])
            copy.start()
            keep.append(copy)

    def keep_run(run):
        sizes = [pl.ds(p * width + starts[run] * TILE, runs[run] * TILE) for p in range(3)]
        keep_more(*[(qkv.at[:, size], qkv_hbm.at[:, size]) for size in sizes])

    keep_run(0)
    if not alone:

        @pl.when(odd)
        def _():
            for copy in near:
                copy.wait_recv()

        @pl.when(even & far_got)
        def _():
            for copy in relay:
                copy.wait_recv()

        @pl.when(odd & far_got)
        def _():
            for copy in relay:
                copy.wait_send()

    groups[1].move(0)
    lax.fori_loop(0, 2 * per, norm_step, 0)

    mine = seg_ext[2].astype(F32)
    for j in range(3):
        column = jnp.broadcast_to(seg_ext[j].astype(F32), (8, length)).T[:, 0:1]
        column = jnp.where(shard + j >= 2, column, -1.0)
        place = lax.broadcasted_iota(jnp.int32, (length, length), 0) + j * length
        lane = lax.broadcasted_iota(jnp.int32, (length, length), 1)
        near_by = (place > lane) & (place <= lane + WINDOW)
        mask[j * length : (j + 1) * length, :] = jnp.where(near_by & (column == mine), 0.0, MASKED)

    keep_more((acted_t, acted_t_hbm), (mask, mask_hbm))
    groups[1].move(1)
    for group in groups[2:]:
        group.send(0)
    lax.fori_loop(0, runs[0], project_earlier, 0)
    groups[1].move(2)

    half = length // 2

    def attend(h):
        sl = at(h * HEAD, HEAD, 16)
        key, query = k_t[sl, :].T, q_t[sl, :]
        first, last = pl.ds(0, half), pl.ds(total - half, half)
        middle = pl.ds(half, total - length)
        score_m = mul(key[half : total - half], query) + mask[middle, :]
        score_f = mul(key[:half], query[:, :half]) + mask[first, :half]
        score_l = mul(key[total - half :], query[:, half:]) + mask[last, half:]
        ends = [jnp.max(score, axis=0, keepdims=True) for score in (score_f, score_l)]
        top = jnp.maximum(jnp.max(score_m, axis=0, keepdims=True), jnp.concatenate(ends, axis=1))
        prob_m = jnp.exp2(score_m - top)
        prob_f = jnp.exp2(score_f - top[:, :half])
        prob_l = jnp.exp2(score_l - top[:, half:])
        ends = [jnp.sum(prob, axis=0, keepdims=True) for prob in (prob_f, prob_l)]
        norm = jnp.sum(prob_m, axis=0, keepdims=True) + jnp.concatenate(ends, axis=1)
        ends = [mul(v_t[sl, first], prob_f.astype(BF16)), mul(v_t[sl, last], prob_l.astype(BF16))]
        mixed = mul(v_t[sl, middle], prob_m.astype(BF16)) + jnp.concatenate(ends, axis=1)
        o_t[sl, :] = (mixed * (1.0 / norm)).astype(BF16)
        lse[h] = top + jnp.log2(norm)

    pairs = [start * TILE // HEAD // 2 for start in starts]
    last = groups[0].stages - 1

    def steps(index, table):
        for number, actions in table.items():

            @pl.when(index == number)
            def _():
                for group, what in actions:
                    if what == "send":
                        groups[group].send(0)
                    elif what == "settle":
                        groups[group].settle(last)
                    else:
                        groups[group].move(what)

    def attend_run(first, stop, table):
        def attend_pair(pair, carry):
            attend(2 * pair)
            attend(2 * pair + 1)
            steps(pair, table)
            return carry

        lax.fori_loop(first, stop, attend_pair, 0)

    def project_run(first, stop, table):
        def project_step(i, carry):
            project(i, carry)
            steps(i, table)
            return carry

        lax.fori_loop(first, stop, project_step, 0)

    attend_run(0, pairs[1], {pairs[1] - 2: [(2, 0), (3, 0), (4, 0)], pairs[1] - 1: [(1, "settle")]})
    groups[1].finish()
    keep_run(1)
    project_run(starts[1], starts[2], {starts[1]: [(2, 1), (3, 1), (4, 1)]})
    keep_more((q_t, q_t_hbm), (k_t, k_t_hbm), (v_t, v_t_hbm))
    attend_run(
        pairs[1], pairs[2],
        {pairs[1]: [(2, 2), (3, 2)], pairs[2] - 2: [(2, "settle"), (4, 2)]},
    )

    keep_more((o_t, o_t_hbm))

    def turn(i, carry):
        sl = at(i * TILE, TILE, TILE)
        heads[:, sl] = o_t[sl, :].T
        return carry

    lax.fori_loop(0, tiles, turn, 0)
    groups[2].finish()
    keep_more((out, out_hbm))

    def out_step(i, carry):
        sl = at(i * TILE, TILE, TILE)
        hidden[:, sl] = state_low[:, sl].astype(F32) + mul(heads[...], out[:, sl])
        return carry

    lax.fori_loop(0, tiles, out_step, 0)
    keep_more((hidden, hidden_hbm))

    def norm_two(i, carry):
        sl = at(i * TILE, TILE, TILE)
        value = hidden[sl, :]
        scale = lax.rsqrt(jnp.mean(value * value, axis=-1, keepdims=True) + EPS)
        normed = (value * scale * rows_out[1:2, :]).astype(BF16)
        inner[sl, :] = normed
        inner_t[:, sl] = normed.T
        return carry

    lax.fori_loop(0, length // TILE, norm_two, 0)
    keep_more((inner_t, inner_t_hbm))

    groups[3].settle(last)
    groups[3].finish()
    keep_more((up, up_hbm))

    def up_step(i, carry):
        sl = at(i * TILE, TILE, TILE)
        value = mul(inner[...], up[:, sl]) + rows_out[2:3, sl]
        upper[:, sl] = value
        act = (value / (1.0 + jnp.exp(-value))).astype(BF16)
        lower[:, sl] = act
        lower_t[sl, :] = act.T
        return carry

    lax.fori_loop(0, tiles, up_step, 0)
    keep_more((upper, upper_hbm), (lower_t, lower_t_hbm))

    groups[4].settle(last)
    groups[4].finish()
    keep_more((down, down_hbm))

    def down_step(i, carry):
        sl = at(i * TILE, TILE, TILE)
        output[:, sl] = (hidden[:, sl] + (mul(lower[...], down[:, sl]) + rows_out[3:4, sl])).astype(BF16)
        return carry

    lax.fori_loop(0, tiles, down_step, 0)
    keep_more((output, output_hbm))

    if not alone:

        @pl.when(far_ok)
        def _():
            for copy in far[nchunk - 2 :]:
                copy.wait_send()

        @pl.when(even)
        def _():
            for copy in near[nchunk - 2 :]:
                copy.wait_send()

    for copy in vecs:
        copy.wait_send()
    for group in groups:
        group.drain()
    for copy in keep:
        copy.wait()


def forward(count, tokens, earlier, segs, vec, query_scale, w_qkv, w_out, w_up, w_down):
    length, width = tokens.shape
    total = 3 * length
    heads = width // HEAD
    bits = count.bit_length() - 1
    sends = recvs = 1
    if earlier is None:
        single = 2 * (HALO_CHUNKS + 1) + count - 1
        sends, recvs = 5 * 6 + single, 5 * 3 * (bits + 2) + single
    inputs = [x for x in (tokens, earlier, segs, vec, query_scale, w_qkv, w_out, w_up, w_down) if x is not None]
    if earlier is None:
        params = pltpu.CompilerParams(collective_id=0, has_side_effects=True, vmem_limit_bytes=VMEM_LIMIT)
    else:
        params = pltpu.CompilerParams(vmem_limit_bytes=VMEM_LIMIT)
    shape = jax.ShapeDtypeStruct
    outs = (
        shape((length, width), BF16),
        shape((width, total), BF16),
        shape((width, length), BF16),
        shape((width, total), BF16),
        shape((width, total), BF16),
        shape((width, length), BF16),
        shape((heads, 1, length), F32),
        shape((length, width), F32),
        shape((width, length), BF16),
        shape((length, width), F32),
        shape((width, length), BF16),
        shape((8, width), F32),
        shape((width, 3 * width), BF16),
        shape((width, width), BF16),
        shape((width, width), BF16),
        shape((width, width), BF16),
        shape((total, length), F32),
    )
    specs = [ANY] * 17
    specs[6] = specs[11] = VM
    buffer = pltpu.VMEM
    return pl.pallas_call(
        functools.partial(forward_kernel, count) if earlier is not None else lambda *refs: forward_kernel(count, refs[0], None, *refs[1:]),
        name="forward_layer",
        out_shape=outs,
        in_specs=[ANY] * (len(inputs) - 5) + [VM] + [ANY] * 4,
        out_specs=tuple(specs),
        scratch_shapes=[
            buffer((3,) + segs.shape[-2:], jnp.int32),
            buffer((count,) + vec.shape[-2:], F32),
            buffer((width, 3 * width), BF16),
            buffer((width, width), BF16),
            buffer((width, width), BF16),
            buffer((width, width), BF16),
            buffer((total, width), BF16),
            buffer((width, total), BF16),
            buffer((width, length), BF16),
            buffer((width, total), BF16),
            buffer((width, total), BF16),
            buffer((width, length), BF16),
            buffer((length, width), BF16),
            buffer((length, width), BF16),
            buffer((length, width), F32),
            buffer((length, width), F32),
            buffer((width, length), BF16),
            buffer((width, length), BF16),
            buffer((total, length), F32),
            buffer((length, width), BF16),
            pltpu.SemaphoreType.DMA((sends,)),
            pltpu.SemaphoreType.DMA((recvs,)),
            pltpu.SemaphoreType.DMA((28,)),
        ],
        compiler_params=params,
    )(*inputs)


class Halving:
    def __init__(self, sems, credits, count, rows, orders, acc, other, land, result, reused):
        self.sems, self.credits, self.rows, self.half, self.reused = sems, credits, rows, rows // 2, reused
        self.acc, self.other, self.land, self.result = acc, other, land, result
        self.bits = count.bit_length() - 1
        self.plan, self.core_slot, self.cross_slot, self.share_slot = [], [], [], []
        self.stage_send, self.stage_recv = [], []
        self.at_stage = [0] * len(orders)
        for order in orders:
            left, whole, base, stages = list(range(self.bits)), True, 0, []
            for what in order:
                steps = []
                if what == "x":
                    whole = False
                else:
                    left.remove(what)
                for mask in span(left):
                    size = rows if whole else self.half
                    steps.append((mask, base, size, len(stages)))
                    base += size
                stages.append((what, whole, steps))
            self.plan.append(stages)
            self.core_slot.append(sems.slot())
            self.cross_slot.append(sems.slot())
            self.share_slot.append(sems.slot())
            self.stage_send.append(sems.send_slot())
            self.stage_recv.append([sems.recv_slot() for _ in order])

    def partner(self, what):
        rep, shard = lax.axis_index("rep"), lax.axis_index("shard")
        if what == "core":
            return flip(rep, 1), shard
        if what == "x":
            return flip(rep, 2), shard
        return rep, flip(shard, 1 << what)

    def credit(self, part, what):
        place = 0 if what == "core" else 1 if what == "x" else 2 + what
        return self.credits.at[part * (self.bits + 2) + place]

    def allow(self, part, what):
        rep, shard = self.partner(what)
        pl.semaphore_signal(
            self.credit(part, what), inc=1, device_id={"rep": rep, "shard": shard}, device_id_type=MESH
        )

    def core_copy(self, part):
        return self.sems.remote(self.other[part], self.land[part], *self.partner("core"), self.core_slot[part])

    def core_send(self, part):
        if self.reused:
            pl.semaphore_wait(self.credit(part, "core"), 1)
        self.core_copy(part).start()

    def core_add(self, part):
        self.core_copy(part).wait_recv()
        acc, land = self.acc[part], self.land[part]

        def step(i, carry):
            sl = at(i * TILE, TILE, TILE)
            acc[sl, :] = (acc[sl, :].astype(F32) + land[sl, :].astype(F32)).astype(BF16)
            return carry

        lax.fori_loop(0, acc.shape[0] // TILE, step, 0)
        for what, _, _ in self.plan[part]:
            self.allow(part, what)
        self.send(part, 0)

    def copy(self, part, stage, step):
        what, whole, _ = self.plan[part][stage]
        mask, base, size, _ = step
        slot = self.stage_send[part], self.stage_recv[part][stage]
        shard, cross = lax.axis_index("shard"), lax.div(lax.axis_index("rep"), 2)
        if what == "x":
            row = flip(shard, mask) * self.rows + (1 - cross) * self.half
        else:
            row = flip(shard, mask | (1 << what)) * self.rows
            row = row if whole else row + cross * self.half
        src = self.acc[part].at[at(row, size, 16)]
        return self.sems.remote(src, self.land[part].at[pl.ds(base, size)], *self.partner(what), slot)

    def send(self, part, stage):
        what, _, steps = self.plan[part][stage]
        pl.semaphore_wait(self.credit(part, what), 1)
        for step in steps:
            self.copy(part, stage, step).start()

    def receive(self, part, stage):
        what, whole, steps = self.plan[part][stage]
        shard, cross = lax.axis_index("shard"), lax.div(lax.axis_index("rep"), 2)
        slot = self.stage_send[part], self.stage_recv[part][stage]
        spot = self.land[part].at[pl.ds(steps[0][1], sum(step[2] for step in steps))]
        self.sems.remote(spot, spot, *self.partner(what), slot).wait_recv()
        for mask, base, size, _ in steps:
            row = flip(shard, mask) * self.rows
            row = row if whole else row + cross * self.half
            sl = at(row, size, 16)
            new = self.acc[part][sl, :].astype(F32) + self.land[part][pl.ds(base, size), :].astype(F32)
            self.acc[part][sl, :] = new.astype(BF16)

    def advance(self, part):
        stage = self.at_stage[part]
        self.at_stage[part] += 1
        if stage <= self.bits:
            self.receive(part, stage)
        if stage < self.bits:
            self.send(part, stage + 1)
        elif stage == self.bits:
            core, cross = self.sides()
            shard = lax.axis_index("shard")
            row = shard * self.rows + cross * self.half
            self.result[part].at[core][at(cross * self.half, self.half, 16), :] = self.acc[part][at(row, self.half, 16), :]
            self.cross_copy(part).start()
        elif stage == self.bits + 1:
            self.cross_copy(part).wait_recv()
            self.share_copy(part).start()
        else:
            self.share_copy(part).wait_recv()

    def sides(self):
        rep = lax.axis_index("rep")
        return lax.rem(rep, 2), lax.div(rep, 2)

    def cross_copy(self, part):
        core, cross = self.sides()
        spot = self.result[part].at[core, at(cross * self.half, self.half, 16)]
        return self.sems.remote(spot, spot, *self.partner("x"), self.cross_slot[part])

    def share_copy(self, part):
        core, _ = self.sides()
        spot = self.result[part].at[core]
        return self.sems.remote(spot, spot, *self.partner("core"), self.share_slot[part])

    def drain_other(self, part):
        self.core_copy(part).wait_send()

    def drain_acc(self, part):
        size = sum(step[2] for _, _, steps in self.plan[part] for step in steps)
        spot = self.acc[part].at[pl.ds(0, size)]
        slot = self.stage_send[part], self.stage_recv[part][0]
        self.sems.remote(spot, spot, *self.partner("core"), slot).wait_send()

    def drain_result(self, part):
        self.cross_copy(part).wait_send()
        self.share_copy(part).wait_send()


def backward_kernel(count, alone, *refs):
    (
        cot_hbm, tokens_hbm, hidden_hbm, inner_t_hbm, upper_hbm, lower_t_hbm, o_t_hbm, q_t_hbm, k_t_hbm, v_t_hbm,
        acted_t_hbm, qkv_hbm, out_hbm, up_hbm, down_hbm, mask_hbm, lse, rows_in,
    ) = refs[:18]
    if alone:
        (hidden_out, qkv_out, out_out, up_out, down_out, acted_out, small_out) = refs[18:25]
    else:
        (input_grad, qkv_out, out_out, up_out, down_out, small_out) = refs[18:24]
    scratch = refs[25:] if alone else refs[24:]
    (
        wide, flat, wtile, first_f32, grad_hidden, q_t, k_t, v_t, do_t, delta, mask, scale_sum, acc, other, land,
        result_ff, result_qkv, factor, near_in, far_in, state_low, small_now, small_in, lsem, send, recv, credits,
    ) = scratch
    rep, shard = lax.axis_index("rep"), lax.axis_index("shard")
    core = lax.rem(rep, 2)
    length, width = cot_hbm.shape
    total = 3 * length
    tiles = width // TILE
    rows = width // count
    cols = width // 2
    heads = width // HEAD
    own = pl.ds(total - length, length)
    bits = count.bit_length() - 1
    sems = Sems(send, recv)
    lower_t, inner_t, o_t = (wide.at[:, pl.ds(i * length, length)] for i in range(3))
    cot, grad_upper, grad_attn = (flat.at[i] for i in range(3))
    parts = [[ref.at[i] for i in range(3)] for ref in (acc, other, land, result_ff, result_qkv)]

    def local(src, dst, slot):
        return pltpu.make_async_copy(src, dst, lsem.at[slot])

    loads = {
        "cot": local(cot_hbm, cot, 0),
        "lower": local(lower_t_hbm, lower_t, 1),
        "upper": local(upper_hbm, first_f32, 2),
        "inner": local(inner_t_hbm, inner_t, 3),
        "o": local(o_t_hbm, o_t, 4),
        "q": local(q_t_hbm, q_t, 5),
        "k": local(k_t_hbm, k_t, 6),
        "v": local(v_t_hbm, v_t, 7),
        "mask": local(mask_hbm, mask, 8),
        "state": local(tokens_hbm, state_low, 9),
    }
    load_hidden = local(hidden_hbm, first_f32, 10)
    load_acted = local(acted_t_hbm, wide, 11)

    def tile_copy(src, order, i):
        slot = lax.rem(order * tiles + i, 6)
        return local(src.at[at(i * TILE, TILE, TILE)], wtile.at[slot], 12 + slot)

    def wide_copies(i):
        first = 3 * (i % 2)
        return [
            local(qkv_hbm.at[pl.ds(i * TILE, TILE), pl.ds(k * width, width)], wtile.at[first + k], 12 + first + k)
            for k in range(3)
        ]

    def tile_next(src, after, order, i):
        tile_copy(src, order, i).wait()
        if after is not None:
            tile_copy(after, order + 1, i).start()
        return lax.rem(order * tiles + i, 6)

    for name in ("lower", "cot"):
        loads[name].start()
    loads["upper"].start()
    for i in range(tiles):
        tile_copy(down_hbm, 0, i).start()
    for name in ("inner", "o"):
        loads[name].start()
    if alone:
        ff = qkv = None
    else:
        greet(count)
        ff = Halving(sems, credits.at[0], count, rows, beside_orders(bits), *parts[:4], False)
        cut = cols * 3 // 5 // 128 * 128
        runs = ((0, 0, cols), (1, 0, cut), (1, cut, cols - cut), (2, 0, cut), (2, cut, cols - cut))
        back = [[ref.at[2 - m, :, pl.ds(at_col, size)] for m, at_col, size in runs] for ref in (acc, other, land)]
        ends = [result_qkv.at[m, :, :, pl.ds(at_col, size)] for m, at_col, size in runs]
        qkv = Halving(sems, credits.at[1], count, rows, tail_orders(bits), *back, ends, True)
    copies_out = []

    def group_parts(first_use, part):
        return (part,) if first_use else ((0,), (1, 2), (3, 4))[part]

    def weight_side(group, part, left, right, side_core, first_use=False):
        theirs = side_core is not core
        dest = (other if theirs else acc).at[part if first_use else 2 - part]

        def step(i, carry):
            sl = at(i * cols, cols, 16)
            dest[sl, :] = right(left(sl), side_core * cols).astype(BF16)
            return carry

        lax.fori_loop(0, 2, step, 0)
        if theirs and group is not None:
            for run in group_parts(first_use, part):
                group.core_send(run)

    def weight_out(part, target, first, first_use=False):
        for ref, side_core in ((other, 1 - core), (acc, core)):
            copy = local(ref.at[part if first_use else 2 - part], target.at[:, at(first + side_core * cols, cols, 128)], 20 + len(copies_out))
            copy.start()
            copies_out.append(copy)

    def weight_grad(group, part, left, right, target):
        weight_side(group, part, left, right, 1 - core, True)
        weight_side(group, part, left, right, core, True)
        if alone:
            weight_out(part, target, 0, True)

    small_now[0] = jnp.zeros_like(small_now[0])
    loads["lower"].wait()
    loads["cot"].wait()
    weight_grad(
        ff, 2, lambda sl: lower_t[sl, :], lambda left, col: mul(left, cot[:, at(col, cols, 128)]), down_out
    )
    loads["upper"].wait()

    def down_step(i, carry):
        sl = at(i * TILE, TILE, TILE)
        slot = tile_next(down_hbm, up_hbm, 0, i)
        grad_lower = mul(cot[...], wtile[slot], 1, 1)
        value = first_f32[:, sl]
        gate = 1.0 / (1.0 + jnp.exp(-value))
        grad = (grad_lower * (gate + value * gate * (1.0 - gate))).astype(BF16)
        grad_upper[:, sl] = grad
        small_now[0, 2:3, sl] = jnp.sum(grad.astype(F32), axis=0, keepdims=True)
        small_now[0, 3:4, sl] = jnp.sum(cot[:, sl].astype(F32), axis=0, keepdims=True)
        return carry

    lax.fori_loop(0, tiles, down_step, 0)
    load_hidden.start()
    for name in ("q", "k", "v", "mask", "state"):
        loads[name].start()
    loads["inner"].wait()
    weight_grad(
        ff, 1, lambda sl: inner_t[sl, :], lambda left, col: mul(left, grad_upper[:, at(col, cols, 128)]), up_out
    )
    if not alone:
        ff.core_add(2)

    def up_step(i, carry):
        sl = at(i * TILE, TILE, TILE)
        slot = tile_next(up_hbm, out_hbm, 1, i)
        grad_hidden[:, sl] = mul(grad_upper[...], wtile[slot], 1, 1)
        return carry

    lax.fori_loop(0, tiles, up_step, 0)
    load_hidden.wait()
    if not alone:
        ff.core_add(1)

    def norm_step(i, carry):
        sl = at(i * TILE, TILE, TILE)
        value = first_f32[sl, :]
        scale = lax.rsqrt(jnp.mean(value * value, axis=-1, keepdims=True) + EPS)
        normed = value * scale
        grad = grad_hidden[sl, :]
        small_now[0, 1:2, :] += jnp.sum(grad * normed, axis=0, keepdims=True)
        weighted = grad * rows_in[1:2, :]
        along = jnp.mean(weighted * normed, axis=-1, keepdims=True)
        whole = cot[sl, :].astype(F32) + scale * (weighted - normed * along)
        grad_hidden[sl, :] = whole
        grad_attn[sl, :] = whole.astype(BF16)
        return carry

    lax.fori_loop(0, length // TILE, norm_step, 0)
    loads["o"].wait()
    weight_grad(
        ff, 0, lambda sl: o_t[sl, :], lambda left, col: mul(left, grad_attn[:, at(col, cols, 128)]), out_out
    )

    def out_step(i, carry):
        sl = at(i * TILE, TILE, TILE)
        slot = tile_next(out_hbm, None, 2, i)
        do_t[sl, :] = mul(grad_attn[...], wtile[slot], 1, 1).astype(BF16).T
        return carry

    lax.fori_loop(0, tiles, out_step, 0)
    if not alone:
        ff.core_add(0)

    def delta_step(h, carry):
        sl = at(h * HEAD, HEAD, 16)
        delta[h] = jnp.sum(o_t[sl, :].astype(F32) * do_t[sl, :].astype(F32), axis=0, keepdims=True)
        return carry

    lax.fori_loop(0, heads, delta_step, 0)
    load_acted.start()
    for i in range(2):
        for copy in wide_copies(i):
            copy.start()
    for name in ("q", "k", "v", "mask"):
        loads[name].wait()
    scale_sum[...] = jnp.zeros_like(scale_sum)
    factor[...] = jnp.broadcast_to(rows_in[4:5, 0:HEAD] * LN2, (128, HEAD)).T
    half = length // 2
    pieces = (
        (0, half, (0,)),
        (half, length, (0, 1)),
        (half + length, length, (0, 1)),
        (total - half, half, (1,)),
    )

    def attend(h, carry):
        sl = at(h * HEAD, HEAD, 16)
        query, grad = q_t[sl, :], do_t[sl, :]
        parts_dq = [jnp.zeros((HEAD, half), F32)] * 2
        for first, size, sides in pieces:
            ks, qs = pl.ds(first, size), slice(sides[0] * half, (sides[-1] + 1) * half)
            key, value = k_t[sl, ks], v_t[sl, ks]
            query_part, grad_part = query[:, qs], grad[:, qs]
            probs = jnp.exp2(mul(key.T, query_part) + mask[ks, qs] - lse[h][:, qs])
            scores = (probs * (mul(value.T, grad_part) - delta[h][:, qs])).astype(BF16)
            v_t[sl, ks] = mul(grad_part, probs.astype(BF16), 1, 1).astype(BF16)
            k_t[sl, ks] = (mul(query_part, scores, 1, 1) * LN2).astype(BF16)
            term = mul(key, scores)
            for place, side in enumerate(sides):
                parts_dq[side] = parts_dq[side] + term[:, place * half : (place + 1) * half]
        dq = jnp.concatenate(parts_dq, axis=1)
        scale_sum[...] += dq * query.astype(F32)
        q_t[sl, :] = (dq * factor[:, 0:1]).astype(BF16)
        if not alone:
            for head in sorted({step[0] for step in FF_STEPS}):

                @pl.when(h == head)
                def _():
                    for _, part, stage in [step for step in FF_STEPS if step[0] == head]:
                        ff.at_stage[part] = stage
                        ff.advance(part)
                        if stage == bits:
                            for run in group_parts(False, 2 - part):
                                qkv.allow(run, "core")

        return carry

    lax.fori_loop(0, heads, attend, 0)

    def give_result(group, part, target, first):
        for side in range(2):
            src = (result_ff if group is ff else result_qkv).at[part, side]
            copy = local(src, target.at[:, pl.ds(first + side * cols, cols)], 20 + len(copies_out))
            copy.start()
            copies_out.append(copy)

    load_acted.wait()
    odd = lax.rem(shard, 2) == 1
    even = jnp.logical_not(odd)
    far_ok, far_got = shard >= 2, shard < count - 2
    buddy = flip(shard, 1)
    far_to = lax.rem(shard + count - 2, count)
    give_slots = [sems.slot() for _ in range(tiles)]
    far_slots = [sems.slot() for _ in range(tiles)]

    def give(i):
        sl = pl.ds(i * TILE, TILE)
        return sems.remote(flat.at[1, :, sl], near_in.at[:, sl], rep, buddy, give_slots[i])

    def far(i):
        sl = pl.ds(i * TILE, TILE)
        return sems.remote(flat.at[0, :, sl], far_in.at[:, sl], rep, far_to, far_slots[i])

    def state_step(i):
        sl = pl.ds(i * TILE, TILE)
        for copy in wide_copies(i):
            copy.wait()
        slot = 3 * (i % 2)
        both = mul(wtile[slot + 1], k_t[...]) + mul(wtile[slot + 2], v_t[...])
        mine = both[:, total - length :] + mul(wtile[slot], q_t[...])
        both = jnp.concatenate([both[:, : total - length], mine], axis=1)
        low = both.astype(BF16)
        sums = jnp.sum(both * wide[sl, :].astype(F32), axis=1, keepdims=True)
        small_now[0, 0:1, sl] = jnp.broadcast_to(sums, (TILE, 128)).T[0:1, :] / rows_in[0:1, sl]
        for j in range(3):
            flat[j, :, sl] = low[:, j * length : (j + 1) * length].T
        if i + 2 < tiles:
            for copy in wide_copies(i + 2):
                copy.start()

    def give_start(i):
        @pl.when(odd | far_ok)
        def _():
            give(i).start()

    def far_start(i):
        @pl.when(even | far_ok)
        def _():
            give(i).wait_recv()

        @pl.when(odd & far_ok)
        def _():
            sl = pl.ds(i * TILE, TILE)
            flat[0, :, sl] = (flat[0, :, sl].astype(F32) + near_in[:, sl].astype(F32)).astype(BF16)

        @pl.when(far_ok)
        def _():
            far(i).start()

    if alone:
        for copy in copies_out:
            copy.wait()
    else:
        ff.at_stage = [max([step[2] + 1 for step in FF_STEPS if step[1] == part]) for part in range(3)]
        for part in (1, 2):
            ff.drain_other(part)
            ff.drain_acc(part)
    for side_core in (1 - core, core):
        weight_side(
            qkv, 0, lambda sl: wide[sl, own], lambda left, col: mul(left, q_t[at(col, cols, 16), :], 1, 1), side_core
        )
    for i in range(tiles):
        state_step(i)
        if alone:
            continue
        give_start(i)
        if i == 0:
            qkv.core_add(0)
            ff.advance(0)
        if i == 4:
            far_start(0)
    spread = jnp.sum(scale_sum[...], axis=1, keepdims=True)
    small_now[0, 4:5, 0:HEAD] = jnp.broadcast_to(spread, (HEAD, 128)).T[0:1, :]
    partners = ("core", "x") + tuple(range(bits))
    small_slots = [sems.slot() for _ in partners]

    def small_copy(number):
        return sems.remote(
            small_now.at[number], small_in.at[number], *ff.partner(partners[number]), small_slots[number]
        )

    def small_step(number):
        small_copy(number).wait()
        small_now[number + 1] = small_now[number] + small_in[number]
        if number + 1 < len(partners):
            small_copy(number + 1).start()

    if not alone:
        small_copy(0).start()
        ff.advance(0)
        for run in group_parts(False, 2):
            qkv.allow(run, "core")
        far_start(1)
    weight_side(qkv, 1, lambda sl: wide[sl, :], lambda left, col: mul(left, k_t[at(col, cols, 16), :], 1, 1), 1 - core)
    if not alone:
        far_start(2)
        small_step(0)
    weight_side(qkv, 1, lambda sl: wide[sl, :], lambda left, col: mul(left, k_t[at(col, cols, 16), :], 1, 1), core)
    if not alone:
        ff.drain_other(0)
        ff.drain_acc(0)
        qkv.core_add(1)
        qkv.core_add(2)
        qkv.advance(0)
        far_start(3)
        small_step(1)
    weight_side(qkv, 2, lambda sl: wide[sl, :], lambda left, col: mul(left, v_t[at(col, cols, 16), :], 1, 1), 1 - core)
    if not alone:
        far_start(4)
    weight_side(qkv, 2, lambda sl: wide[sl, :], lambda left, col: mul(left, v_t[at(col, cols, 16), :], 1, 1), core)
    if alone:
        for part in range(3):
            weight_out(part, qkv_out, part * width)
    if alone:
        small_out[...] = small_now[0]
        tail = [local(grad_hidden, hidden_out, 18), local(flat, acted_out, 19)]
        for copy in tail:
            copy.start()
        loads["state"].wait()
        for copy in tail + copies_out[6:]:
            copy.wait()
        return

    qkv.core_add(3)
    qkv.core_add(4)
    small_step(2)

    def round_robin(*order):
        for part in order:
            qkv.advance(part)

    round_robin(0, 2, 1)
    round_robin(4, 3)
    ff.advance(0)
    for part, target in enumerate((out_out, up_out, down_out)):
        ff.advance(part)
        give_result(ff, part, target, 0)
    small_step(3)
    round_robin(0, 2, 1)
    round_robin(4, 3)

    loads["state"].wait()
    for i in range(tiles):

        @pl.when(far_got)
        def _():
            far(i).wait_recv()


    def final_step(i, carry):
        sl = at(i * 128, 128, 128)
        state = state_low[sl, :].astype(F32)
        inverse = lax.rsqrt(jnp.mean(state * state, axis=-1, keepdims=True) + EPS)
        normed = state * inverse
        grad = flat[2, sl, :].astype(F32)
        grad += jnp.where(even, near_in[sl, :].astype(F32), 0.0)
        grad += jnp.where(far_got, far_in[sl, :].astype(F32), 0.0)
        weighted = grad * rows_in[0:1, :]
        along = jnp.mean(weighted * normed, axis=-1, keepdims=True)
        state_low[sl, :] = (grad_hidden[sl, :] + inverse * (weighted - normed * along)).astype(BF16)
        return carry

    lax.fori_loop(0, length // 128, final_step, 0)
    write = local(state_low, input_grad, 18)
    write.start()
    for number in range(4, len(partners)):
        small_step(number)
    last = len(partners)
    small_out[...] = jnp.zeros_like(small_out)
    for place in range(count):

        @pl.when(shard == place)
        def _():
            small_out[0:4, 0:rows] = small_now[last, 0:4, place * rows : (place + 1) * rows]

    small_out[4:5, 0:HEAD] = small_now[last, 4:5, 0:HEAD] * rows_in[5:6, 0:HEAD]
    while min(qkv.at_stage) <= bits + 2:
        round_robin(*[part for part in (0, 2, 1, 4, 3) if qkv.at_stage[part] <= bits + 2])
    for part in range(3):
        give_result(qkv, part, qkv_out, part * width)

    for i in range(tiles):

        @pl.when(odd | far_ok)
        def _():
            give(i).wait_send()

        @pl.when(far_ok)
        def _():
            far(i).wait_send()

    for part in range(5):
        qkv.drain_other(part)
        qkv.drain_acc(part)
        qkv.drain_result(part)
    for part in range(3):
        ff.drain_result(part)
    for copy in copies_out:
        copy.wait()
    write.wait()


FF_STEPS = (
    (2, 2, 0), (4, 1, 0), (7, 2, 1), (8, 1, 1), (9, 2, 2), (10, 0, 0),
    (11, 1, 2), (12, 2, 3), (13, 1, 3), (14, 0, 1), (15, 2, 4), (15, 1, 4),
)


def backward(count, alone, *inputs):
    length, width = inputs[0].shape
    total = 3 * length
    rows = width // count
    cols = width // 2
    heads = width // HEAD
    bits = count.bit_length() - 1
    sends = recvs = 1
    if not alone:
        single = 2 * (width // TILE) + bits + 2
        sends, recvs = 8 * 4 + single, 8 * (bits + 4) + single
    shape = jax.ShapeDtypeStruct
    if alone:
        outs = (
            shape((length, width), F32),
            shape((width, 3 * width), BF16),
            shape((width, width), BF16),
            shape((width, width), BF16),
            shape((width, width), BF16),
            shape((3, length, width), BF16),
            shape((8, width), F32),
        )
        params = pltpu.CompilerParams(vmem_limit_bytes=VMEM_LIMIT)
    else:
        outs = (
            shape((length, width), BF16),
            shape((rows, 3 * width), BF16),
            shape((rows, width), BF16),
            shape((rows, width), BF16),
            shape((rows, width), BF16),
            shape((8, 256), F32),
        )
        params = pltpu.CompilerParams(collective_id=1, has_side_effects=True, vmem_limit_bytes=VMEM_LIMIT)
    buffer = pltpu.VMEM
    return pl.pallas_call(
        functools.partial(backward_kernel, count, alone),
        name="backward_layer",
        out_shape=outs,
        in_specs=[ANY] * 16 + [VM] * 2,
        out_specs=(ANY,) * (len(outs) - 1) + (VM,),
        scratch_shapes=[
            buffer((width, total), BF16),
            buffer((3, length, width), BF16),
            buffer((6, TILE, width), BF16),
            buffer((length, width), F32),
            buffer((length, width), F32),
            buffer((width, length), BF16),
            buffer((width, total), BF16),
            buffer((width, total), BF16),
            buffer((width, length), BF16),
            buffer((heads, 1, length), F32),
            buffer((total, length), F32),
            buffer((HEAD, length), F32),
            buffer((3, width, cols), BF16),
            buffer((3, width, cols), BF16),
            buffer((3, width, cols), BF16),
            buffer((3, 2, rows, cols), BF16),
            buffer((3, 2, rows, cols), BF16),
            buffer((HEAD, 128), F32),
            buffer((length, width), BF16),
            buffer((length, width), BF16),
            buffer((length, width), BF16),
            buffer((bits + 3, 8, width), F32),
            buffer((bits + 2, 8, width), F32),
            pltpu.SemaphoreType.DMA((32,)),
            pltpu.SemaphoreType.DMA((sends,)),
            pltpu.SemaphoreType.DMA((recvs,)),
            pltpu.SemaphoreType.REGULAR((2, 5 * (bits + 2))),
        ],
        compiler_params=params,
    )(*inputs)


def finish_kernel(*refs):
    small = refs[6]
    for src, dst in zip(refs[:6], refs[7:13]):
        dst[...] = src[...].astype(dst.dtype)
    for row, dst in enumerate(refs[13:]):
        dst[...] = small[row, 0 : dst.shape[0]]


def finish(small, *arrays):
    shape = jax.ShapeDtypeStruct
    outs = [shape(array.shape, F32 if place < 4 else array.dtype) for place, array in enumerate(arrays)]
    specs = [pl.BlockSpec((array.shape[0] // 2, array.shape[1]), lambda i: (i, 0)) for array in arrays]
    lines = [arrays[0].shape[0]] * 4 + [HEAD]
    outs += [shape((line,), F32) for line in lines]
    line_specs = [pl.BlockSpec((line,), lambda i: (0,)) for line in lines]
    return pl.pallas_call(
        finish_kernel,
        name="finish",
        grid=(2,),
        out_shape=tuple(outs),
        in_specs=specs + [pl.BlockSpec(small.shape, lambda i: (0, 0))],
        out_specs=tuple(specs + line_specs),
        compiler_params=pltpu.CompilerParams(vmem_limit_bytes=VMEM_LIMIT),
    )(*arrays, small)


def shifted(value, steps):
    count = lax.axis_size("shard")
    first, last = (max(0, -steps), min(count, count - steps))
    return lax.ppermute(value, "shard", [(source, source + steps) for source in range(first, last)])


def gather_plain(tokens, segs, vec, *weights):
    whole = tuple(lax.all_gather(weight, "shard", axis=0, tiled=True) for weight in weights)
    earlier = jnp.concatenate([shifted(tokens, 2), shifted(tokens, 1)])
    seg_ext = jnp.stack([shifted(segs, 2), shifted(segs, 1), segs])
    return (earlier, seg_ext, lax.all_gather(vec, "shard", axis=0)) + whole


def reduce_plain(qkv_grad, out_grad, up_grad, down_grad, grad_acted, small):
    owned = []
    for grad in (qkv_grad, out_grad, up_grad, down_grad):
        part = lax.psum_scatter(grad, "shard", scatter_dimension=0, tiled=True)
        owned.append(lax.psum(part, "rep").astype(F32))
    parts = [grad_acted[2], shifted(grad_acted[0], -2), shifted(grad_acted[1], -1)]
    return (*owned, sum(part.astype(F32) for part in parts), lax.psum(small, ("rep", "shard")))


def body(
    tokens,
    segments,
    cotangent,
    gain_one,
    qkv_weight,
    query_scale,
    out_weight,
    gain_two,
    up_weight,
    up_bias,
    down_weight,
    down_bias,
):
    count = lax.axis_size("shard")
    shard = lax.axis_index("shard")
    length, width = tokens.shape[1:]
    rows = qkv_weight.shape[0]

    vec = jnp.concatenate([gain_one, gain_two, up_bias, down_bias]).astype(F32)
    vec = jnp.pad(vec, (0, -vec.shape[0] % 1024)).reshape(-1, 128)
    segs = segments
    whole_tiles = rows % 32 == 0 and count >= 4 and count & (count - 1) == 0 and lax.axis_size("rep") == 4
    weights = (qkv_weight, out_weight, up_weight, down_weight)
    earlier = None
    if not whole_tiles:
        earlier, segs, vec, *weights = gather_plain(tokens[0], segs, vec, *weights)
    output, acted_t, q_t, k_t, v_t, o_t, lse, hidden, inner_t, upper, lower_t, rows_in, qkv, out, up, down, mask = forward(
        count, tokens[0], earlier, segs, vec, query_scale[None], *weights
    )
    results = backward(
        count, not whole_tiles, cotangent[0], tokens[0], hidden, inner_t, upper, lower_t, o_t, q_t, k_t, v_t, acted_t,
        qkv, out, up, down, mask, lse, rows_in,
    )
    if whole_tiles:
        qkv_own, out_own, up_own, down_own, output, input_grad, *vectors = finish(
            results[5], *results[1:5], output, results[0]
        )
    else:
        grad_hidden, *partial = results
        qkv_own, out_own, up_own, down_own, grad_acted, small = reduce_plain(*partial)
        state = tokens[0].astype(F32)
        inverse = lax.rsqrt(jnp.mean(state * state, axis=-1, keepdims=True) + EPS)
        normed = state * inverse
        weighted = grad_acted * rows_in[0:1]
        along = jnp.mean(weighted * normed, axis=-1, keepdims=True)
        input_grad = (grad_hidden + inverse * (weighted - normed * along)).astype(BF16)
        mine = lax.dynamic_slice_in_dim(small[:4], shard * rows, rows, 1)
        vectors = [*mine, small[4, :HEAD] * rows_in[5, :HEAD]]

    return (
        output[None],
        input_grad[None],
        vectors[0],
        qkv_own,
        vectors[4],
        out_own,
        vectors[1],
        up_own,
        vectors[2],
        down_own,
        vectors[3],
    )


def solution(mesh):
    return jax.shard_map(
        body,
        mesh=mesh,
        in_specs=(
            P("rep", "shard", None),
            P("rep", "shard"),
            P("rep", "shard", None),
            P("shard"),
            P("shard", None),
            P(),
            P("shard", None),
            P("shard"),
            P("shard", None),
            P("shard"),
            P("shard", None),
            P("shard"),
        ),
        out_specs=(
            P("rep", "shard", None),
            P("rep", "shard", None),
            P("shard"),
            P("shard", None),
            P(),
            P("shard", None),
            P("shard"),
            P("shard", None),
            P("shard"),
            P("shard", None),
            P("shard"),
        ),
        check_vma=False,
    )
```
